32 devices in a mesh: item: 2 (over x), lat: 4 (over y, core), pix: 4 (over z).
Axes of the slice: x: 2, y: 2, z: 4, core: 2. Of those that a mesh axis runs over, the one named last changes fastest.
Arguments:
- latents: bfloat16 [8, 512, 1024], P('item', ('lat', 'pix')), may hold values from -6 to 6
- pixels: bfloat16 [8, 32768, 261], P('item', ('lat', 'pix')), may hold values from -6 to 6
- size_ids: int32 [8], P('item'), may hold values from 0 to 2, as said below
- cross_gain: float32 [1024], replicated, may hold values from 0.25 to 1.75
- pixel_gain: float32 [261], replicated, may hold values from 0.25 to 1.75
- query_weight: bfloat16 [1024, 1024], replicated, may hold values from -0.1875 to 0.1875
- key_weight: bfloat16 [261, 1024], replicated, may hold values from -0.375 to 0.375
- value_weight: bfloat16 [261, 1024], replicated, may hold values from -0.375 to 0.375
- cross_output: bfloat16 [1024, 1024], replicated, may hold values from -9 to 9
- first_gain: float32 [1024], replicated, may hold values from 0.25 to 1.75
- first_up: bfloat16 [1024, 1024], replicated, may hold values from -0.1875 to 0.1875
- first_down: bfloat16 [1024, 1024], replicated, may hold values from -0.1875 to 0.1875
- self_gain: float32 [1024], replicated, may hold values from 0.25 to 1.75
- self_inputs: bfloat16 [1024, 3072], replicated, may hold values from -0.1875 to 0.1875
- self_output: bfloat16 [1024, 1024], replicated, may hold values from -2.5 to 2.5
- second_gain: float32 [1024], replicated, may hold values from 0.25 to 1.75
- second_up: bfloat16 [1024, 1024], replicated, may hold values from -0.1875 to 0.1875
- second_down: bfloat16 [1024, 1024], replicated, may hold values from -0.1875 to 0.1875
- cotangent: bfloat16 [8, 512, 1024], P('item', ('lat', 'pix')), may hold values from -6 to 6
Outputs:
- latents_out: bfloat16 [8, 512, 1024], P('item', ('lat', 'pix'))
- latent_grad: bfloat16 [8, 512, 1024], P('item', ('lat', 'pix'))
- pixel_grad: bfloat16 [8, 32768, 261], P('item', ('lat', 'pix'))
- query_grad: float32 [1024, 1024], P(('item', 'lat', 'pix'))
- cross_out_grad: float32 [1024, 1024], P(('item', 'lat', 'pix'))
- first_up_grad: float32 [1024, 1024], P(('item', 'lat', 'pix'))
- first_down_grad: float32 [1024, 1024], P(('item', 'lat', 'pix'))
- self_in_grad: float32 [1024, 3072], P(('item', 'lat', 'pix'))
- self_out_grad: float32 [1024, 1024], P(('item', 'lat', 'pix'))
- second_up_grad: float32 [1024, 1024], P(('item', 'lat', 'pix'))
- second_down_grad: float32 [1024, 1024], P(('item', 'lat', 'pix'))
- key_grad: float32 [261, 1024], replicated
- value_grad: float32 [261, 1024], replicated
- cross_gain_grad: float32 [1024], replicated
- pixel_gain_grad: float32 [261], replicated
- first_gain_grad: float32 [1024], replicated
- self_gain_grad: float32 [1024], replicated
- second_gain_grad: float32 [1024], replicated
The draws below stay inside these ranges and needn't reach their ends.
Inputs may be any that keep to these rules, and one draw needn't show every extreme that they name: `size_ids`: each of the sizes 0, 1 and 2 is given to at least one image.
All inputs are finite; a program needn't handle non-finite values.
Results may differ from the reference program's by a relative error of at most 0.025.
Values may be sent and summed in bfloat16 or wider, within the bound.
No kernel may reach another device: no remote copies, remote signals or barrier semaphores. Data moves between devices by JAX's collectives and lax.ppermute only.
A program may use at most 256 MiB of HBM per device.

```python
import math
from functools import partial
import jax
import jax.numpy as jnp
from jax import lax

D = 1024
C = 261
HEADS = 8
HEAD_DIM = 128
LATENTS = 512
ITEMS = 8
PIX = 32768


def draw_size_ids(key, part):
    base = jnp.arange(ITEMS, dtype=jnp.int32) % 3
    return jax.random.permutation(key, base)


def levels(stream_key, shape, split, smallest, top_value):
    def one(axis_at, shards_of):
        steps = jax.random.uniform(jax.random.fold_in(jax.random.fold_in(stream_key, 6), axis_at), (shards_of,), jnp.float32, smallest / len(split), top_value / len(split))
        return jnp.repeat(jnp.exp(steps), shape[axis_at] // shards_of).reshape((-1,) + (1,) * (len(shape) - axis_at - 1))

    loudness = one(*split[0])
    for cut in split[1:]:
        loudness = loudness * one(*cut)
    return loudness


def noise(rng, dims, width, most, pieces=(), held_as=jnp.bfloat16):
    entries = width * jax.random.normal(rng, dims, jnp.float32)
    if pieces:
        entries = entries * levels(rng, dims, pieces, -0.22, 0.18)
    return jnp.clip(entries, -most, most).astype(held_as)


def setup_inputs(seed: int = 0) -> dict:
    key_list = jax.random.split(jax.random.key(seed), 20)
    return {
        "latents": noise(key_list[0], (ITEMS, LATENTS, D), 1.0, 6.0, ((0, 2), (1, 16))),
        "pixels": noise(key_list[1], (ITEMS, PIX, C), 1.0, 6.0, ((0, 2), (1, 16))),
        "size_ids": draw_size_ids(jax.random.fold_in(key_list[19], 71), 0),
        "cross_gain": jnp.clip(1.0 + 0.15 * jax.random.normal(key_list[3], (D,), jnp.float32), 0.25, 1.75),
        "pixel_gain": jnp.clip(1.0 + 0.15 * jax.random.normal(key_list[4], (C,), jnp.float32), 0.25, 1.75),
        "query_weight": noise(key_list[5], (D, D), D ** -0.5, 0.1875),
        "key_weight": noise(key_list[6], (C, D), C ** -0.5, 0.375),
        "value_weight": noise(key_list[7], (C, D), C ** -0.5, 0.375),
        "cross_output": noise(key_list[8], (D, D), 1.5, 9.0),
        "first_gain": jnp.clip(1.0 + 0.15 * jax.random.normal(key_list[9], (D,), jnp.float32), 0.25, 1.75),
        "first_up": noise(key_list[10], (D, D), D ** -0.5, 0.1875),
        "first_down": noise(key_list[11], (D, D), D ** -0.5, 0.1875),
        "self_gain": jnp.clip(1.0 + 0.15 * jax.random.normal(key_list[12], (D,), jnp.float32), 0.25, 1.75),
        "self_inputs": noise(key_list[13], (D, 3 * D), D ** -0.5, 0.1875),
        "self_output": noise(key_list[14], (D, D), (max(1, 3 * D // LATENTS)) ** -0.5, 2.5),
        "second_gain": jnp.clip(1.0 + 0.15 * jax.random.normal(key_list[15], (D,), jnp.float32), 0.25, 1.75),
        "second_up": noise(key_list[16], (D, D), D ** -0.5, 0.1875),
        "second_down": noise(key_list[17], (D, D), D ** -0.5, 0.1875),
        "cotangent": noise(key_list[18], (ITEMS, LATENTS, D), 1.0, 6.0, ((0, 2), (1, 16))),
    }


@jax.custom_vjp
def low(v):
    return lax.optimization_barrier(v.astype(jnp.bfloat16)).astype(jnp.float32)

@jax.custom_vjp
def low_back(v):
    return v

def low_keep(v):
    return (low(v), None)

def low_pass(kept, grad):
    return (grad,)

def back_keep(v):
    return (v, None)

def back_low(kept, grad):
    return (low(grad),)
low.defvjp(low_keep, low_pass)
low_back.defvjp(back_keep, back_low)
epsilon = 1e-05
highest = lax.Precision.HIGHEST

def norm_rows(inputs, gain):
    centred = inputs - lax.optimization_barrier(jnp.mean(inputs, axis=-1, keepdims=True))
    inverse = lax.rsqrt(lax.optimization_barrier(jnp.mean(centred * centred, axis=-1, keepdims=True)) + epsilon)
    return centred * inverse * gain

def activation(inputs):
    return jax.nn.gelu(inputs, approximate=True)

def project(inputs, matrix):
    return jnp.einsum('...d,de->...e', inputs, matrix, precision=highest)

def cross_item(operands, pixel_gain, key_weight, value_weight):
    query_rows, pixel_rows, valid_rows = operands
    normed = low(norm_rows(pixel_rows, pixel_gain))
    pixel_keys = low_back(low(project(normed, key_weight)))
    pixel_values = low_back(low(project(normed, value_weight)))
    scores = low_back(jnp.dot(query_rows, pixel_keys.T, precision=highest) * (1.0 / math.sqrt(D)))
    powered = jnp.where(valid_rows[None, :], jnp.exp(scores), 0.0)
    totals = lax.optimization_barrier(jnp.sum(powered, axis=1, keepdims=True))
    numerator = low_back(jnp.dot(low(powered), pixel_values, precision=highest))
    return numerator / totals

def forward(latents, pixels, valid, cross_gain, pixel_gain, query_weight, key_weight, value_weight, cross_output, first_gain, first_up, first_down, self_gain, self_inputs, self_output, second_gain, second_up, second_down):
    images = latents.shape[0]
    normed_one = low(norm_rows(latents, cross_gain))
    cross_query = low_back(low(project(normed_one, query_weight)))
    item_step = jax.checkpoint(partial(cross_item, pixel_gain=pixel_gain, key_weight=key_weight, value_weight=value_weight))
    attended = lax.map(item_step, (cross_query, pixels, valid))
    cross_mixed = low_back(low(attended))
    residual_one = latents + low_back(project(cross_mixed, cross_output))
    normed_two = low(norm_rows(residual_one, first_gain))
    hidden_one = low_back(project(normed_two, first_up))
    residual_two = residual_one + low_back(project(low(activation(hidden_one)), first_down))
    normed_three = low(norm_rows(residual_two, self_gain))
    projected = low_back(low(project(normed_three, self_inputs)))
    head_shape = (images, LATENTS, HEADS, HEAD_DIM)
    self_query = projected[..., :D].reshape(head_shape)
    self_keys = projected[..., D:2 * D].reshape(head_shape)
    self_values = projected[..., 2 * D:].reshape(head_shape)
    self_scores = low_back(jnp.einsum('ilhe,imhe->ihlm', self_query, self_keys, precision=highest) * (1.0 / math.sqrt(HEAD_DIM)))
    self_powered = jnp.exp(self_scores)
    self_totals = lax.optimization_barrier(jnp.sum(self_powered, axis=3))
    self_numerator = low_back(jnp.einsum('ihlm,imhe->ilhe', low(self_powered), self_values, precision=highest))
    self_mixed = self_numerator / jnp.transpose(self_totals, (0, 2, 1))[..., None]
    self_rounded = low_back(low(self_mixed.reshape(images, LATENTS, D)))
    residual_three = residual_two + low_back(project(self_rounded, self_output))
    normed_four = low(norm_rows(residual_three, second_gain))
    hidden_two = low_back(project(normed_four, second_up))
    return residual_three + low_back(project(low(activation(hidden_two)), second_down))

def reference(latents, pixels, size_ids, cross_gain, pixel_gain, query_weight, key_weight, value_weight, cross_output, first_gain, first_up, first_down, self_gain, self_inputs, self_output, second_gain, second_up, second_down, cotangent):
    factor = jnp.where(size_ids == 0, 25, jnp.where(size_ids == 1, 49, 81)).astype(jnp.int32)
    counts = PIX * factor // 81
    valid = jnp.arange(PIX, dtype=jnp.int32)[None, :] < counts[:, None]
    floats = tuple((array.astype(jnp.float32) for array in (latents, pixels, cross_gain, pixel_gain, query_weight, key_weight, value_weight, cross_output, first_gain, first_up, first_down, self_gain, self_inputs, self_output, second_gain, second_up, second_down)))

    def closed(latent_in, pixel_in, *params):
        return forward(latent_in, pixel_in, valid, *params)
    result, pullback = jax.vjp(closed, *floats)
    latent_grad, pixel_grad, cross_gain_grad, pixel_gain_grad, query_grad, key_grad, value_grad, cross_out_grad, first_gain_grad, first_up_grad, first_down_grad, self_gain_grad, self_in_grad, self_out_grad, second_gain_grad, second_up_grad, second_down_grad = pullback(cotangent.astype(jnp.float32))
    return (result.astype(jnp.bfloat16), latent_grad.astype(jnp.bfloat16), pixel_grad.astype(jnp.bfloat16), query_grad, cross_out_grad, first_up_grad, first_down_grad, self_in_grad, self_out_grad, second_up_grad, second_down_grad, key_grad, value_grad, cross_gain_grad, pixel_gain_grad, first_gain_grad, self_gain_grad, second_gain_grad)
```

```python
import math

import jax
import jax.numpy as jnp
from jax import lax
from jax.experimental import pallas as pl
from jax.experimental.pallas import tpu as pltpu
from jax.sharding import PartitionSpec as P

HEADS = 8
EPS = 1e-05
LOG2E = 1.4426950408889634
LN2 = 0.6931471805599453
BF = jnp.bfloat16
F32 = jnp.float32
VM = pl.BlockSpec(memory_space=pltpu.VMEM)
SM = pl.BlockSpec(memory_space=pltpu.SMEM)
LIMIT = 58 * 1024 * 1024


def nn(a, b):
    return lax.dot_general(a, b, (((1,), (0,)), ((), ())), preferred_element_type=F32)


def nt(a, b):
    return lax.dot_general(a, b, (((1,), (1,)), ((), ())), preferred_element_type=F32)


def tn(a, b):
    return lax.dot_general(a, b, (((0,), (0,)), ((), ())), preferred_element_type=F32)


def stats(v):
    c = v - jnp.mean(v, axis=-1, keepdims=True)
    r = lax.rsqrt(jnp.mean(c * c, axis=-1, keepdims=True) + EPS)
    return c * r, r


def norm_back(scaled, n, r):
    return r * (
        scaled
        - jnp.mean(scaled, axis=-1, keepdims=True)
        - n * jnp.mean(scaled * n, axis=-1, keepdims=True)
    )


K0 = math.sqrt(2.0 / math.pi)
K1 = 0.044715


def gelu(v):
    return 0.5 * v * (1.0 + jnp.tanh(K0 * (v + K1 * v * v * v)))


def gelu_grad(v):
    t = jnp.tanh(K0 * (v + K1 * v * v * v))
    return 0.5 * (1.0 + t) + 0.5 * v * (1.0 - t * t) * (K0 * (1.0 + 3.0 * K1 * v * v))


def cost(flops, nbytes=0):
    return pl.CostEstimate(flops=int(flops), bytes_accessed=int(nbytes), transcendentals=0)


def call(kernel, outs, ins, scratch=(), flops=0, **kw):
    return pl.pallas_call(
        kernel,
        out_shape=tuple(jax.ShapeDtypeStruct(s, d) for s, d in outs),
        in_specs=[SM if a.dtype == jnp.int32 else VM for a in ins],
        out_specs=tuple(VM for _ in outs),
        scratch_shapes=list(scratch),
        compiler_params=pltpu.CompilerParams(vmem_limit_bytes=LIMIT),
        cost_estimate=cost(flops, 4000000),
        **kw,
    )(*ins)


def query_kernel(lat, gain, wq, wk, gcol, out, scr, *, scale):
    chans = wk.shape[0]
    n, _ = stats(lat[...].astype(F32))
    rounded = (n * gain[...]).astype(BF)
    query = nn(rounded, wq[...]).astype(BF)
    t = nt(wk[...], query) * gcol[...]
    t = (t - jnp.sum(t, axis=0, keepdims=True) / chans) * (scale * LOG2E)
    scr[...] = jnp.zeros(scr.shape, F32)
    scr[0:chans, :] = t
    out[...] = scr[...].astype(BF)


def pixel_norm_kernel(cnt, pix, out, eye, *, chans, tile):
    i, t = pl.program_id(0), pl.program_id(1)
    feat = out.shape[1]

    @pl.when((i == 0) & (t == 0))
    def _():
        rows = lax.broadcasted_iota(jnp.int32, eye.shape, 0)
        cols = lax.broadcasted_iota(jnp.int32, eye.shape, 1)
        eye[...] = (rows == cols).astype(F32).astype(BF)

    xt = nt(eye[...], pix[0])
    base = feat - 16
    mean = jnp.sum(xt, axis=0, keepdims=True) / chans
    low = xt[0:base] - mean
    row = lax.broadcasted_iota(jnp.int32, (16, tile), 0) + base
    high = jnp.where(row < chans, xt[base:feat] - mean, 0.0)
    var = (
        jnp.sum(low * low, axis=0, keepdims=True) + jnp.sum(high * high, axis=0, keepdims=True)
    ) / chans
    lane = lax.broadcasted_iota(jnp.int32, (1, tile), 1) + t * tile
    valid = jnp.where(lane < cnt[i], 1.0, 0.0)
    inv = lax.rsqrt(var + EPS) * valid
    inv_high = inv.astype(BF).astype(F32)
    out[0, 0:base, :] = (low * inv).astype(BF)
    high = high * inv
    high = jnp.where(row == chans, valid, high)
    high = jnp.where(row == chans + 1, valid, high)
    high = jnp.where(row == chans + 2, inv_high, high)
    high = jnp.where(row == chans + 3, inv - inv_high, high)
    out[0, base:feat, :] = high.astype(BF)


def cross_kernel(*refs, images, lat_rows, scale):
    pos = refs[0]
    pieces = refs[1:17]
    nt_ref = refs[17]
    p_out, qkt_out, mine, send = refs[18:22]
    qkt, qk, acc = refs[22:25]
    i, t = pl.program_id(0), pl.program_id(1)
    lpos, core, z = pos[0], pos[1], pos[2]
    group = 4 * lat_rows

    @pl.when((i == 0) & (t == 0))
    def _():
        for rl in range(4):
            for im in range(images):
                parts = [
                    pieces[rl * 4 + rz][:, lat_rows * im : lat_rows * (im + 1)].astype(F32)
                    for rz in range(4)
                ]
                v = pltpu.roll(jnp.concatenate(parts, axis=1), lat_rows * z, 1)
                at = pl.multiple_of(group * (lpos ^ rl), group)
                qkt[im, :, pl.ds(at, group)] = v.astype(BF)

    @pl.when(t == 0)
    def _():
        qk[...] = jnp.transpose(qkt[i].astype(F32), (1, 0)).astype(BF)
        qkt_out[0] = qkt[i]

    n = nt_ref[0]
    p = jnp.exp2(nn(qk[...], n)).astype(BF)
    p_out[0] = p
    part = nt(n, p)

    @pl.when(t == 0)
    def _():
        acc[...] = part

    @pl.when(t != 0)
    def _():
        acc[...] = acc[...] + part

    @pl.when(t == pl.num_programs(1) - 1)
    def _():
        split_halves(acc, mine, send, core, group)


def split_halves(acc, mine, send, core, group):
    for y in range(2):
        a = pl.multiple_of(2 * group * y + group * core, group)
        b = pl.multiple_of(2 * group * y + group * (1 - core), group)
        mine[0, :, group * y : group * (y + 1)] = acc[:, pl.ds(a, group)].astype(BF)
        send[0, :, group * y : group * (y + 1)] = acc[:, pl.ds(b, group)].astype(BF)


def pixel_back_kernel(*refs, chans, images):
    pos = refs[0]
    pieces = refs[1:9]
    nt_ref, p_ref, qkt_ref = refs[9:12]
    grad, mine, send = refs[12:15]
    gvt, gv, qktb, acc = refs[15:19]
    i, t = pl.program_id(0), pl.program_id(1)
    core, z = pos[1], pos[2]
    feat, lats = gv.shape[1], gv.shape[0]
    group = lats // 4
    base = feat - 16

    @pl.when((i == 0) & (t == 0))
    def _():
        for other in range(2):
            for rz in range(4):
                im = lax.rem(z + rz, 4)
                for y in range(2):
                    at = pl.multiple_of(2 * group * y + group * (core ^ other), group)
                    gvt[im, :, pl.ds(at, group)] = pieces[other * 4 + rz][
                        :, group * y : group * (y + 1)
                    ]

    @pl.when(t == 0)
    def _():
        gv[...] = jnp.transpose(gvt[i].astype(F32), (1, 0)).astype(BF)
        qktb[...] = (qkt_ref[0].astype(F32) * LN2).astype(BF)

    n = nt_ref[0]
    p = p_ref[0]
    ds = (p.astype(F32) * nn(gv[...], n)).astype(BF)
    part = nt(n, ds)
    dn = nn(qktb[...], ds) + nn(gvt[i], p)
    nf = n.astype(F32)
    low, high = nf[0:base], nf[base:feat]
    row = lax.broadcasted_iota(jnp.int32, high.shape, 0) + base
    inv = jnp.sum(
        jnp.where((row == chans + 2) | (row == chans + 3), high, 0.0), axis=0, keepdims=True
    )
    high = jnp.where(row < chans, high, 0.0)
    m2 = (
        jnp.sum(dn[0:base] * low, axis=0, keepdims=True)
        + jnp.sum(dn[base:feat] * high, axis=0, keepdims=True)
    ) / chans
    out = jnp.concatenate([inv * (dn[0:base] - low * m2), inv * (dn[base:feat] - high * m2)], axis=0)
    grad[0] = jnp.transpose(out, (1, 0))[:, 0:chans].astype(BF)

    @pl.when(t == 0)
    def _():
        acc[...] = part

    @pl.when(t != 0)
    def _():
        acc[...] = acc[...] + part

    @pl.when(t == pl.num_programs(1) - 1)
    def _():
        split_halves(acc, mine, send, core, group)


def first_kernel(pos, a_mine, a_recv, lat_mine, lat_recv, gcol, wv, co, g1, fu, fd, gs, si,
                 att_out, tot_out, res1_out, nt2_out, hid1_out, act1_out, res2_out, nt3_out, q_out, kv_out, lat):
    y = pos[3]
    half = lat_mine.shape[0]
    width = lat.shape[1]
    chans = wv.shape[0]
    lat[pl.ds(pl.multiple_of(half * y, half), half), :] = lat_mine[...]
    lat[pl.ds(pl.multiple_of(half * (1 - y), half), half), :] = lat_recv[...]
    a = a_mine[...].astype(F32) + a_recv[...].astype(F32)
    tot = a[chans : chans + 1, :]
    att = a[0:chans, :] / tot
    att_out[...] = att
    tot_out[...] = tot
    mixed = tn((att * gcol[...]).astype(BF), wv[...]).astype(BF)
    res1 = lat[...].astype(F32) + nn(mixed, co[...])
    res1_out[...] = res1
    n2, _ = stats(res1)
    nt2 = (n2 * g1[...]).astype(BF)
    nt2_out[...] = nt2
    hid = nn(nt2, fu[...])
    hid1_out[...] = hid
    act = gelu(hid).astype(BF)
    act1_out[...] = act
    res2 = res1 + nn(act, fd[...])
    res2_out[...] = res2
    n3, _ = stats(res2)
    nt3 = (n3 * gs[...]).astype(BF)
    nt3_out[...] = nt3
    kv_out[...] = nn(nt3, si[:, width : 3 * width]).astype(BF)
    q_out[...] = nn(nt3, si[:, 0:width]).astype(BF)


def second_kernel(pos, q, kv, kv2, res2, cot_mine, cot_recv, so, g2, su, sd,
                  out, selfr_out, sent3_out, back3_out, nt4_out, act2_out, hg2_out, gain_out, dq_out, dkv_out, dkv2_out,
                  prob, cot, mixed_scr, tots):
    y = pos[3]
    half = cot_mine.shape[0]
    rows, width = res2.shape
    hd = width // HEADS
    hs = 1.0 / math.sqrt(hd)
    cot[pl.ds(pl.multiple_of(half * y, half), half), :] = cot_mine[...]
    cot[pl.ds(pl.multiple_of(half * (1 - y), half), half), :] = cot_recv[...]
    for h in range(HEADS):
        cols = slice(h * hd, (h + 1) * hd)
        vcols = slice(width + h * hd, width + (h + 1) * hd)
        qh = q[:, cols]
        pa = jnp.exp2(nt(qh, kv[:, cols]) * (hs * LOG2E))
        pb = jnp.exp2(nt(qh, kv2[:, cols]) * (hs * LOG2E))
        tot = jnp.sum(pa, axis=1, keepdims=True) + jnp.sum(pb, axis=1, keepdims=True)
        pa, pb = pa.astype(BF), pb.astype(BF)
        prob[h, :, 0:rows] = pa
        prob[h, :, rows : 2 * rows] = pb
        rt = 1.0 / tot
        tots[h] = rt
        mixed_scr[:, cols] = (nn(pa, kv[:, vcols]) + nn(pb, kv2[:, vcols])) * rt
    selfr = mixed_scr[...].astype(BF)
    selfr_out[...] = selfr
    res3 = res2[...] + nn(selfr, so[...])
    n4, r4 = stats(res3)
    nt4 = (n4 * g2[...]).astype(BF)
    nt4_out[...] = nt4
    hid = nn(nt4, su[...])
    act = gelu(hid).astype(BF)
    act2_out[...] = act
    out[...] = (res3 + nn(act, sd[...])).astype(BF)
    hg = (nt(cot[...], sd[...]) * gelu_grad(hid)).astype(BF)
    hg2_out[...] = hg
    ng = nt(hg, su[...])
    gain_out[...] = jnp.sum(ng * n4, axis=0, keepdims=True)
    back3 = cot[...].astype(F32) + norm_back(ng * g2[...], n4, r4)
    back3_out[...] = back3
    sent3 = back3.astype(BF)
    sent3_out[...] = sent3
    mg_all = nt(sent3, so[...]).astype(BF)
    for h in range(HEADS):
        cols = slice(h * hd, (h + 1) * hd)
        vcols = slice(width + h * hd, width + (h + 1) * hd)
        mg = mg_all[:, cols].astype(F32)
        rt = tots[h]
        ng_h = (mg * rt).astype(BF)
        tg = -jnp.sum(mg * mixed_scr[:, cols], axis=1, keepdims=True) * rt
        qh = q[:, cols]
        dq = None
        for src, dst, at in ((kv, dkv_out, 0), (kv2, dkv2_out, rows)):
            p = prob[h, :, at : at + rows]
            sg = (p.astype(F32) * (nt(ng_h, src[:, vcols]) + tg)).astype(BF)
            d = nn(sg, src[:, cols])
            dq = d if dq is None else dq + d
            dst[:, cols] = (tn(sg, qh) * hs).astype(dst.dtype)
            dst[:, vcols] = tn(p, ng_h).astype(dst.dtype)
        dq_out[:, cols] = (dq * hs).astype(BF)


def third_kernel(dq, dkv, dkv2, back3, res2, res1, hid1, att, tot, gcol, wv, co, g1, fu, fd, gs, si, gain2,
                 pg_out, sent2_out, hg1_out, back1_out, gv_out, ht_out, scr):
    rows, width = back3.shape
    chans = wv.shape[0]
    feat = scr.shape[0]
    base = feat - 16
    pg_out[:, 0:width] = dq[...]
    pg_out[:, width : 3 * width] = (dkv[...] + dkv2[...].astype(F32)).astype(BF)
    ng = nt(pg_out[...], si[...])
    n3, r3 = stats(res2[...])
    gain_self = jnp.sum(ng * n3, axis=0, keepdims=True)
    back2 = back3[...] + norm_back(ng * gs[...], n3, r3)
    sent2 = back2.astype(BF)
    sent2_out[...] = sent2
    hg = (nt(sent2, fd[...]) * gelu_grad(hid1[...])).astype(BF)
    hg1_out[...] = hg
    ng = nt(hg, fu[...])
    n2, r2 = stats(res1[...])
    gain_first = jnp.sum(ng * n2, axis=0, keepdims=True)
    back1 = back2 + norm_back(ng * g1[...], n2, r2)
    back1_out[...] = back1
    sent1 = back1.astype(BF)
    ag = nt(sent1, co[...]).astype(BF)
    rt = 1.0 / tot[...]
    raw = nt(wv[...], ag) * (rt * gcol[...])
    tg = -jnp.sum(att[...] * raw, axis=0, keepdims=True)
    raw = raw - jnp.sum(raw, axis=0, keepdims=True) / chans
    scr[...] = jnp.zeros(scr.shape, F32)
    scr[0:chans, :] = raw
    gv_out[0:base, :] = scr[0:base, :].astype(BF)
    row = lax.broadcasted_iota(jnp.int32, (16, rows), 0) + base
    tg_high = tg.astype(BF).astype(F32)
    high = jnp.where(row == chans, tg_high, scr[base:feat, :])
    high = jnp.where(row == chans + 1, tg - tg_high, high)
    gv_out[base:feat, :] = high.astype(BF)
    scr[0:chans, :] = att[...]
    ht = nn(scr[...].astype(BF), sent1)
    ht_out[0:base, :] = (0.5 * ht[0:base]).astype(BF)
    row = lax.broadcasted_iota(jnp.int32, (16, width), 0) + base
    high = ht[base:feat]
    for k, v in enumerate((gain_first, gain_self, gain2[...])):
        v_high = v.astype(BF).astype(F32)
        high = jnp.where(row == chans + 2 * k, v_high, high)
        high = jnp.where(row == chans + 2 * k + 1, v - v_high, high)
    ht_out[base:feat, :] = (0.5 * high).astype(BF)


def last_kernel(b_mine, b_recv, lat, back1, gain, gcol, wq, wk, out, gt_out, scr, *, scale):
    chans, width = wk.shape
    feat = scr.shape[0]
    base = feat - 16
    b = (b_mine[...].astype(F32) + b_recv[...].astype(F32)) * (scale * LN2 * LOG2E)
    bs = b[0:chans, :]
    rows_grad = tn((bs * gcol[...]).astype(BF), wk[...]).astype(BF)
    ng = nt(rows_grad, wq[...])
    n, r = stats(lat[...].astype(F32))
    rounded = (n * gain[...]).astype(BF)
    gain_grad = jnp.sum(ng * n, axis=0, keepdims=True)
    out[...] = (back1[...] + norm_back(ng * gain[...], n, r)).astype(BF)
    scr[...] = jnp.zeros(scr.shape, F32)
    scr[0:chans, :] = bs
    gt = nn(scr[...].astype(BF), rounded)
    gt_out[0:base, :] = gt[0:base].astype(BF)
    row = lax.broadcasted_iota(jnp.int32, (16, width), 0) + base
    high = gt[base:feat]
    g_high = gain_grad.astype(BF).astype(F32)
    high = jnp.where(row == chans, g_high, high)
    high = jnp.where(row == chans + 1, gain_grad - g_high, high)
    gt_out[base:feat, :] = high.astype(BF)


def value_kernel(pos, ht, gcol, wv, co, value_out, cross_out, vsum_out, gains_out):
    chans, width = wv.shape
    rows = cross_out.shape[0]
    h = ht[...].astype(F32)
    hb = ht[0:chans, :]
    v = nt(hb, co[...])
    vsum_out[...] = jnp.sum(v * wv[...].astype(F32), axis=1, keepdims=True)
    value_out[...] = v * gcol[...]
    one = own_columns(width, rows, pos[4])
    wsel = (nn(wv[...], one) * gcol[...]).astype(BF)
    cross_out[...] = tn(wsel, hb)
    for k in range(3):
        gains_out[k : k + 1, :] = (
            h[chans + 2 * k : chans + 2 * k + 1, :] + h[chans + 2 * k + 1 : chans + 2 * k + 2, :]
        )


def own_columns(width, rows, index):
    r = lax.broadcasted_iota(jnp.int32, (width, rows), 0)
    c = lax.broadcasted_iota(jnp.int32, (width, rows), 1)
    return (r == c + index * rows).astype(F32).astype(BF)


def key_kernel(pos, gt, gcol, wk, wq, vsum, key_out, query_out, psum_out, gain_out):
    chans, width = wk.shape
    rows = query_out.shape[0]
    g = gt[...].astype(F32)
    gb = gt[0:chans, :]
    k = nn(gb, wq[...])
    psum_out[...] = jnp.sum(k * wk[...].astype(F32), axis=1, keepdims=True) + vsum[...]
    key_out[...] = k * gcol[...]
    one = own_columns(width, rows, pos[4])
    sel = (nn(gb, one) * gcol[...]).astype(BF)
    query_out[...] = tn(sel, wk[...])
    gain_out[...] = g[chans : chans + 1, :] + g[chans + 1 : chans + 2, :]


def swap(x, kind, lat):
    if kind == "core":
        perm = [(s, s ^ 1) for s in range(lat)]
    else:
        perm = [(s, s ^ 2) for s in range(lat)]
    return lax.ppermute(x, "lat", perm)


def around(x, n):
    got = [x]
    for r in range(1, n):
        got.append(lax.ppermute(x, "pix", [((d + r) % n, d) for d in range(n)]))
    return got


def sum_over(x):
    return jnp.sum(x.astype(F32), axis=0)


def all_sum(x, items, lat):
    feat, width = x.shape
    parts = items * lat
    lanes = width // parts
    x = jnp.transpose(x.reshape(feat, parts, lanes), (1, 0, 2))
    x = lax.all_to_all(x, ("item", "lat"), 0, 0, tiled=True)
    x = sum_over(x).astype(BF)
    x = sum_over(lax.all_gather(x, "pix", axis=0)).astype(BF)
    x = lax.all_gather(x, ("item", "lat"), axis=0)
    return jnp.transpose(x, (1, 0, 2)).reshape(feat, width)


def reduce_units(units, items, lat, pix, yy, core):
    width = units[0][0].shape[1]
    chunk = width // (2 * items)
    outs = []
    for left, right in units:
        rows = left.shape[0]
        sel = lax.dynamic_index_in_dim(left.reshape(rows, items, 2, chunk), yy, 2, keepdims=False)
        outs.append(
            lax.dot_general(
                sel.reshape(rows, items * chunk),
                right,
                (((0,), (0,)), ((), ())),
                preferred_element_type=F32,
            ).astype(BF)
        )
    cols = [o.shape[1] for o in outs]
    x = jnp.concatenate(outs, axis=1) if len(outs) > 1 else outs[0]
    x = x.reshape(items, 2, chunk // 2, sum(cols))
    mine = lax.dynamic_index_in_dim(x, core, 1, keepdims=False)
    give = lax.dynamic_index_in_dim(x, 1 - core, 1, keepdims=False)
    got = swap(give, "core", lat)
    x = (mine.astype(F32) + got.astype(F32)).astype(BF)
    x = sum_over(lax.all_to_all(x, "item", 0, 0, tiled=True)).astype(BF)
    x = x.reshape(pix, chunk // (2 * pix), sum(cols))
    x = sum_over(lax.all_to_all(x, "pix", 0, 0, tiled=True))
    res, at = [], 0
    for c in cols:
        res.append(x[:, at : at + c])
        at += c
    return res


def body(
    latents,
    pixels,
    size_ids,
    cross_gain,
    pixel_gain,
    query_weight,
    key_weight,
    value_weight,
    cross_output,
    first_gain,
    first_up,
    first_down,
    self_gain,
    self_inputs,
    self_output,
    second_gain,
    second_up,
    second_down,
    cotangent,
):
    images, lat_rows, width = latents.shape
    pix_rows, chans = pixels.shape[1:]
    lat, pix, items = lax.axis_size("lat"), lax.axis_size("pix"), lax.axis_size("item")
    assert lat == 4 and pix == 4 and images == pix
    feat = -(-(chans + 4) // 16) * 16
    l, z, it = lax.axis_index("lat"), lax.axis_index("pix"), lax.axis_index("item")
    core, yy = l % 2, l // 2
    block = l * pix + z
    pos = jnp.stack([l, core, z, yy, it * (lat * pix) + block]).astype(jnp.int32)
    rows = images * lat_rows
    lats = lat * rows
    scale = 1.0 / math.sqrt(width)
    factor = jnp.where(size_ids == 0, 25, jnp.where(size_ids == 1, 49, 81)).astype(jnp.int32)
    counts = pix_rows * (lat * pix) * factor // 81 - block * pix_rows
    gcol = pixel_gain.reshape(chans, 1)
    row = lambda v: v.reshape(1, width)

    (qkt,) = call(
        lambda *r: query_kernel(*r, scale=scale),
        [((feat, rows), BF)],
        [latents.reshape(rows, width), row(cross_gain), query_weight, key_weight, gcol],
        [pltpu.VMEM((feat, rows), F32)],
        flops=2 * rows * width * width,
    )
    level = around(qkt, pix)
    level_y = [swap(v, "y", lat) for v in level]
    pieces = {0: level, 2: level_y}
    pieces[1] = [swap(v, "core", lat) for v in level]
    pieces[3] = [swap(v, "core", lat) for v in level_y]

    tile = min(1024, pix_rows)
    tiles = pix_rows // tile
    params = pltpu.CompilerParams(
        dimension_semantics=("arbitrary", "arbitrary"), vmem_limit_bytes=LIMIT
    )
    normed = pl.pallas_call(
        lambda *r: pixel_norm_kernel(*r, chans=chans, tile=tile),
        grid=(images, tiles),
        in_specs=[SM, pl.BlockSpec((1, tile, chans), lambda i, t: (i, t, 0))],
        out_specs=pl.BlockSpec((1, feat, tile), lambda i, t: (i, 0, t)),
        out_shape=jax.ShapeDtypeStruct((images, feat, pix_rows), BF),
        scratch_shapes=[pltpu.VMEM((feat, chans), BF)],
        compiler_params=params,
        cost_estimate=cost(images * pix_rows * 512 * feat * 4, images * pix_rows * feat * 4),
    )(counts, pixels)

    both = jnp.concatenate([latents, cotangent], axis=1)
    both = lax.all_to_all(both, "pix", 0, 0, tiled=True)
    lat_mine = both[:, :lat_rows].reshape(rows, width)
    cot_mine = both[:, lat_rows:].reshape(rows, width)
    lat_recv = swap(lat_mine, "y", lat)
    cot_recv = swap(cot_mine, "y", lat)

    whole = lambda a: pl.BlockSpec(a.shape, lambda i, t: (0,) * a.ndim)
    half_spec = pl.BlockSpec((1, feat, lats // 2), lambda i, t: (i, 0, 0))
    half_shape = jax.ShapeDtypeStruct((images, feat, lats // 2), BF)
    flat = [v for rl in range(4) for v in pieces[rl]]
    powered, qkt_all, mine, give = pl.pallas_call(
        lambda *r: cross_kernel(*r, images=images, lat_rows=lat_rows, scale=scale),
        grid=(images, tiles),
        in_specs=[SM]
        + [whole(v) for v in flat]
        + [pl.BlockSpec((1, feat, tile), lambda i, t: (i, 0, t))],
        out_specs=(
            pl.BlockSpec((1, lats, tile), lambda i, t: (i, 0, t)),
            pl.BlockSpec((1, feat, lats), lambda i, t: (i, 0, 0)),
            half_spec,
            half_spec,
        ),
        out_shape=(
            jax.ShapeDtypeStruct((images, lats, pix_rows), BF),
            jax.ShapeDtypeStruct((images, feat, lats), BF),
            half_shape,
            half_shape,
        ),
        scratch_shapes=[
            pltpu.VMEM((images, feat, lats), BF),
            pltpu.VMEM((lats, feat), BF),
            pltpu.VMEM((feat, lats), F32),
        ],
        compiler_params=params,
        cost_estimate=cost(images * pix_rows * 512 * lats * 4, images * pix_rows * lats * 3),
    )(pos, *flat, normed)

    def to_owner(mine, give):
        got = swap(give, "core", lat)
        x = (mine.astype(F32) + got.astype(F32)).astype(BF)
        return sum_over(lax.all_to_all(x, "pix", 0, 0, tiled=True))

    a_mine = to_owner(mine, give).astype(BF)
    a_recv = swap(a_mine, "y", lat)
    r2 = 2 * rows
    sq = (r2, width)
    att, tot, res1, nt2, hid1, act1, res2, nt3, q, kv = call(
        first_kernel,
        [((chans, r2), F32), ((1, r2), F32), (sq, F32), (sq, BF), (sq, F32), (sq, BF), (sq, F32), (sq, BF), (sq, BF), ((r2, 2 * width), BF)],
        [pos, a_mine, a_recv, lat_mine, lat_recv, gcol, value_weight, cross_output, row(first_gain), first_up, first_down, row(self_gain), self_inputs],
        [pltpu.VMEM(sq, BF)],
        flops=2 * r2 * width * width * 6,
    )
    kv2 = swap(kv, "core", lat)
    out, selfr, sent3, back3, nt4, act2, hg2, gain2, dq, dkv, dkv_send = call(
        second_kernel,
        [(sq, BF), (sq, BF), (sq, BF), (sq, F32), (sq, BF), (sq, BF), (sq, BF), ((1, width), F32), (sq, BF), ((r2, 2 * width), F32), ((r2, 2 * width), BF)],
        [pos, q, kv, kv2, res2, cot_mine, cot_recv, self_output, row(second_gain), second_up, second_down],
        [
            pltpu.VMEM((HEADS, r2, 2 * r2), BF),
            pltpu.VMEM(sq, BF),
            pltpu.VMEM(sq, F32),
            pltpu.VMEM((HEADS, r2, 1), F32),
        ],
        flops=2 * r2 * width * width * 10,
    )
    dkv2 = swap(dkv_send, "core", lat)
    pg, sent2, hg1, back1, gvt, ht = call(
        third_kernel,
        [((r2, 3 * width), BF), (sq, BF), (sq, BF), (sq, F32), ((feat, r2), BF), ((feat, width), BF)],
        [dq, dkv, dkv2, back3, res2, res1, hid1, att, tot, gcol, value_weight, cross_output, row(first_gain), first_up, first_down, row(self_gain), self_inputs, gain2],
        [pltpu.VMEM((feat, r2), F32)],
        flops=2 * r2 * width * width * 7,
    )
    gv_level = around(gvt, pix)
    gv_flat = gv_level + [swap(v, "core", lat) for v in gv_level]

    pixel_grad, mine, give = pl.pallas_call(
        lambda *r: pixel_back_kernel(*r, chans=chans, images=images),
        grid=(images, tiles),
        in_specs=[SM]
        + [whole(v) for v in gv_flat]
        + [
            pl.BlockSpec((1, feat, tile), lambda i, t: (i, 0, t)),
            pl.BlockSpec((1, lats, tile), lambda i, t: (i, 0, t)),
            pl.BlockSpec((1, feat, lats), lambda i, t: (i, 0, 0)),
        ],
        out_specs=(
            pl.BlockSpec((1, tile, chans), lambda i, t: (i, t, 0)),
            half_spec,
            half_spec,
        ),
        out_shape=(
            jax.ShapeDtypeStruct((images, pix_rows, chans), BF),
            half_shape,
            half_shape,
        ),
        scratch_shapes=[
            pltpu.VMEM((images, feat, lats), BF),
            pltpu.VMEM((lats, feat), BF),
            pltpu.VMEM((feat, lats), BF),
            pltpu.VMEM((feat, lats), F32),
        ],
        compiler_params=params,
        cost_estimate=cost(images * pix_rows * 512 * lats * 8, images * pix_rows * lats * 3),
    )(pos, *gv_flat, normed, powered, qkt_all)

    own = to_owner(mine, give).astype(BF)
    b_mine = lax.dynamic_slice_in_dim(own, yy * rows, rows, 1)
    b_recv = swap(lax.dynamic_slice_in_dim(own, (1 - yy) * rows, rows, 1), "y", lat)
    back1_own = lax.dynamic_slice_in_dim(back1, yy * rows, rows, 0)
    latent_grad, gt = call(
        lambda *r: last_kernel(*r, scale=scale),
        [((rows, width), BF), ((feat, width), BF)],
        [b_mine, b_recv, lat_mine, back1_own, row(cross_gain), gcol, query_weight, key_weight],
        [pltpu.VMEM((feat, rows), F32)],
        flops=2 * rows * width * width * 2,
    )

    def back_home(x):
        x = x.reshape(pix, lat_rows, width)
        return lax.all_to_all(x, "pix", 0, 0, tiled=True)

    latents_out = back_home(lax.dynamic_slice_in_dim(out, yy * rows, rows, 0))
    latent_grad = back_home(latent_grad)

    own_rows = width // (items * lat * pix)
    ht = all_sum(ht, items, lat)
    value_grad, cross_out_grad, vsum, gains = call(
        value_kernel,
        [((chans, width), F32), ((own_rows, width), F32), ((chans, 1), F32), ((3, width), F32)],
        [pos, ht, gcol, value_weight, cross_output],
        flops=2 * chans * width * width,
    )
    second_up_grad, second_down_grad, self_out_grad = reduce_units(
        [(nt4, hg2), (act2, cot_rows(cot_mine, cot_recv, yy)), (selfr, sent3)],
        items, lat, pix, yy, core,
    )
    (self_in_grad,) = reduce_units([(nt3, pg)], items, lat, pix, yy, core)
    first_up_grad, first_down_grad = reduce_units(
        [(nt2, hg1), (act1, sent2)], items, lat, pix, yy, core
    )
    gt = all_sum(gt, items, lat)
    key_grad, query_grad, psum, cross_gain_grad = call(
        key_kernel,
        [((chans, width), F32), ((own_rows, width), F32), ((chans, 1), F32), ((1, width), F32)],
        [pos, gt, gcol, key_weight, query_weight, vsum],
        flops=2 * chans * width * width,
    )
    return (
        latents_out,
        latent_grad,
        pixel_grad,
        query_grad,
        cross_out_grad,
        first_up_grad,
        first_down_grad,
        self_in_grad,
        self_out_grad,
        second_up_grad,
        second_down_grad,
        key_grad,
        value_grad,
        cross_gain_grad.reshape(width),
        psum.reshape(chans),
        gains[0],
        gains[1],
        gains[2],
    )


def cot_rows(mine, recv, yy):
    first = jnp.where(yy == 0, mine, recv)
    second = jnp.where(yy == 0, recv, mine)
    return jnp.concatenate([first, second], axis=0)


def solution(mesh):
    split = P("item", ("lat", "pix"), None)
    in_specs = (split, split, P("item")) + (P(),) * 15 + (split,)
    grads = P(("item", "lat", "pix"), None)
    out_specs = (split, split, split) + (grads,) * 8 + (P(),) * 7
    return jax.shard_map(body, mesh=mesh, in_specs=in_specs, out_specs=out_specs, check_vma=False)
```

```python
import math

import jax
import jax.numpy as jnp
from jax import lax
from jax.experimental import pallas as pl
from jax.experimental.pallas import tpu as pltpu
from jax.sharding import PartitionSpec as P

HEADS = 8
EPS = 1e-05
LOG2E = 1.4426950408889634
LN2 = 0.6931471805599453
BF = jnp.bfloat16
F32 = jnp.float32
VM = pl.BlockSpec(memory_space=pltpu.VMEM)
SM = pl.BlockSpec(memory_space=pltpu.SMEM)
LIMIT = 24 * 1024 * 1024


def nn(a, b):
    return lax.dot_general(a, b, (((1,), (0,)), ((), ())), preferred_element_type=F32)


def nt(a, b):
    return lax.dot_general(a, b, (((1,), (1,)), ((), ())), preferred_element_type=F32)


def tn(a, b):
    return lax.dot_general(a, b, (((0,), (0,)), ((), ())), preferred_element_type=F32)


def stats(v):
    c = v - jnp.mean(v, axis=-1, keepdims=True)
    r = lax.rsqrt(jnp.mean(c * c, axis=-1, keepdims=True) + EPS)
    return c * r, r


def norm_back(scaled, n, r):
    return r * (
        scaled
        - jnp.mean(scaled, axis=-1, keepdims=True)
        - n * jnp.mean(scaled * n, axis=-1, keepdims=True)
    )


K0 = math.sqrt(2.0 / math.pi)
K1 = 0.044715


def gelu(v):
    return 0.5 * v * (1.0 + jnp.tanh(K0 * (v + K1 * v * v * v)))


def gelu_grad(v):
    t = jnp.tanh(K0 * (v + K1 * v * v * v))
    return 0.5 * (1.0 + t) + 0.5 * v * (1.0 - t * t) * (K0 * (1.0 + 3.0 * K1 * v * v))


def cost(flops, nbytes=0):
    return pl.CostEstimate(flops=int(flops), bytes_accessed=int(nbytes), transcendentals=0)


def with_deps(kernel, n_ins, n_deps):
    if not n_deps:
        return kernel
    return lambda *refs: kernel(*refs[:n_ins], *refs[n_ins + n_deps :])


def call(kernel, outs, ins, scratch=(), flops=0, deps=()):
    return pl.pallas_call(
        with_deps(kernel, len(ins), len(deps)),
        out_shape=tuple(jax.ShapeDtypeStruct(s, d) for s, d in outs),
        in_specs=[SM if a.dtype == jnp.int32 else VM for a in ins]
        + [pl.BlockSpec(memory_space=pl.ANY)] * len(deps),
        out_specs=tuple(VM for _ in outs),
        scratch_shapes=list(scratch),
        compiler_params=pltpu.CompilerParams(vmem_limit_bytes=LIMIT),
        cost_estimate=cost(flops, 4000000),
    )(*ins, *deps)


def query_kernel(lat, gain, wq, wk, gcol, out, scr, *, scale):
    chans = wk.shape[0]
    x = lat[...].astype(F32)
    n, _ = stats(x.reshape(out.shape[1], x.shape[-1]))
    rounded = (n * gain[...]).astype(BF)
    query = nn(rounded, wq[...]).astype(BF)
    t = nt(wk[...], query) * gcol[...]
    t = (t - jnp.sum(t, axis=0, keepdims=True) / chans) * (scale * LOG2E)
    scr[...] = jnp.zeros(scr.shape, F32)
    scr[0:chans, :] = t
    out[...] = scr[...].astype(BF)


def stack_kernel(pos, *refs, order, images):
    level, lat, cot = refs[:images], refs[images], refs[images + 1]
    outs, sends = refs[images + 2 : 2 * images + 2], refs[2 * images + 2 :]
    z = pos[2]
    lat_rows = lat.shape[1]
    wide = [v[...].astype(F32) for v in level]
    slot = lax.broadcasted_iota(jnp.int32, wide[0].shape, 1) // lat_rows
    for r in range(images):
        im = lax.rem(z + r, images)
        total = None
        for rz in range(images):
            s = lax.rem(z + rz, images)
            v = pltpu.roll(wide[rz], lax.rem(s - im + images, images) * lat_rows, 1)
            total = v if total is None else jnp.where(slot == s, v, total)
        outs[r][...] = total.astype(BF)
        sends[r][0:lat_rows, :] = lat[im]
        sends[r][lat_rows : 2 * lat_rows, :] = cot[im]


def gather_kernel(pos, *refs):
    pieces, out = refs[:-1], refs[-1]
    n = len(pieces)
    lat_rows = pieces[0].shape[0] // 2
    for r in range(n):
        src = lax.rem(pos[2] - r + n, n)
        for half in range(2):
            at = pl.multiple_of(half * n * lat_rows + src * lat_rows, lat_rows)
            out[pl.ds(at, lat_rows), :] = pieces[r][half * lat_rows : (half + 1) * lat_rows, :]


def pixel_norm_kernel(pos, cnt, pix, out, wide, tail, *, tile, start):
    t = pl.program_id(0) + start
    chans, images = pix.shape[:2]
    feat = out.shape[1]
    base = feat - 16
    wide[...] = pix[...].astype(F32)
    row = lax.broadcasted_iota(jnp.int32, (16, tile), 0) + base
    lane = lax.broadcasted_iota(jnp.int32, (1, tile), 1) + t * tile
    for i in range(images):
        x = wide[:, i, :]
        x = x - jnp.sum(x, axis=0, keepdims=True) / chans
        var = jnp.sum(x * x, axis=0, keepdims=True) / chans
        valid = jnp.where(lane < cnt[i], 1.0, 0.0)
        inv = lax.rsqrt(var + EPS) * valid
        inv_high = inv.astype(BF).astype(F32)
        x = x * inv
        out[i, 0:base, :] = x[0:base].astype(BF)
        tail[...] = jnp.zeros(tail.shape, F32)
        tail[0 : chans - base, :] = x[base:chans]
        high = tail[...]
        high = jnp.where((row == chans) | (row == chans + 1), valid, high)
        high = jnp.where(row == chans + 2, inv_high, high)
        high = jnp.where(row == chans + 3, inv - inv_high, high)
        out[i, base:feat, :] = high.astype(BF)


def cross_kernel(pos, *refs):
    pieces, refs = refs[:4], refs[4:]
    nt_ref, p_out, mine, send, qkt, qk, acc = refs
    t = pl.program_id(0)
    lpos, core = pos[0], pos[1]
    group = pieces[0].shape[1]

    @pl.when(t == 0)
    def _():
        for rl in range(4):
            at = pl.multiple_of(group * (lpos ^ rl), group)
            qkt[:, pl.ds(at, group)] = pieces[rl][...]
        qk[...] = jnp.transpose(qkt[...].astype(F32), (1, 0)).astype(BF)

    n = nt_ref[0]
    p = jnp.exp2(nn(qk[...], n)).astype(BF)
    p_out[...] = p
    part = nt(n, p)

    @pl.when(t == 0)
    def _():
        acc[...] = part

    @pl.when(t != 0)
    def _():
        acc[...] = acc[...] + part

    @pl.when(t == pl.num_programs(0) - 1)
    def _():
        split_halves(acc, mine, send, core, group)


def split_halves(acc, mine, send, core, group):
    for y in range(2):
        a = pl.multiple_of(2 * group * y + group * core, group)
        b = pl.multiple_of(2 * group * y + group * (1 - core), group)
        mine[:, group * y : group * (y + 1)] = acc[:, pl.ds(a, group)].astype(BF)
        send[:, group * y : group * (y + 1)] = acc[:, pl.ds(b, group)].astype(BF)


def pixel_back_kernel(pos, *refs, chans):
    gv_mine, gv_other, nt_ref, p_ref, qkt_ref = refs[:5]
    refs = refs[5:]
    grad, mine, send, gvt, gv, qktb, acc = refs
    t = pl.program_id(0)
    core = pos[1]
    feat, lats = gv.shape[1], gv.shape[0]
    group = lats // 4
    base = feat - 16

    @pl.when(t == 0)
    def _():
        for ref, c in ((gv_mine, core), (gv_other, 1 - core)):
            for y in range(2):
                at = pl.multiple_of(2 * group * y + group * c, group)
                gvt[:, pl.ds(at, group)] = ref[:, group * y : group * (y + 1)]
        gv[...] = jnp.transpose(gvt[...].astype(F32), (1, 0)).astype(BF)
        qktb[...] = (qkt_ref[...].astype(F32) * LN2).astype(BF)

    n = nt_ref[0]
    p = p_ref[...]
    ds = (p.astype(F32) * nn(gv[...], n)).astype(BF)
    part = nt(n, ds)
    dn = nn(qktb[...], ds) + nn(gvt[...], p)
    nf = n.astype(F32)
    low, high = nf[0:base], nf[base:feat]
    row = lax.broadcasted_iota(jnp.int32, high.shape, 0) + base
    inv = jnp.sum(
        jnp.where((row == chans + 2) | (row == chans + 3), high, 0.0), axis=0, keepdims=True
    )
    high = jnp.where(row < chans, high, 0.0)
    m2 = (
        jnp.sum(dn[0:base] * low, axis=0, keepdims=True)
        + jnp.sum(dn[base:feat] * high, axis=0, keepdims=True)
    ) / chans
    grad[0, 0:base, :] = (inv * (dn[0:base] - low * m2)).astype(BF)
    grad[0, base:feat, :] = (inv * (dn[base:feat] - high * m2)).astype(BF)

    @pl.when(t == 0)
    def _():
        acc[...] = part

    @pl.when(t != 0)
    def _():
        acc[...] = acc[...] + part

    @pl.when(t == pl.num_programs(0) - 1)
    def _():
        split_halves(acc, mine, send, core, group)


def interleave_kernel(src, out, wide):
    chans, images = out.shape[:2]
    for i in range(images):
        wide[:, i, :] = src[i, 0:chans, :].astype(F32)
    out[...] = wide[...].astype(BF)


def matrix_kernel(pos, *refs, units, items, pix):
    z, y, core, it = pos[2], pos[3], pos[1], pos[4]
    pairs = [(refs[2 * u], refs[2 * u + 1]) for u in range(units)]
    outs = refs[2 * units : 2 * units + 2 * items]
    scr, sel = refs[2 * units + 2 * items :]
    width = scr.shape[0]
    part = width // items
    quarter = part // 4
    each = quarter // pix
    at_col = 0
    for left, right in pairs:
        cols = right.shape[1]
        scr[...] = jnp.transpose(left[...].astype(F32), (1, 0))
        for cc in range(2):
            for k in range(items):
                for kp in range(pix):
                    off = (
                        lax.rem(it + k, items) * part
                        + (2 * y + (core ^ cc)) * quarter
                        + lax.rem(z + kp, pix) * each
                    )
                    to = k * quarter + kp * each
                    sel[to : to + each, :] = scr[pl.ds(pl.multiple_of(off, each), each), :]
            res = nn(sel[...].astype(BF), right[...]).astype(BF)
            for k in range(items):
                outs[cc * items + k][:, at_col : at_col + cols] = res[
                    k * quarter : (k + 1) * quarter
                ]
        at_col += cols


def first_kernel(pos, a_mine, a_recv, lc_mine, lc_recv, gcol, wv, co, g1, fu, fd, gs, si,
                 att_out, tot_out, res1_out, nt2_out, hid1_out, act1_out, res2_out, nt3_out, q_out, kv_out, lat):
    y = pos[3]
    half = lc_mine.shape[0] // 2
    width = lat.shape[1]
    chans = wv.shape[0]
    lat[pl.ds(pl.multiple_of(half * y, half), half), :] = lc_mine[0:half, :]
    lat[pl.ds(pl.multiple_of(half * (1 - y), half), half), :] = lc_recv[0:half, :]
    a = a_mine[...].astype(F32) + a_recv[...].astype(F32)
    tot = a[chans : chans + 1, :]
    att = a[0:chans, :] / tot
    att_out[...] = att
    tot_out[...] = tot
    mixed = tn((att * gcol[...]).astype(BF), wv[...]).astype(BF)
    res1 = lat[...].astype(F32) + nn(mixed, co[...])
    res1_out[...] = res1
    n2, _ = stats(res1)
    nt2 = (n2 * g1[...]).astype(BF)
    nt2_out[...] = nt2
    hid = nn(nt2, fu[...])
    hid1_out[...] = hid
    act = gelu(hid).astype(BF)
    act1_out[...] = act
    res2 = res1 + nn(act, fd[...])
    res2_out[...] = res2
    n3, _ = stats(res2)
    nt3 = (n3 * gs[...]).astype(BF)
    nt3_out[...] = nt3
    kv_out[...] = nn(nt3, si[:, width : 3 * width]).astype(BF)
    q_out[...] = nn(nt3, si[:, 0:width]).astype(BF)


def to_pix(outs, rows_ref, start, z):
    n = len(outs)
    each = outs[0].shape[0]
    for r in range(n):
        at = pl.multiple_of(start + lax.rem(z + r, n) * each, each)
        outs[r][...] = rows_ref[pl.ds(at, each), :].astype(BF)


def second_kernel(pos, q, kv, kv2, res2, lc_mine, lc_recv, so, g2, su, sd,
                  out0, out1, out2, out3, selfr_out, sent3_out, back3_out, nt4_out, act2_out, hg2_out, gain_out, dq_out, dkv_out, dkv2_out, cot,
                  prob, mixed_scr, tots, mixed_out):
    y = pos[3]
    half = lc_mine.shape[0] // 2
    rows, width = res2.shape
    hd = width // HEADS
    hs = 1.0 / math.sqrt(hd)
    cot[pl.ds(pl.multiple_of(half * y, half), half), :] = lc_mine[half : 2 * half, :]
    cot[pl.ds(pl.multiple_of(half * (1 - y), half), half), :] = lc_recv[half : 2 * half, :]
    for h in range(HEADS):
        cols = slice(h * hd, (h + 1) * hd)
        vcols = slice(width + h * hd, width + (h + 1) * hd)
        qh = q[:, cols]
        pa = jnp.exp2(nt(qh, kv[:, cols]) * (hs * LOG2E))
        pb = jnp.exp2(nt(qh, kv2[:, cols]) * (hs * LOG2E))
        tot = jnp.sum(pa, axis=1, keepdims=True) + jnp.sum(pb, axis=1, keepdims=True)
        pa, pb = pa.astype(BF), pb.astype(BF)
        prob[h, :, 0:rows] = pa
        prob[h, :, rows : 2 * rows] = pb
        rt = 1.0 / tot
        tots[h] = rt
        mixed_scr[:, cols] = (nn(pa, kv[:, vcols]) + nn(pb, kv2[:, vcols])) * rt
    selfr = mixed_scr[...].astype(BF)
    selfr_out[...] = selfr
    res3 = res2[...] + nn(selfr, so[...])
    n4, r4 = stats(res3)
    nt4 = (n4 * g2[...]).astype(BF)
    nt4_out[...] = nt4
    hid = nn(nt4, su[...])
    act = gelu(hid).astype(BF)
    act2_out[...] = act
    mixed_out[...] = res3 + nn(act, sd[...])
    to_pix((out0, out1, out2, out3), mixed_out, half * y, pos[2])
    hg = (nt(cot[...], sd[...]) * gelu_grad(hid)).astype(BF)
    hg2_out[...] = hg
    ng = nt(hg, su[...])
    gain_out[...] = jnp.sum(ng * n4, axis=0, keepdims=True)
    back3 = cot[...].astype(F32) + norm_back(ng * g2[...], n4, r4)
    back3_out[...] = back3
    sent3 = back3.astype(BF)
    sent3_out[...] = sent3
    mg_all = nt(sent3, so[...]).astype(BF)
    for h in range(HEADS):
        cols = slice(h * hd, (h + 1) * hd)
        vcols = slice(width + h * hd, width + (h + 1) * hd)
        mg = mg_all[:, cols].astype(F32)
        rt = tots[h]
        ng_h = (mg * rt).astype(BF)
        tg = -jnp.sum(mg * mixed_scr[:, cols], axis=1, keepdims=True) * rt
        qh = q[:, cols]
        dq = None
        for src, dst, at in ((kv, dkv_out, 0), (kv2, dkv2_out, rows)):
            p = prob[h, :, at : at + rows]
            sg = (p.astype(F32) * (nt(ng_h, src[:, vcols]) + tg)).astype(BF)
            d = nn(sg, src[:, cols])
            dq = d if dq is None else dq + d
            dst[:, cols] = (tn(sg, qh) * hs).astype(dst.dtype)
            dst[:, vcols] = tn(p, ng_h).astype(dst.dtype)
        dq_out[:, cols] = (dq * hs).astype(BF)


def third_kernel(pos, dq, dkv, dkv2, back3, res2, res1, hid1, att, tot, gcol, wv, co, g1, fu, fd, gs, si, gain2,
                 pg_out, sent2_out, hg1_out, back1_out, gv_out, ht_give, ht_keep, scr, back1_scr, *, items):
    rows, width = back3.shape
    chans = wv.shape[0]
    feat = scr.shape[0]
    base = feat - 16
    pg_out[:, 0:width] = dq[...]
    pg_out[:, width : 3 * width] = (dkv[...] + dkv2[...].astype(F32)).astype(BF)
    ng = nt(pg_out[...], si[...])
    n3, r3 = stats(res2[...])
    gain_self = jnp.sum(ng * n3, axis=0, keepdims=True)
    back2 = back3[...] + norm_back(ng * gs[...], n3, r3)
    sent2 = back2.astype(BF)
    sent2_out[...] = sent2
    hg = (nt(sent2, fd[...]) * gelu_grad(hid1[...])).astype(BF)
    hg1_out[...] = hg
    ng = nt(hg, fu[...])
    n2, r2 = stats(res1[...])
    gain_first = jnp.sum(ng * n2, axis=0, keepdims=True)
    back1 = back2 + norm_back(ng * g1[...], n2, r2)
    back1_scr[...] = back1
    half = rows // 2
    back1_out[...] = back1_scr[pl.ds(pl.multiple_of(half * pos[3], half), half), :]
    sent1 = back1.astype(BF)
    ag = nt(sent1, co[...]).astype(BF)
    rt = 1.0 / tot[...]
    raw = nt(wv[...], ag) * (rt * gcol[...])
    tg = -jnp.sum(att[...] * raw, axis=0, keepdims=True)
    raw = raw - jnp.sum(raw, axis=0, keepdims=True) / chans
    scr[...] = jnp.zeros(scr.shape, F32)
    scr[0:chans, :] = raw
    gv_out[0:base, :] = scr[0:base, :].astype(BF)
    row = lax.broadcasted_iota(jnp.int32, (16, rows), 0) + base
    tg_high = tg.astype(BF).astype(F32)
    high = jnp.where(row == chans, tg_high, scr[base:feat, :])
    high = jnp.where(row == chans + 1, tg - tg_high, high)
    gv_out[base:feat, :] = high.astype(BF)
    scr[0:chans, :] = att[...]
    ht = nn(scr[...].astype(BF), sent1)
    row = lax.broadcasted_iota(jnp.int32, (16, width), 0) + base
    high = ht[base:feat]
    for k, v in enumerate((gain_first, gain_self, gain2[...])):
        v_high = v.astype(BF).astype(F32)
        high = jnp.where(row == chans + 2 * k, v_high, high)
        high = jnp.where(row == chans + 2 * k + 1, v - v_high, high)
    lanes = width // (4 * items)
    for i in range(items):
        for q in range(4):
            k = lax.rem(i - pos[4] + items, items)
            cut = slice(i * 4 * lanes + q * lanes, i * 4 * lanes + (q + 1) * lanes)

            @pl.when((q // 2 == pos[3]) & (q % 2 == pos[1]))
            def _():
                ht_keep[k, 0:base, :] = ht[0:base, cut].astype(BF)
                ht_keep[k, base:feat, :] = high[:, cut].astype(BF)

            @pl.when((q // 2 == pos[3]) & (q % 2 != pos[1]))
            def _():
                ht_give[k, 0:base, :] = ht[0:base, cut].astype(BF)
                ht_give[k, base:feat, :] = high[:, cut].astype(BF)


def last_kernel(pos, b_mine, b_recv, lat, back1, gain, gcol, wq, wk, out0, out1, out2, out3, gt_keep, *refs, scale, items):
    gt_give, scr, out_scr = refs
    chans, width = wk.shape
    feat = scr.shape[0]
    base = feat - 16
    b = (b_mine[...].astype(F32) + b_recv[...].astype(F32)) * scale
    bs = b[0:chans, :]
    rows_grad = tn((bs * gcol[...]).astype(BF), wk[...]).astype(BF)
    ng = nt(rows_grad, wq[...])
    n, r = stats(lat[0 : back1.shape[0], :].astype(F32))
    rounded = (n * gain[...]).astype(BF)
    gain_grad = jnp.sum(ng * n, axis=0, keepdims=True)
    out_scr[...] = back1[...] + norm_back(ng * gain[...], n, r)
    to_pix((out0, out1, out2, out3), out_scr, 0, pos[2])
    scr[...] = jnp.zeros(scr.shape, F32)
    scr[0:chans, :] = bs
    gt = nn(scr[...].astype(BF), rounded)
    row = lax.broadcasted_iota(jnp.int32, (16, width), 0) + base
    high = gt[base:feat]
    g_high = gain_grad.astype(BF).astype(F32)
    high = jnp.where(row == chans, g_high, high)
    high = jnp.where(row == chans + 1, gain_grad - g_high, high)
    lanes = width // (4 * items)
    for i in range(items):
        for q in range(4):
            k = lax.rem(i - pos[4] + items, items)
            yr = (q // 2) ^ pos[3]
            cut = slice(i * 4 * lanes + q * lanes, i * 4 * lanes + (q + 1) * lanes)

            @pl.when(q % 2 == pos[1])
            def _():
                gt_keep[yr, k, 0:base, :] = gt[0:base, cut].astype(BF)
                gt_keep[yr, k, base:feat, :] = high[:, cut].astype(BF)

            @pl.when(q % 2 != pos[1])
            def _():
                gt_give[yr, k, 0:base, :] = gt[0:base, cut].astype(BF)
                gt_give[yr, k, base:feat, :] = high[:, cut].astype(BF)


def columns(pos, width, items):
    lanes = width // (4 * items)
    at = []
    for lr in range(4):
        for k in range(items):
            start = lax.rem(pos[4] + k, items) * 4 * lanes + (pos[0] ^ lr) * lanes
            at.append(pl.multiple_of(start, lanes))
    return at, lanes


def join(full, parts, at, lanes):
    if lanes % 128 == 0:
        for off, part in zip(at, parts):
            full[:, pl.ds(off, lanes)] = part[...].astype(F32)
        return
    r = lax.broadcasted_iota(jnp.int32, (lanes, full.shape[1]), 0)
    c = lax.broadcasted_iota(jnp.int32, (lanes, full.shape[1]), 1)
    full[...] = jnp.zeros(full.shape, F32)
    for off, part in zip(at, parts):
        full[...] = full[...] + nn(part[...], (c == r + off).astype(F32).astype(BF))


def row_sums(prod):
    ones = jnp.ones((8, prod.shape[1]), BF)
    return nt(ones, prod.astype(BF))[0:1]


def home(out, pieces, z):
    n = len(pieces)
    for r in range(n):
        out[lax.rem(z - r + n, n)] = pieces[r][...]


def value_kernel(pos, *refs, items):
    parts, refs = refs[: 4 * items], refs[4 * items :]
    gcol, wv, co, *refs = refs
    home(refs[8], refs[:4], pos[2])
    value_out, cross_out, vsum_out, gains_out, _, full = refs[4:]
    chans, width = wv.shape
    rows = cross_out.shape[0]
    at, lanes = columns(pos, width, items)
    join(full, parts, at, lanes)
    hb = full[0:chans, :].astype(BF)
    for k in range(3):
        lo = chans + 2 * k
        gains_out[k : k + 1, :] = full[lo : lo + 1, :] + full[lo + 1 : lo + 2, :]
    one = own_columns(width, rows, pos[5])
    wsel = (nn(wv[...], one) * gcol[...]).astype(BF)
    cross_out[...] = tn(wsel, hb)
    v = nt(hb, co[...])
    vsum_out[...] = row_sums(v * wv[...].astype(F32))
    value_out[...] = v * gcol[...]


def own_columns(width, rows, index):
    r = lax.broadcasted_iota(jnp.int32, (width, rows), 0)
    c = lax.broadcasted_iota(jnp.int32, (width, rows), 1)
    return (r == c + index * rows).astype(F32).astype(BF)


def key_kernel(pos, *refs, items):
    parts, refs = refs[: 4 * items], refs[4 * items :]
    gcol, wk, wq, vsum, *refs = refs
    home(refs[8], refs[:4], pos[2])
    key_out, query_out, psum_out, gain_out, _, full = refs[4:]
    chans, width = wk.shape
    rows = query_out.shape[0]
    at, lanes = columns(pos, width, items)
    join(full, parts, at, lanes)
    gb = full[0:chans, :].astype(BF)
    gain_out[...] = full[chans : chans + 1, :] + full[chans + 1 : chans + 2, :]
    one = own_columns(lanes, rows, pos[2])
    sel = (nn(parts[0][0:chans, :], one) * gcol[...]).astype(BF)
    query_out[...] = tn(sel, wk[...])
    k = nn(gb, wq[...])
    psum_out[...] = row_sums(k * wk[...].astype(F32)) + vsum[...]
    key_out[...] = k * gcol[...]


def swap(x, kind, lat):
    if kind == "core":
        perm = [(s, s ^ 1) for s in range(lat)]
    else:
        perm = [(s, s ^ 2) for s in range(lat)]
    return lax.ppermute(x, "lat", perm)


def fetch(x, axis, n, r):
    return lax.ppermute(x, axis, [((d + r) % n, d) for d in range(n)])


def send(x, axis, n, r):
    return lax.ppermute(x, axis, [(d, (d + r) % n) for d in range(n)])


def near_first(n):
    return sorted(range(1, n), key=lambda r: min(r, n - r))


def add(*xs):
    total = xs[0].astype(F32)
    for x in xs[1:]:
        total = total + x.astype(F32)
    return total


def low(*xs):
    return add(*xs).astype(BF)


def plane(x, items, lat, y, k, back=False):
    perm = []
    for i in range(items):
        for l in range(lat):
            far = ((i + k) % items) * lat + (l ^ (2 * y))
            near = i * lat + l
            perm.append((far, near) if back else (near, far))
    return lax.ppermute(x, ("item", "lat"), perm)


class AllSum:
    def __init__(self, keep, give, items, pix, lat):
        self.sizes = items, pix, lat
        self.keep, self.give = keep, give
        self.got = swap(give, "core", lat)
        part = lambda y, k: (y, k) if keep.ndim == 4 else (k,)
        ys = 2 if keep.ndim == 4 else 1
        self.sent = {
            (y, k): low(keep[part(y, k)], self.got[part(y, k)])
            for y in range(ys)
            for k in range(items)
            if y or k
        }
        self.arrived = [plane(v, items, lat, *at) for at, v in self.sent.items()]
        self.own = low(keep[part(0, 0)], self.got[part(0, 0)], *self.arrived)
        self.around = [fetch(self.own, "pix", pix, r) for r in near_first(pix)]
        self.total = low(self.own, *self.around)
        near = [
            self.total if not (y or k) else plane(self.total, items, lat, y, k, back=True)
            for y in range(2)
            for k in range(items)
        ]
        far = [swap(v, "core", lat) for v in near]
        self.parts = near[:items] + far[:items] + near[items:] + far[items:]


class Units:
    def __init__(self, pos, units, items, pix, lat, deps=()):
        rows, width = units[0][0].shape
        self.cols = [right.shape[1] for _, right in units]
        total = sum(self.cols)
        quarter = width // (4 * items)
        each = quarter // pix
        self.outs = call(
            lambda *r: matrix_kernel(*r, units=len(units), items=items, pix=pix),
            [((quarter, total), BF)] * (2 * items),
            [pos] + [v for pair in units for v in pair],
            [pltpu.VMEM((width, rows), F32), pltpu.VMEM((width // 4, rows), F32)],
            flops=2 * rows * width * total,
            deps=deps,
        )
        mine, give = self.outs[:items], self.outs[items:]
        got = [swap(v, "core", lat) for v in give]
        self.to_x = [low(mine[k], got[k]) for k in range(1, items)]
        from_x = [send(v, "item", items, k + 1) for k, v in enumerate(self.to_x)]
        here = [mine[0], got[0]] + from_x
        part = lambda v, p: v[p * each : (p + 1) * each]
        self.to_z = {p: low(*[part(v, p) for v in here]) for p in near_first(pix)}
        from_z = [send(v, "pix", pix, p) for p, v in self.to_z.items()]
        x = add(*[part(v, 0) for v in here], *from_z)
        self.grads, at = [], 0
        for c in self.cols:
            self.grads.append(x[:, at : at + c])
            at += c


def body(
    latents,
    pixels,
    size_ids,
    cross_gain,
    pixel_gain,
    query_weight,
    key_weight,
    value_weight,
    cross_output,
    first_gain,
    first_up,
    first_down,
    self_gain,
    self_inputs,
    self_output,
    second_gain,
    second_up,
    second_down,
    cotangent,
):
    images, lat_rows, width = latents.shape
    pix_rows, chans = pixels.shape[1:]
    lat, pix, items = lax.axis_size("lat"), lax.axis_size("pix"), lax.axis_size("item")
    assert lat == 4 and pix == 4 and images == pix
    feat = -(-(chans + 4) // 16) * 16
    l, z, it = lax.axis_index("lat"), lax.axis_index("pix"), lax.axis_index("item")
    core, yy = l % 2, l // 2
    block = l * pix + z
    pos = jnp.stack([l, core, z, yy, it, it * (lat * pix) + block]).astype(jnp.int32)
    rows = images * lat_rows
    lats = lat * rows
    scale = 1.0 / math.sqrt(width)
    factor = jnp.where(size_ids == 0, 25, jnp.where(size_ids == 1, 49, 81)).astype(jnp.int32)
    counts = pix_rows * (lat * pix) * factor // 81 - block * pix_rows
    gcol = pixel_gain.reshape(chans, 1)
    row = lambda v: v.reshape(1, width)

    (qkt,) = call(
        lambda *r: query_kernel(*r, scale=scale),
        [((feat, rows), BF)],
        [latents, row(cross_gain), query_weight, key_weight, gcol],
        [pltpu.VMEM((feat, rows), F32)],
        flops=2 * rows * width * width,
    )
    level = [qkt] + [fetch(qkt, "pix", pix, r) for r in range(1, pix)]

    order = near_first(pix) + [0]
    ptile = min(512, pix_rows // 2)
    feats = jnp.transpose(pixels, (2, 0, 1))

    def norm_half(part, before, deps):
        steps = pix_rows // ptile // 2
        start = part * steps
        ins, specs = [counts, feats], [SM, pl.BlockSpec((chans, images, ptile), lambda t, pos: (0, 0, t + start))]
        if part:
            deps = [before, *deps]
        return pl.pallas_call(
            with_deps(
                lambda *r: pixel_norm_kernel(*r, tile=ptile, start=start), 3, len(deps)
            ),
            grid_spec=pltpu.PrefetchScalarGridSpec(
                num_scalar_prefetch=1,
                grid=(steps,),
                in_specs=specs + [pl.BlockSpec(memory_space=pl.ANY)] * len(deps),
                out_specs=pl.BlockSpec((images, feat, ptile), lambda t, pos: (0, 0, t + start)),
                scratch_shapes=[
                    pltpu.VMEM((chans, images, ptile), F32),
                    pltpu.VMEM((16, ptile), F32),
                ],
            ),
            out_shape=jax.ShapeDtypeStruct((images, feat, pix_rows), BF),
            input_output_aliases={3: 0} if part else {},
            compiler_params=params(),
            cost_estimate=cost(images * pix_rows * 512 * feat, images * pix_rows * feat * 2),
        )(pos, *ins, *deps)

    normed = norm_half(0, None, [qkt])
    outs = call(
        lambda *r: stack_kernel(*r, order=order, images=images),
        [((feat, rows), BF)] * images + [((2 * lat_rows, width), BF)] * images,
        [pos, *level, latents, cotangent],
        deps=[normed],
    )
    feats_of, shares = outs[:images], outs[images:]
    normed = norm_half(1, normed, [feats_of[0]])
    query = {}
    for r in order:
        v = feats_of[r]
        v_y = swap(v, "y", lat)
        query[r] = [v, swap(v, "core", lat), v_y, swap(v_y, "core", lat)]
    shares = [shares[0]] + [send(shares[r], "pix", pix, r) for r in range(1, pix)]

    tile = min(2048, pix_rows)
    tiles = pix_rows // tile
    image_of = lambda r: lambda t, pos: (lax.rem(pos[2] + r, images), 0, t)
    whole = lambda v: pl.BlockSpec(v.shape, lambda t, pos: (0,) * v.ndim)
    half = jax.ShapeDtypeStruct((feat, lats // 2), BF)
    full = jax.ShapeDtypeStruct((feat, lats), BF)
    anyspace = pl.BlockSpec(memory_space=pl.ANY)
    powered, query_all, to_z, from_z, own_a, deps = {}, {}, {}, [], None, []
    for n, r in enumerate(order):
        if n == 1:
            (lc_mine,) = call(
                gather_kernel, [((2 * rows, width), BF)], [pos, *shares], deps=[powered[order[0]]]
            )
            lc_recv = swap(lc_mine, "y", lat)
            deps = [lc_mine]
        if n >= 2:
            deps = [to_z[order[n - 2]], powered[order[n - 1]]]
        powered[r], mine, give, query_all[r] = pl.pallas_call(
            with_deps(cross_kernel, 6, len(deps)),
            grid_spec=pltpu.PrefetchScalarGridSpec(
                num_scalar_prefetch=1,
                grid=(tiles,),
                in_specs=[whole(v) for v in query[r]]
                + [pl.BlockSpec((1, feat, tile), image_of(r))]
                + [anyspace] * len(deps),
                out_specs=(
                    pl.BlockSpec((lats, tile), lambda t, pos: (0, t)),
                    whole(half),
                    whole(half),
                    whole(full),
                ),
                scratch_shapes=[pltpu.VMEM((lats, feat), BF), pltpu.VMEM((feat, lats), F32)],
            ),
            out_shape=(jax.ShapeDtypeStruct((lats, pix_rows), BF), half, half, full),
            compiler_params=params(),
            cost_estimate=cost(pix_rows * 512 * lats * 4, pix_rows * lats * 3),
        )(pos, *query[r], normed, *deps)
        got = swap(give, "core", lat)
        if r:
            to_z[r] = low(mine, got)
            from_z.append(send(to_z[r], "pix", pix, r))
        else:
            own_a = [mine, got]
    a_mine = low(*own_a, *from_z)
    a_recv = swap(a_mine, "y", lat)
    r2 = 2 * rows
    sq = (r2, width)
    att, tot, res1, nt2, hid1, act1, res2, nt3, q, kv = call(
        first_kernel,
        [((chans, r2), F32), ((1, r2), F32), (sq, F32), (sq, BF), (sq, F32), (sq, BF), (sq, F32), (sq, BF), (sq, BF), ((r2, 2 * width), BF)],
        [pos, a_mine, a_recv, lc_mine, lc_recv, gcol, value_weight, cross_output, row(first_gain), first_up, first_down, row(self_gain), self_inputs],
        [pltpu.VMEM(sq, BF)],
        flops=2 * r2 * width * width * 6,
    )
    kv2 = swap(kv, "core", lat)
    piece = ((lat_rows, width), BF)
    *out, selfr, sent3, back3, nt4, act2, hg2, gain2, dq, dkv, dkv_send, cot = call(
        second_kernel,
        [piece] * 4 + [(sq, BF), (sq, BF), (sq, F32), (sq, BF), (sq, BF), (sq, BF), ((1, width), F32), (sq, BF), ((r2, 2 * width), F32), ((r2, 2 * width), BF), (sq, BF)],
        [pos, q, kv, kv2, res2, lc_mine, lc_recv, self_output, row(second_gain), second_up, second_down],
        [
            pltpu.VMEM((HEADS, r2, 2 * r2), BF),
            pltpu.VMEM(sq, F32),
            pltpu.VMEM((HEADS, r2, 1), F32),
            pltpu.VMEM(sq, F32),
        ],
        flops=2 * r2 * width * width * 10,
    )
    dkv2 = swap(dkv_send, "core", lat)
    units_two = Units(pos, [(nt4, hg2), (act2, cot), (selfr, sent3)], items, pix, lat)
    pg, sent2, hg1, back1, gvt, ht_give, ht_keep = call(
        lambda *r: third_kernel(*r, items=items),
        [((r2, 3 * width), BF), (sq, BF), (sq, BF), ((rows, width), F32), ((feat, r2), BF)]
        + [((items, feat, width // (4 * items)), BF)] * 2,
        [pos, dq, dkv, dkv2, back3, res2, res1, hid1, att, tot, gcol, value_weight, cross_output, row(first_gain), first_up, first_down, row(self_gain), self_inputs, gain2],
        [pltpu.VMEM((feat, r2), F32), pltpu.VMEM(sq, F32)],
        flops=2 * r2 * width * width * 7,
        deps=[units_two.outs[0]],
    )
    gv_at = {r: (fetch(gvt, "pix", pix, r) if r else gvt) for r in order}
    units_self = Units(pos, [(nt3, pg)], items, pix, lat)
    units_one = Units(
        pos, [(nt2, hg1), (act1, sent2)], items, pix, lat, deps=[units_self.outs[0]]
    )
    ht = AllSum(ht_keep, ht_give, items, pix, lat)
    held = [
        [units_one.outs[0], *units_two.to_x],
        [*units_self.to_x, *ht.sent.values()],
        [*units_one.to_x, ht.own],
        [*units_two.to_z.values(), ht.total],
    ]

    grad, to_z, from_z, own_b, deps = None, {}, [], None, []
    for n, r in enumerate(order):
        deps = list(held[n])
        if n >= 2:
            deps.append(to_z[order[n - 2]])
        if n:
            deps = [grad] + deps
        ins = [gv_at[r], swap(gv_at[r], "core", lat), normed, powered[r], query_all[r]]
        grad, mine, give = pl.pallas_call(
            with_deps(lambda *a: pixel_back_kernel(*a, chans=chans), 6, len(deps)),
            grid_spec=pltpu.PrefetchScalarGridSpec(
                num_scalar_prefetch=1,
                grid=(tiles,),
                in_specs=[
                    whole(half),
                    whole(half),
                    pl.BlockSpec((1, feat, tile), image_of(r)),
                    pl.BlockSpec((lats, tile), lambda t, pos: (0, t)),
                    whole(full),
                ]
                + [anyspace] * len(deps),
                out_specs=(pl.BlockSpec((1, feat, tile), image_of(r)), whole(half), whole(half)),
                scratch_shapes=[
                    pltpu.VMEM((feat, lats), BF),
                    pltpu.VMEM((lats, feat), BF),
                    pltpu.VMEM((feat, lats), BF),
                    pltpu.VMEM((feat, lats), F32),
                ],
            ),
            out_shape=(jax.ShapeDtypeStruct((images, feat, pix_rows), BF), half, half),
            input_output_aliases={6: 0} if n else {},
            compiler_params=params(),
            cost_estimate=cost(pix_rows * 512 * lats * 8, pix_rows * lats * 3),
        )(pos, *ins, *deps)
        got = swap(give, "core", lat)
        if r:
            to_z[r] = low(mine, got)
            from_z.append(send(to_z[r], "pix", pix, r))
        else:
            own_b = [mine, got]
    own = low(*own_b, *from_z)
    b_mine = lax.dynamic_slice_in_dim(own, yy * rows, rows, 1)
    b_recv = swap(lax.dynamic_slice_in_dim(own, (1 - yy) * rows, rows, 1), "y", lat)

    deal = lambda v: [v[0]] + [send(v[r], "pix", pix, r) for r in range(1, pix)]
    pixel_grad = pl.pallas_call(
        with_deps(interleave_kernel, 1, 1),
        grid=(pix_rows // ptile,),
        in_specs=[pl.BlockSpec((images, feat, ptile), lambda t: (0, 0, t)), anyspace],
        out_specs=pl.BlockSpec((chans, images, ptile), lambda t: (0, 0, t)),
        out_shape=jax.ShapeDtypeStruct((chans, images, pix_rows), BF),
        scratch_shapes=[pltpu.VMEM((chans, images, ptile), F32)],
        compiler_params=params(),
        cost_estimate=cost(0, images * pix_rows * feat * 4),
    )(grad, to_z[order[-2]])

    own_rows = width // (items * lat * pix)
    sums = [((chans, width), F32), ((own_rows, width), F32), ((1, chans), F32)]
    image_rows = [((images, lat_rows, width), BF)]
    value_grad, cross_out_grad, vsum, gains, latents_out = call(
        lambda *r: value_kernel(*r, items=items),
        sums + [((3, width), F32)] + image_rows,
        [pos, *ht.parts, gcol, value_weight, cross_output, *deal(out)],
        [pltpu.VMEM((feat, width), F32)],
        flops=2 * chans * width * width,
        deps=[grad],
    )
    *latent_grad, gt_keep, gt_give = call(
        lambda *r: last_kernel(*r, scale=scale, items=items),
        [piece] * 4 + [((2, items, feat, width // (4 * items)), BF)] * 2,
        [pos, b_mine, b_recv, lc_mine, back1, row(cross_gain), gcol, query_weight, key_weight],
        [pltpu.VMEM((feat, rows), F32), pltpu.VMEM((rows, width), F32)],
        flops=2 * rows * width * width * 2,
        deps=[pixel_grad, vsum],
    )
    pixel_grad = jnp.transpose(pixel_grad, (1, 2, 0))
    gt = AllSum(gt_keep, gt_give, items, pix, lat)
    key_grad, query_grad, psum, cross_gain_grad, latent_grad = call(
        lambda *r: key_kernel(*r, items=items),
        sums + [((1, width), F32)] + image_rows,
        [pos, *gt.parts, gcol, key_weight, query_weight, vsum, *deal(latent_grad)],
        [pltpu.VMEM((feat, width), F32)],
        flops=2 * chans * width * width,
    )
    second_up_grad, second_down_grad, self_out_grad = units_two.grads
    (self_in_grad,) = units_self.grads
    first_up_grad, first_down_grad = units_one.grads
    return (
        latents_out,
        latent_grad,
        pixel_grad,
        query_grad,
        cross_out_grad,
        first_up_grad,
        first_down_grad,
        self_in_grad,
        self_out_grad,
        second_up_grad,
        second_down_grad,
        key_grad,
        value_grad,
        cross_gain_grad.reshape(width),
        psum.reshape(chans),
        gains[0],
        gains[1],
        gains[2],
    )


def params():
    return pltpu.CompilerParams(dimension_semantics=("arbitrary",), vmem_limit_bytes=LIMIT)


def solution(mesh):
    split = P("item", ("lat", "pix"), None)
    in_specs = (split, split, P("item")) + (P(),) * 15 + (split,)
    grads = P(("item", "lat", "pix"), None)
    out_specs = (split, split, split) + (grads,) * 8 + (P(),) * 7
    return jax.shard_map(body, mesh=mesh, in_specs=in_specs, out_specs=out_specs, check_vma=False)
```

```python
import math

import jax
import jax.numpy as jnp
from jax import lax
from jax.experimental import pallas as pl
from jax.experimental.pallas import tpu as pltpu
from jax.sharding import PartitionSpec as P

HEADS = 8
EPS = 1e-05
LOG2E = 1.4426950408889634
LN2 = 0.6931471805599453
BF = jnp.bfloat16
F32 = jnp.float32
VM = pl.BlockSpec(memory_space=pltpu.VMEM)
SM = pl.BlockSpec(memory_space=pltpu.SMEM)
LIMIT = 16 * 1024 * 1024


def nn(a, b):
    return lax.dot_general(a, b, (((1,), (0,)), ((), ())), preferred_element_type=F32)


def nt(a, b):
    return lax.dot_general(a, b, (((1,), (1,)), ((), ())), preferred_element_type=F32)


def tn(a, b):
    return lax.dot_general(a, b, (((0,), (0,)), ((), ())), preferred_element_type=F32)


def stats(v):
    c = v - jnp.mean(v, axis=-1, keepdims=True)
    r = lax.rsqrt(jnp.mean(c * c, axis=-1, keepdims=True) + EPS)
    return c * r, r


def norm_back(scaled, n, r):
    return r * (
        scaled
        - jnp.mean(scaled, axis=-1, keepdims=True)
        - n * jnp.mean(scaled * n, axis=-1, keepdims=True)
    )


K0 = math.sqrt(2.0 / math.pi)
K1 = 0.044715


def gelu(v):
    return 0.5 * v * (1.0 + jnp.tanh(K0 * (v + K1 * v * v * v)))


def gelu_grad(v):
    t = jnp.tanh(K0 * (v + K1 * v * v * v))
    return 0.5 * (1.0 + t) + 0.5 * v * (1.0 - t * t) * (K0 * (1.0 + 3.0 * K1 * v * v))


def cost(flops, nbytes=0):
    return pl.CostEstimate(flops=0, bytes_accessed=0, transcendentals=0)


def with_deps(kernel, n_ins, n_deps):
    if not n_deps:
        return kernel
    return lambda *refs: kernel(*refs[:n_ins], *refs[n_ins + n_deps :])


def call(kernel, outs, ins, scratch=(), flops=0, deps=()):
    return pl.pallas_call(
        with_deps(kernel, len(ins), len(deps)),
        out_shape=tuple(jax.ShapeDtypeStruct(s, d) for s, d in outs),
        in_specs=[SM if a.dtype == jnp.int32 else VM for a in ins]
        + [pl.BlockSpec(memory_space=pl.ANY)] * len(deps),
        out_specs=tuple(VM for _ in outs),
        scratch_shapes=list(scratch),
        compiler_params=pltpu.CompilerParams(vmem_limit_bytes=LIMIT),
        cost_estimate=cost(flops, 4000000),
    )(*ins, *deps)


def query_kernel(lat, gain, wq, wk, gcol, out, scr, *, scale):
    chans = wk.shape[0]
    x = lat[...].astype(F32)
    n, _ = stats(x.reshape(out.shape[1], x.shape[-1]))
    rounded = (n * gain[...]).astype(BF)
    query = nn(rounded, wq[...]).astype(BF)
    t = nt(wk[...], query) * gcol[...]
    t = (t - jnp.sum(t, axis=0, keepdims=True) / chans) * (scale * LOG2E)
    scr[...] = jnp.zeros(scr.shape, F32)
    scr[0:chans, :] = t
    out[...] = scr[...].astype(BF)


def stack_kernel(pos, *refs, order, images):
    level, lat, cot = refs[:images], refs[images], refs[images + 1]
    outs, sends = refs[images + 2 : 2 * images + 2], refs[2 * images + 2 :]
    z = pos[2]
    lat_rows = lat.shape[1]
    wide = [v[...].astype(F32) for v in level]
    slot = lax.broadcasted_iota(jnp.int32, wide[0].shape, 1) // lat_rows
    for r in range(images):
        im = lax.rem(z + r, images)
        total = None
        for rz in range(images):
            s = lax.rem(z + rz, images)
            v = pltpu.roll(wide[rz], lax.rem(s - im + images, images) * lat_rows, 1)
            total = v if total is None else jnp.where(slot == s, v, total)
        outs[r][...] = total.astype(BF)
        sends[r][0:lat_rows, :] = lat[im]
        sends[r][lat_rows : 2 * lat_rows, :] = cot[im]


def gather_kernel(pos, *refs):
    pieces, out = refs[:-1], refs[-1]
    n = len(pieces)
    lat_rows = pieces[0].shape[0] // 2
    for r in range(n):
        src = lax.rem(pos[2] - r + n, n)
        for half in range(2):
            at = pl.multiple_of(half * n * lat_rows + src * lat_rows, lat_rows)
            out[pl.ds(at, lat_rows), :] = pieces[r][half * lat_rows : (half + 1) * lat_rows, :]


def pixel_norm_kernel(pos, cnt, pix, out, wide, tail, *, tile, start):
    t = pl.program_id(0) + start
    chans, images = pix.shape[:2]
    feat = out.shape[1]
    base = feat - 16
    wide[...] = pix[...].astype(F32)
    row = lax.broadcasted_iota(jnp.int32, (16, tile), 0) + base
    lane = lax.broadcasted_iota(jnp.int32, (1, tile), 1) + t * tile
    for i in range(images):
        x = wide[:, i, :]
        x = x - jnp.sum(x, axis=0, keepdims=True) / chans
        var = jnp.sum(x * x, axis=0, keepdims=True) / chans
        valid = jnp.where(lane < cnt[i], 1.0, 0.0)
        inv = lax.rsqrt(var + EPS) * valid
        inv_high = inv.astype(BF).astype(F32)
        x = x * inv
        out[i, 0:base, :] = x[0:base].astype(BF)
        tail[...] = jnp.zeros(tail.shape, F32)
        tail[0 : chans - base, :] = x[base:chans]
        high = tail[...]
        high = jnp.where((row == chans) | (row == chans + 1), valid, high)
        high = jnp.where(row == chans + 2, inv_high, high)
        high = jnp.where(row == chans + 3, inv - inv_high, high)
        out[i, base:feat, :] = high.astype(BF)


def cross_kernel(pos, *refs):
    pieces, refs = refs[:4], refs[4:]
    nt_ref, p_out, mine, send, qkt, qk, acc = refs
    t = pl.program_id(0)
    lpos, core = pos[0], pos[1]
    group = pieces[0].shape[1]

    @pl.when(t == 0)
    def _():
        for rl in range(4):
            at = pl.multiple_of(group * (lpos ^ rl), group)
            qkt[:, pl.ds(at, group)] = pieces[rl][...]
        qk[...] = jnp.transpose(qkt[...].astype(F32), (1, 0)).astype(BF)

    n = nt_ref[0]
    p = jnp.exp2(nn(qk[...], n)).astype(BF)
    p_out[...] = p
    part = nt(n, p)

    @pl.when(t == 0)
    def _():
        acc[...] = part

    @pl.when(t != 0)
    def _():
        acc[...] = acc[...] + part

    @pl.when(t == pl.num_programs(0) - 1)
    def _():
        split_halves(acc, mine, send, core, group)


def split_halves(acc, mine, send, core, group):
    for y in range(2):
        a = pl.multiple_of(2 * group * y + group * core, group)
        b = pl.multiple_of(2 * group * y + group * (1 - core), group)
        mine[:, group * y : group * (y + 1)] = acc[:, pl.ds(a, group)].astype(BF)
        send[:, group * y : group * (y + 1)] = acc[:, pl.ds(b, group)].astype(BF)


def pixel_back_kernel(pos, *refs, chans):
    gv_mine, gv_other, nt_ref, p_ref, qkt_ref = refs[:5]
    refs = refs[5:]
    grad, mine, send, gvt, gv, qktb, acc = refs
    t = pl.program_id(0)
    core = pos[1]
    feat, lats = gv.shape[1], gv.shape[0]
    group = lats // 4
    base = feat - 16

    @pl.when(t == 0)
    def _():
        for ref, c in ((gv_mine, core), (gv_other, 1 - core)):
            for y in range(2):
                at = pl.multiple_of(2 * group * y + group * c, group)
                gvt[:, pl.ds(at, group)] = ref[:, group * y : group * (y + 1)]
        gv[...] = jnp.transpose(gvt[...].astype(F32), (1, 0)).astype(BF)
        qktb[...] = (qkt_ref[...].astype(F32) * LN2).astype(BF)

    n = nt_ref[0]
    p = p_ref[...]
    ds = (p.astype(F32) * nn(gv[...], n)).astype(BF)
    part = nt(n, ds)
    dn = nn(qktb[...], ds) + nn(gvt[...], p)
    nf = n.astype(F32)
    low, high = nf[0:base], nf[base:feat]
    row = lax.broadcasted_iota(jnp.int32, high.shape, 0) + base
    inv = jnp.sum(
        jnp.where((row == chans + 2) | (row == chans + 3), high, 0.0), axis=0, keepdims=True
    )
    high = jnp.where(row < chans, high, 0.0)
    m2 = (
        jnp.sum(dn[0:base] * low, axis=0, keepdims=True)
        + jnp.sum(dn[base:feat] * high, axis=0, keepdims=True)
    ) / chans
    grad[0, 0:base, :] = (inv * (dn[0:base] - low * m2)).astype(BF)
    grad[0, base:feat, :] = (inv * (dn[base:feat] - high * m2)).astype(BF)

    @pl.when(t == 0)
    def _():
        acc[...] = part

    @pl.when(t != 0)
    def _():
        acc[...] = acc[...] + part

    @pl.when(t == pl.num_programs(0) - 1)
    def _():
        split_halves(acc, mine, send, core, group)


def interleave_kernel(src, out, wide):
    chans, images = out.shape[:2]
    for i in range(images):
        wide[:, i, :] = src[i, 0:chans, :].astype(F32)
    out[...] = wide[...].astype(BF)


def matrix_kernel(pos, *refs, units, items, pix):
    z, y, core, it = pos[2], pos[3], pos[1], pos[4]
    pairs = [(refs[2 * u], refs[2 * u + 1]) for u in range(units)]
    outs = refs[2 * units : 2 * units + 2 * items]
    scr, sel = refs[2 * units + 2 * items :]
    width = scr.shape[0]
    part = width // items
    quarter = part // 4
    each = quarter // pix
    at_col = 0
    for left, right in pairs:
        cols = right.shape[1]
        scr[...] = jnp.transpose(left[...].astype(F32), (1, 0))
        for cc in range(2):
            for k in range(items):
                for kp in range(pix):
                    off = (
                        lax.rem(it + k, items) * part
                        + (2 * y + (core ^ cc)) * quarter
                        + lax.rem(z + kp, pix) * each
                    )
                    to = k * quarter + kp * each
                    sel[to : to + each, :] = scr[pl.ds(pl.multiple_of(off, each), each), :]
            res = nn(sel[...].astype(BF), right[...]).astype(BF)
            for k in range(items):
                outs[cc * items + k][:, at_col : at_col + cols] = res[
                    k * quarter : (k + 1) * quarter
                ]
        at_col += cols


def first_kernel(pos, a_mine, a_recv, lc_mine, lc_recv, gcol, wv, co, g1, fu, fd, gs, si,
                 att_out, tot_out, res1_out, nt2_out, hid1_out, act1_out, res2_out, nt3_out, q_out, kv_out, lat):
    y = pos[3]
    half = lc_mine.shape[0] // 2
    width = lat.shape[1]
    chans = wv.shape[0]
    lat[pl.ds(pl.multiple_of(half * y, half), half), :] = lc_mine[0:half, :]
    lat[pl.ds(pl.multiple_of(half * (1 - y), half), half), :] = lc_recv[0:half, :]
    a = a_mine[...].astype(F32) + a_recv[...].astype(F32)
    tot = a[chans : chans + 1, :]
    att = a[0:chans, :] / tot
    att_out[...] = att
    tot_out[...] = tot
    mixed = tn((att * gcol[...]).astype(BF), wv[...]).astype(BF)
    res1 = lat[...].astype(F32) + nn(mixed, co[...])
    res1_out[...] = res1
    n2, _ = stats(res1)
    nt2 = (n2 * g1[...]).astype(BF)
    nt2_out[...] = nt2
    hid = nn(nt2, fu[...])
    hid1_out[...] = hid
    act = gelu(hid).astype(BF)
    act1_out[...] = act
    res2 = res1 + nn(act, fd[...])
    res2_out[...] = res2
    n3, _ = stats(res2)
    nt3 = (n3 * gs[...]).astype(BF)
    nt3_out[...] = nt3
    kv_out[...] = nn(nt3, si[:, width : 3 * width]).astype(BF)
    q_out[...] = nn(nt3, si[:, 0:width]).astype(BF)


def to_pix(outs, rows_ref, start, z):
    n = len(outs)
    each = outs[0].shape[0]
    for r in range(n):
        at = pl.multiple_of(start + lax.rem(z + r, n) * each, each)
        outs[r][...] = rows_ref[pl.ds(at, each), :].astype(BF)


def second_kernel(pos, q, kv, kv2, res2, lc_mine, lc_recv, so, g2, su, sd,
                  out0, out1, out2, out3, selfr_out, sent3_out, back3_out, nt4_out, act2_out, hg2_out, gain_out, dq_out, dkv_out, dkv2_out, cot,
                  prob, mixed_scr, tots, mixed_out):
    y = pos[3]
    half = lc_mine.shape[0] // 2
    rows, width = res2.shape
    hd = width // HEADS
    hs = 1.0 / math.sqrt(hd)
    cot[pl.ds(pl.multiple_of(half * y, half), half), :] = lc_mine[half : 2 * half, :]
    cot[pl.ds(pl.multiple_of(half * (1 - y), half), half), :] = lc_recv[half : 2 * half, :]
    for h in range(HEADS):
        cols = slice(h * hd, (h + 1) * hd)
        vcols = slice(width + h * hd, width + (h + 1) * hd)
        qh = q[:, cols]
        pa = jnp.exp2(nt(qh, kv[:, cols]) * (hs * LOG2E))
        pb = jnp.exp2(nt(qh, kv2[:, cols]) * (hs * LOG2E))
        tot = jnp.sum(pa, axis=1, keepdims=True) + jnp.sum(pb, axis=1, keepdims=True)
        pa, pb = pa.astype(BF), pb.astype(BF)
        prob[h, :, 0:rows] = pa
        prob[h, :, rows : 2 * rows] = pb
        rt = 1.0 / tot
        tots[h] = rt
        mixed_scr[:, cols] = (nn(pa, kv[:, vcols]) + nn(pb, kv2[:, vcols])) * rt
    selfr = mixed_scr[...].astype(BF)
    selfr_out[...] = selfr
    res3 = res2[...] + nn(selfr, so[...])
    n4, r4 = stats(res3)
    nt4 = (n4 * g2[...]).astype(BF)
    nt4_out[...] = nt4
    hid = nn(nt4, su[...])
    act = gelu(hid).astype(BF)
    act2_out[...] = act
    mixed_out[...] = res3 + nn(act, sd[...])
    to_pix((out0, out1, out2, out3), mixed_out, half * y, pos[2])
    hg = (nt(cot[...], sd[...]) * gelu_grad(hid)).astype(BF)
    hg2_out[...] = hg
    ng = nt(hg, su[...])
    gain_out[...] = jnp.sum(ng * n4, axis=0, keepdims=True)
    back3 = cot[...].astype(F32) + norm_back(ng * g2[...], n4, r4)
    back3_out[...] = back3
    sent3 = back3.astype(BF)
    sent3_out[...] = sent3
    mg_all = nt(sent3, so[...]).astype(BF)
    for h in range(HEADS):
        cols = slice(h * hd, (h + 1) * hd)
        vcols = slice(width + h * hd, width + (h + 1) * hd)
        mg = mg_all[:, cols].astype(F32)
        rt = tots[h]
        ng_h = (mg * rt).astype(BF)
        tg = -jnp.sum(mg * mixed_scr[:, cols], axis=1, keepdims=True) * rt
        qh = q[:, cols]
        dq = None
        for src, dst, at in ((kv, dkv_out, 0), (kv2, dkv2_out, rows)):
            p = prob[h, :, at : at + rows]
            sg = (p.astype(F32) * (nt(ng_h, src[:, vcols]) + tg)).astype(BF)
            d = nn(sg, src[:, cols])
            dq = d if dq is None else dq + d
            dst[:, cols] = (tn(sg, qh) * hs).astype(dst.dtype)
            dst[:, vcols] = tn(p, ng_h).astype(dst.dtype)
        dq_out[:, cols] = (dq * hs).astype(BF)


def third_kernel(pos, dq, dkv, dkv2, back3, res2, res1, hid1, att, tot, gcol, wv, co, g1, fu, fd, gs, si, gain2,
                 pg_out, sent2_out, hg1_out, back1_out, gv_out, ht_give, ht_keep, scr, back1_scr, *, items):
    rows, width = back3.shape
    chans = wv.shape[0]
    feat = scr.shape[0]
    base = feat - 16
    pg_out[:, 0:width] = dq[...]
    pg_out[:, width : 3 * width] = (dkv[...] + dkv2[...].astype(F32)).astype(BF)
    ng = nt(pg_out[...], si[...])
    n3, r3 = stats(res2[...])
    gain_self = jnp.sum(ng * n3, axis=0, keepdims=True)
    back2 = back3[...] + norm_back(ng * gs[...], n3, r3)
    sent2 = back2.astype(BF)
    sent2_out[...] = sent2
    hg = (nt(sent2, fd[...]) * gelu_grad(hid1[...])).astype(BF)
    hg1_out[...] = hg
    ng = nt(hg, fu[...])
    n2, r2 = stats(res1[...])
    gain_first = jnp.sum(ng * n2, axis=0, keepdims=True)
    back1 = back2 + norm_back(ng * g1[...], n2, r2)
    back1_scr[...] = back1
    half = rows // 2
    back1_out[...] = back1_scr[pl.ds(pl.multiple_of(half * pos[3], half), half), :]
    sent1 = back1.astype(BF)
    ag = nt(sent1, co[...]).astype(BF)
    rt = 1.0 / tot[...]
    raw = nt(wv[...], ag) * (rt * gcol[...])
    tg = -jnp.sum(att[...] * raw, axis=0, keepdims=True)
    raw = raw - jnp.sum(raw, axis=0, keepdims=True) / chans
    scr[...] = jnp.zeros(scr.shape, F32)
    scr[0:chans, :] = raw
    gv_out[0:base, :] = scr[0:base, :].astype(BF)
    row = lax.broadcasted_iota(jnp.int32, (16, rows), 0) + base
    tg_high = tg.astype(BF).astype(F32)
    high = jnp.where(row == chans, tg_high, scr[base:feat, :])
    high = jnp.where(row == chans + 1, tg - tg_high, high)
    gv_out[base:feat, :] = high.astype(BF)
    scr[0:chans, :] = att[...]
    ht = nn(scr[...].astype(BF), sent1)
    row = lax.broadcasted_iota(jnp.int32, (16, width), 0) + base
    high = ht[base:feat]
    for k, v in enumerate((gain_first, gain_self, gain2[...])):
        v_high = v.astype(BF).astype(F32)
        high = jnp.where(row == chans + 2 * k, v_high, high)
        high = jnp.where(row == chans + 2 * k + 1, v - v_high, high)
    lanes = width // (4 * items)
    for i in range(items):
        for q in range(4):
            k = lax.rem(i - pos[4] + items, items)
            cut = slice(i * 4 * lanes + q * lanes, i * 4 * lanes + (q + 1) * lanes)

            @pl.when((q // 2 == pos[3]) & (q % 2 == pos[1]))
            def _():
                ht_keep[k, 0:base, :] = ht[0:base, cut].astype(BF)
                ht_keep[k, base:feat, :] = high[:, cut].astype(BF)

            @pl.when((q // 2 == pos[3]) & (q % 2 != pos[1]))
            def _():
                ht_give[k, 0:base, :] = ht[0:base, cut].astype(BF)
                ht_give[k, base:feat, :] = high[:, cut].astype(BF)


def last_kernel(pos, b_mine, b_recv, lat, back1, gain, gcol, wq, wk, out0, out1, out2, out3, gt_keep, *refs, scale, items):
    gt_give, scr, out_scr = refs
    chans, width = wk.shape
    feat = scr.shape[0]
    base = feat - 16
    b = (b_mine[...].astype(F32) + b_recv[...].astype(F32)) * scale
    bs = b[0:chans, :]
    rows_grad = tn((bs * gcol[...]).astype(BF), wk[...]).astype(BF)
    ng = nt(rows_grad, wq[...])
    n, r = stats(lat[0 : back1.shape[0], :].astype(F32))
    rounded = (n * gain[...]).astype(BF)
    gain_grad = jnp.sum(ng * n, axis=0, keepdims=True)
    out_scr[...] = back1[...] + norm_back(ng * gain[...], n, r)
    to_pix((out0, out1, out2, out3), out_scr, 0, pos[2])
    scr[...] = jnp.zeros(scr.shape, F32)
    scr[0:chans, :] = bs
    gt = nn(scr[...].astype(BF), rounded)
    row = lax.broadcasted_iota(jnp.int32, (16, width), 0) + base
    high = gt[base:feat]
    g_high = gain_grad.astype(BF).astype(F32)
    high = jnp.where(row == chans, g_high, high)
    high = jnp.where(row == chans + 1, gain_grad - g_high, high)
    lanes = width // (4 * items)
    for i in range(items):
        for q in range(4):
            k = lax.rem(i - pos[4] + items, items)
            yr = (q // 2) ^ pos[3]
            cut = slice(i * 4 * lanes + q * lanes, i * 4 * lanes + (q + 1) * lanes)

            @pl.when(q % 2 == pos[1])
            def _():
                gt_keep[yr, k, 0:base, :] = gt[0:base, cut].astype(BF)
                gt_keep[yr, k, base:feat, :] = high[:, cut].astype(BF)

            @pl.when(q % 2 != pos[1])
            def _():
                gt_give[yr, k, 0:base, :] = gt[0:base, cut].astype(BF)
                gt_give[yr, k, base:feat, :] = high[:, cut].astype(BF)


def columns(pos, width, items):
    lanes = width // (4 * items)
    at = []
    for lr in range(4):
        for k in range(items):
            start = lax.rem(pos[4] + k, items) * 4 * lanes + (pos[0] ^ lr) * lanes
            at.append(pl.multiple_of(start, lanes))
    return at, lanes


def join(full, parts, at, lanes):
    if lanes % 128 == 0:
        for off, part in zip(at, parts):
            full[:, pl.ds(off, lanes)] = part[...].astype(F32)
        return
    r = lax.broadcasted_iota(jnp.int32, (lanes, full.shape[1]), 0)
    c = lax.broadcasted_iota(jnp.int32, (lanes, full.shape[1]), 1)
    full[...] = jnp.zeros(full.shape, F32)
    for off, part in zip(at, parts):
        full[...] = full[...] + nn(part[...], (c == r + off).astype(F32).astype(BF))


def row_sums(prod):
    ones = jnp.ones((8, prod.shape[1]), BF)
    return nt(ones, prod.astype(BF))[0:1]


def home(out, pieces, z):
    n = len(pieces)
    for r in range(n):
        out[lax.rem(z - r + n, n)] = pieces[r][...]


def value_kernel(pos, *refs, items):
    parts, refs = refs[: 4 * items], refs[4 * items :]
    gcol, wv, co, *refs = refs
    home(refs[8], refs[:4], pos[2])
    value_out, cross_out, vsum_out, gains_out, _, full = refs[4:]
    chans, width = wv.shape
    rows = cross_out.shape[0]
    at, lanes = columns(pos, width, items)
    join(full, parts, at, lanes)
    hb = full[0:chans, :].astype(BF)
    for k in range(3):
        lo = chans + 2 * k
        gains_out[k : k + 1, :] = full[lo : lo + 1, :] + full[lo + 1 : lo + 2, :]
    one = own_columns(width, rows, pos[5])
    wsel = (nn(wv[...], one) * gcol[...]).astype(BF)
    cross_out[...] = tn(wsel, hb)
    v = nt(hb, co[...])
    vsum_out[...] = row_sums(v * wv[...].astype(F32))
    value_out[...] = v * gcol[...]


def own_columns(width, rows, index):
    r = lax.broadcasted_iota(jnp.int32, (width, rows), 0)
    c = lax.broadcasted_iota(jnp.int32, (width, rows), 1)
    return (r == c + index * rows).astype(F32).astype(BF)


def key_kernel(pos, *refs, items):
    parts, refs = refs[: 4 * items], refs[4 * items :]
    gcol, wk, wq, vsum, *refs = refs
    home(refs[8], refs[:4], pos[2])
    key_out, query_out, psum_out, gain_out, _, full = refs[4:]
    chans, width = wk.shape
    rows = query_out.shape[0]
    at, lanes = columns(pos, width, items)
    join(full, parts, at, lanes)
    gb = full[0:chans, :].astype(BF)
    gain_out[...] = full[chans : chans + 1, :] + full[chans + 1 : chans + 2, :]
    one = own_columns(lanes, rows, pos[2])
    sel = (nn(parts[0][0:chans, :], one) * gcol[...]).astype(BF)
    query_out[...] = tn(sel, wk[...])
    k = nn(gb, wq[...])
    psum_out[...] = row_sums(k * wk[...].astype(F32)) + vsum[...]
    key_out[...] = k * gcol[...]


def swap(x, kind, lat):
    if kind == "core":
        perm = [(s, s ^ 1) for s in range(lat)]
    else:
        perm = [(s, s ^ 2) for s in range(lat)]
    return lax.ppermute(x, "lat", perm)


def fetch(x, axis, n, r):
    return lax.ppermute(x, axis, [((d + r) % n, d) for d in range(n)])


def send(x, axis, n, r):
    return lax.ppermute(x, axis, [(d, (d + r) % n) for d in range(n)])


def near_first(n):
    return sorted(range(1, n), key=lambda r: min(r, n - r))


def add(*xs):
    total = xs[0].astype(F32)
    for x in xs[1:]:
        total = total + x.astype(F32)
    return total


def low(*xs):
    return add(*xs).astype(BF)


def plane(x, items, lat, y, k, back=False):
    perm = []
    for i in range(items):
        for l in range(lat):
            far = ((i + k) % items) * lat + (l ^ (2 * y))
            near = i * lat + l
            perm.append((far, near) if back else (near, far))
    return lax.ppermute(x, ("item", "lat"), perm)


class AllSum:
    def __init__(self, keep, give, items, pix, lat):
        self.sizes = items, pix, lat
        self.keep, self.give = keep, give
        self.got = swap(give, "core", lat)
        part = lambda y, k: (y, k) if keep.ndim == 4 else (k,)
        ys = 2 if keep.ndim == 4 else 1
        self.sent = {
            (y, k): low(keep[part(y, k)], self.got[part(y, k)])
            for y in range(ys)
            for k in range(items)
            if y or k
        }
        self.arrived = [plane(v, items, lat, *at) for at, v in self.sent.items()]
        self.own = low(keep[part(0, 0)], self.got[part(0, 0)], *self.arrived)
        self.around = [fetch(self.own, "pix", pix, r) for r in near_first(pix)]
        self.total = low(self.own, *self.around)
        near = [
            self.total if not (y or k) else plane(self.total, items, lat, y, k, back=True)
            for y in range(2)
            for k in range(items)
        ]
        far = [swap(v, "core", lat) for v in near]
        self.parts = near[:items] + far[:items] + near[items:] + far[items:]


class Units:
    def __init__(self, pos, units, items, pix, lat, deps=()):
        rows, width = units[0][0].shape
        self.cols = [right.shape[1] for _, right in units]
        total = sum(self.cols)
        quarter = width // (4 * items)
        each = quarter // pix
        self.outs = call(
            lambda *r: matrix_kernel(*r, units=len(units), items=items, pix=pix),
            [((quarter, total), BF)] * (2 * items),
            [pos] + [v for pair in units for v in pair],
            [pltpu.VMEM((width, rows), F32), pltpu.VMEM((width // 4, rows), F32)],
            flops=2 * rows * width * total,
            deps=deps,
        )
        mine, give = self.outs[:items], self.outs[items:]
        got = [swap(v, "core", lat) for v in give]
        self.to_x = [low(mine[k], got[k]) for k in range(1, items)]
        from_x = [send(v, "item", items, k + 1) for k, v in enumerate(self.to_x)]
        here = [mine[0], got[0]] + from_x
        part = lambda v, p: v[p * each : (p + 1) * each]
        self.to_z = {p: low(*[part(v, p) for v in here]) for p in near_first(pix)}
        from_z = [send(v, "pix", pix, p) for p, v in self.to_z.items()]
        x = add(*[part(v, 0) for v in here], *from_z)
        self.grads, at = [], 0
        for c in self.cols:
            self.grads.append(x[:, at : at + c])
            at += c


def body(
    latents,
    pixels,
    size_ids,
    cross_gain,
    pixel_gain,
    query_weight,
    key_weight,
    value_weight,
    cross_output,
    first_gain,
    first_up,
    first_down,
    self_gain,
    self_inputs,
    self_output,
    second_gain,
    second_up,
    second_down,
    cotangent,
):
    images, lat_rows, width = latents.shape
    pix_rows, chans = pixels.shape[1:]
    lat, pix, items = lax.axis_size("lat"), lax.axis_size("pix"), lax.axis_size("item")
    assert lat == 4 and pix == 4 and images == pix
    feat = -(-(chans + 4) // 16) * 16
    l, z, it = lax.axis_index("lat"), lax.axis_index("pix"), lax.axis_index("item")
    core, yy = l % 2, l // 2
    block = l * pix + z
    pos = jnp.stack([l, core, z, yy, it, it * (lat * pix) + block]).astype(jnp.int32)
    rows = images * lat_rows
    lats = lat * rows
    scale = 1.0 / math.sqrt(width)
    factor = jnp.where(size_ids == 0, 25, jnp.where(size_ids == 1, 49, 81)).astype(jnp.int32)
    counts = pix_rows * (lat * pix) * factor // 81 - block * pix_rows
    gcol = pixel_gain.reshape(chans, 1)
    row = lambda v: v.reshape(1, width)

    (qkt,) = call(
        lambda *r: query_kernel(*r, scale=scale),
        [((feat, rows), BF)],
        [latents, row(cross_gain), query_weight, key_weight, gcol],
        [pltpu.VMEM((feat, rows), F32)],
        flops=2 * rows * width * width,
    )
    level = [qkt] + [fetch(qkt, "pix", pix, r) for r in range(1, pix)]

    order = near_first(pix) + [0]
    ptile = min(512, pix_rows // 2)
    feats = jnp.transpose(pixels, (2, 0, 1))

    def norm_half(part, before, deps):
        steps = pix_rows // ptile // 2
        start = part * steps
        ins, specs = [counts, feats], [SM, pl.BlockSpec((chans, images, ptile), lambda t, pos: (0, 0, t + start))]
        if part:
            deps = [before, *deps]
        return pl.pallas_call(
            with_deps(
                lambda *r: pixel_norm_kernel(*r, tile=ptile, start=start), 3, len(deps)
            ),
            grid_spec=pltpu.PrefetchScalarGridSpec(
                num_scalar_prefetch=1,
                grid=(steps,),
                in_specs=specs + [pl.BlockSpec(memory_space=pl.ANY)] * len(deps),
                out_specs=pl.BlockSpec((images, feat, ptile), lambda t, pos: (0, 0, t + start)),
                scratch_shapes=[
                    pltpu.VMEM((chans, images, ptile), F32),
                    pltpu.VMEM((16, ptile), F32),
                ],
            ),
            out_shape=jax.ShapeDtypeStruct((images, feat, pix_rows), BF),
            input_output_aliases={3: 0} if part else {},
            compiler_params=params(),
            cost_estimate=cost(images * pix_rows * 512 * feat, images * pix_rows * feat * 2),
        )(pos, *ins, *deps)

    normed = norm_half(0, None, [qkt])
    outs = call(
        lambda *r: stack_kernel(*r, order=order, images=images),
        [((feat, rows), BF)] * images + [((2 * lat_rows, width), BF)] * images,
        [pos, *level, latents, cotangent],
        deps=[normed],
    )
    feats_of, shares = outs[:images], outs[images:]
    normed = norm_half(1, normed, [feats_of[0]])
    query = {}
    for r in order:
        v = feats_of[r]
        v_y = swap(v, "y", lat)
        query[r] = [v, swap(v, "core", lat), v_y, swap(v_y, "core", lat)]
    shares = [shares[0]] + [send(shares[r], "pix", pix, r) for r in range(1, pix)]

    tile = min(2048, pix_rows)
    tiles = pix_rows // tile
    image_of = lambda r: lambda t, pos: (lax.rem(pos[2] + r, images), 0, t)
    whole = lambda v: pl.BlockSpec(v.shape, lambda t, pos: (0,) * v.ndim)
    half = jax.ShapeDtypeStruct((feat, lats // 2), BF)
    full = jax.ShapeDtypeStruct((feat, lats), BF)
    anyspace = pl.BlockSpec(memory_space=pl.ANY)
    powered, query_all, to_z, from_z, own_a, deps = {}, {}, {}, [], None, []
    for n, r in enumerate(order):
        if n == 1:
            (lc_mine,) = call(
                gather_kernel, [((2 * rows, width), BF)], [pos, *shares], deps=[powered[order[0]]]
            )
            lc_recv = swap(lc_mine, "y", lat)
            deps = [lc_mine]
        if n >= 2:
            deps = [to_z[order[n - 2]], powered[order[n - 1]]]
        powered[r], mine, give, query_all[r] = pl.pallas_call(
            with_deps(cross_kernel, 6, len(deps)),
            grid_spec=pltpu.PrefetchScalarGridSpec(
                num_scalar_prefetch=1,
                grid=(tiles,),
                in_specs=[whole(v) for v in query[r]]
                + [pl.BlockSpec((1, feat, tile), image_of(r))]
                + [anyspace] * len(deps),
                out_specs=(
                    pl.BlockSpec((lats, tile), lambda t, pos: (0, t)),
                    whole(half),
                    whole(half),
                    whole(full),
                ),
                scratch_shapes=[pltpu.VMEM((lats, feat), BF), pltpu.VMEM((feat, lats), F32)],
            ),
            out_shape=(jax.ShapeDtypeStruct((lats, pix_rows), BF), half, half, full),
            compiler_params=params(),
            cost_estimate=cost(pix_rows * 512 * lats * 4, pix_rows * lats * 3),
        )(pos, *query[r], normed, *deps)
        got = swap(give, "core", lat)
        if r:
            to_z[r] = low(mine, got)
            from_z.append(send(to_z[r], "pix", pix, r))
        else:
            own_a = [mine, got]
    a_mine = low(*own_a, *from_z)
    a_recv = swap(a_mine, "y", lat)
    r2 = 2 * rows
    sq = (r2, width)
    att, tot, res1, nt2, hid1, act1, res2, nt3, q, kv = call(
        first_kernel,
        [((chans, r2), F32), ((1, r2), F32), (sq, F32), (sq, BF), (sq, F32), (sq, BF), (sq, F32), (sq, BF), (sq, BF), ((r2, 2 * width), BF)],
        [pos, a_mine, a_recv, lc_mine, lc_recv, gcol, value_weight, cross_output, row(first_gain), first_up, first_down, row(self_gain), self_inputs],
        [pltpu.VMEM(sq, BF)],
        flops=2 * r2 * width * width * 6,
    )
    kv2 = swap(kv, "core", lat)
    piece = ((lat_rows, width), BF)
    *out, selfr, sent3, back3, nt4, act2, hg2, gain2, dq, dkv, dkv_send, cot = call(
        second_kernel,
        [piece] * 4 + [(sq, BF), (sq, BF), (sq, F32), (sq, BF), (sq, BF), (sq, BF), ((1, width), F32), (sq, BF), ((r2, 2 * width), F32), ((r2, 2 * width), BF), (sq, BF)],
        [pos, q, kv, kv2, res2, lc_mine, lc_recv, self_output, row(second_gain), second_up, second_down],
        [
            pltpu.VMEM((HEADS, r2, 2 * r2), BF),
            pltpu.VMEM(sq, F32),
            pltpu.VMEM((HEADS, r2, 1), F32),
            pltpu.VMEM(sq, F32),
        ],
        flops=2 * r2 * width * width * 10,
    )
    dkv2 = swap(dkv_send, "core", lat)
    units_two = Units(pos, [(nt4, hg2), (act2, cot), (selfr, sent3)], items, pix, lat)
    pg, sent2, hg1, back1, gvt, ht_give, ht_keep = call(
        lambda *r: third_kernel(*r, items=items),
        [((r2, 3 * width), BF), (sq, BF), (sq, BF), ((rows, width), F32), ((feat, r2), BF)]
        + [((items, feat, width // (4 * items)), BF)] * 2,
        [pos, dq, dkv, dkv2, back3, res2, res1, hid1, att, tot, gcol, value_weight, cross_output, row(first_gain), first_up, first_down, row(self_gain), self_inputs, gain2],
        [pltpu.VMEM((feat, r2), F32), pltpu.VMEM(sq, F32)],
        flops=2 * r2 * width * width * 7,
        deps=[units_two.outs[0]],
    )
    gv_at = {r: (fetch(gvt, "pix", pix, r) if r else gvt) for r in order}
    units_self = Units(pos, [(nt3, pg)], items, pix, lat)
    units_one = Units(
        pos, [(nt2, hg1), (act1, sent2)], items, pix, lat, deps=[units_self.outs[0]]
    )
    ht = AllSum(ht_keep, ht_give, items, pix, lat)
    held = [
        [units_one.outs[0], *units_two.to_x],
        [*units_self.to_x, *ht.sent.values()],
        [*units_one.to_x, ht.own],
        [*units_two.to_z.values(), ht.total],
    ]

    grad, to_z, from_z, own_b, deps = None, {}, [], None, []
    for n, r in enumerate(order):
        deps = list(held[n])
        if n >= 2:
            deps.append(to_z[order[n - 2]])
        if n:
            deps = [grad] + deps
        ins = [gv_at[r], swap(gv_at[r], "core", lat), normed, powered[r], query_all[r]]
        grad, mine, give = pl.pallas_call(
            with_deps(lambda *a: pixel_back_kernel(*a, chans=chans), 6, len(deps)),
            grid_spec=pltpu.PrefetchScalarGridSpec(
                num_scalar_prefetch=1,
                grid=(tiles,),
                in_specs=[
                    whole(half),
                    whole(half),
                    pl.BlockSpec((1, feat, tile), image_of(r)),
                    pl.BlockSpec((lats, tile), lambda t, pos: (0, t)),
                    whole(full),
                ]
                + [anyspace] * len(deps),
                out_specs=(pl.BlockSpec((1, feat, tile), image_of(r)), whole(half), whole(half)),
                scratch_shapes=[
                    pltpu.VMEM((feat, lats), BF),
                    pltpu.VMEM((lats, feat), BF),
                    pltpu.VMEM((feat, lats), BF),
                    pltpu.VMEM((feat, lats), F32),
                ],
            ),
            out_shape=(jax.ShapeDtypeStruct((images, feat, pix_rows), BF), half, half),
            input_output_aliases={6: 0} if n else {},
            compiler_params=params(),
            cost_estimate=cost(pix_rows * 512 * lats * 8, pix_rows * lats * 3),
        )(pos, *ins, *deps)
        got = swap(give, "core", lat)
        if r:
            to_z[r] = low(mine, got)
            from_z.append(send(to_z[r], "pix", pix, r))
        else:
            own_b = [mine, got]
    own = low(*own_b, *from_z)
    b_mine = lax.dynamic_slice_in_dim(own, yy * rows, rows, 1)
    b_recv = swap(lax.dynamic_slice_in_dim(own, (1 - yy) * rows, rows, 1), "y", lat)

    deal = lambda v: [v[0]] + [send(v[r], "pix", pix, r) for r in range(1, pix)]
    pixel_grad = pl.pallas_call(
        with_deps(interleave_kernel, 1, 1),
        grid=(pix_rows // ptile,),
        in_specs=[pl.BlockSpec((images, feat, ptile), lambda t: (0, 0, t)), anyspace],
        out_specs=pl.BlockSpec((chans, images, ptile), lambda t: (0, 0, t)),
        out_shape=jax.ShapeDtypeStruct((chans, images, pix_rows), BF),
        scratch_shapes=[pltpu.VMEM((chans, images, ptile), F32)],
        compiler_params=params(),
        cost_estimate=cost(0, images * pix_rows * feat * 4),
    )(grad, to_z[order[-2]])

    own_rows = width // (items * lat * pix)
    sums = [((chans, width), F32), ((own_rows, width), F32), ((1, chans), F32)]
    image_rows = [((images, lat_rows, width), BF)]
    value_grad, cross_out_grad, vsum, gains, latents_out = call(
        lambda *r: value_kernel(*r, items=items),
        sums + [((3, width), F32)] + image_rows,
        [pos, *ht.parts, gcol, value_weight, cross_output, *deal(out)],
        [pltpu.VMEM((feat, width), F32)],
        flops=2 * chans * width * width,
        deps=[grad],
    )
    *latent_grad, gt_keep, gt_give = call(
        lambda *r: last_kernel(*r, scale=scale, items=items),
        [piece] * 4 + [((2, items, feat, width // (4 * items)), BF)] * 2,
        [pos, b_mine, b_recv, lc_mine, back1, row(cross_gain), gcol, query_weight, key_weight],
        [pltpu.VMEM((feat, rows), F32), pltpu.VMEM((rows, width), F32)],
        flops=2 * rows * width * width * 2,
        deps=[pixel_grad, vsum],
    )
    pixel_grad = jnp.transpose(pixel_grad, (1, 2, 0))
    gt = AllSum(gt_keep, gt_give, items, pix, lat)
    key_grad, query_grad, psum, cross_gain_grad, latent_grad = call(
        lambda *r: key_kernel(*r, items=items),
        sums + [((1, width), F32)] + image_rows,
        [pos, *gt.parts, gcol, key_weight, query_weight, vsum, *deal(latent_grad)],
        [pltpu.VMEM((feat, width), F32)],
        flops=2 * chans * width * width,
    )
    second_up_grad, second_down_grad, self_out_grad = units_two.grads
    (self_in_grad,) = units_self.grads
    first_up_grad, first_down_grad = units_one.grads
    return (
        latents_out,
        latent_grad,
        pixel_grad,
        query_grad,
        cross_out_grad,
        first_up_grad,
        first_down_grad,
        self_in_grad,
        self_out_grad,
        second_up_grad,
        second_down_grad,
        key_grad,
        value_grad,
        cross_gain_grad.reshape(width),
        psum.reshape(chans),
        gains[0],
        gains[1],
        gains[2],
    )


def params():
    return pltpu.CompilerParams(dimension_semantics=("arbitrary",), vmem_limit_bytes=LIMIT)


def solution(mesh):
    split = P("item", ("lat", "pix"), None)
    in_specs = (split, split, P("item")) + (P(),) * 15 + (split,)
    grads = P(("item", "lat", "pix"), None)
    out_specs = (split, split, split) + (grads,) * 8 + (P(),) * 7
    return jax.shard_map(body, mesh=mesh, in_specs=in_specs, out_specs=out_specs, check_vma=False)
```

```python
import math

import jax
import jax.numpy as jnp
from jax import lax
from jax.experimental import pallas as pl
from jax.experimental.pallas import tpu as pltpu
from jax.sharding import PartitionSpec as P

HEADS = 8
EPS = 1e-05
LOG2E = 1.4426950408889634
LN2 = 0.6931471805599453
BF = jnp.bfloat16
F32 = jnp.float32
VM = pl.BlockSpec(memory_space=pltpu.VMEM)
SM = pl.BlockSpec(memory_space=pltpu.SMEM)
ANY = pl.BlockSpec(memory_space=pl.ANY)
WORK = 5 * 10**9
SMALL = 10**9
LIMIT = 12 * 1024 * 1024
WIDE_LIMIT = 16 * 1024 * 1024


def nn(a, b):
    return lax.dot_general(a, b, (((1,), (0,)), ((), ())), preferred_element_type=F32)


def nt(a, b):
    return lax.dot_general(a, b, (((1,), (1,)), ((), ())), preferred_element_type=F32)


def tn(a, b):
    return lax.dot_general(a, b, (((0,), (0,)), ((), ())), preferred_element_type=F32)


def stats(v):
    c = v - jnp.mean(v, axis=-1, keepdims=True)
    r = lax.rsqrt(jnp.mean(c * c, axis=-1, keepdims=True) + EPS)
    return c * r, r


def norm_back(scaled, n, r):
    return r * (
        scaled
        - jnp.mean(scaled, axis=-1, keepdims=True)
        - n * jnp.mean(scaled * n, axis=-1, keepdims=True)
    )


K0 = math.sqrt(2.0 / math.pi)
K1 = 0.044715


def gelu(v):
    return 0.5 * v * (1.0 + jnp.tanh(K0 * (v + K1 * v * v * v)))


def gelu_grad(v):
    t = jnp.tanh(K0 * (v + K1 * v * v * v))
    return 0.5 * (1.0 + t) + 0.5 * v * (1.0 - t * t) * (K0 * (1.0 + 3.0 * K1 * v * v))


class Chain:
    def __init__(self, pos):
        self.pos = pos
        self.token = None

    def run(self, kernel, outs, ins, scratch=(), grid=None, in_specs=None, out_specs=None,
            deps=(), aliases=None, limit=LIMIT, work=WORK):
        before = [] if self.token is None else [self.token]
        n_ins, n_extra, n_outs = len(ins), len(before) + len(deps), len(outs)

        def body(pos, *refs):
            given = refs[:n_ins]
            results = refs[n_ins + n_extra : n_ins + n_extra + n_outs]
            refs[n_ins + n_extra + n_outs][...] = jnp.zeros((8, 128), F32)
            rest = refs[n_ins + n_extra + n_outs + 1 :]
            kernel(pos, *given, *results, *rest)

        fixed = lambda v: pl.BlockSpec(v.shape, lambda t, pos: (0,) * len(v.shape))
        shapes = [jax.ShapeDtypeStruct(*o) for o in outs]
        small = jax.ShapeDtypeStruct((8, 128), F32)
        where = lambda a: SM if a.dtype == jnp.int32 else fixed(a)
        specs = in_specs or [None] * n_ins
        specs = [s if s is not None else where(a) for s, a in zip(specs, ins)]
        o_specs = out_specs or [None] * n_outs
        o_specs = [s if s is not None else fixed(o) for s, o in zip(o_specs, shapes)]
        res = pl.pallas_call(
            body,
            grid_spec=pltpu.PrefetchScalarGridSpec(
                num_scalar_prefetch=1,
                grid=(grid or 1,),
                in_specs=specs + [fixed(v) for v in before] + [ANY] * len(deps),
                out_specs=tuple(o_specs + [fixed(small)]),
                scratch_shapes=list(scratch),
            ),
            out_shape=tuple(shapes + [small]),
            input_output_aliases=aliases or {},
            compiler_params=pltpu.CompilerParams(
                dimension_semantics=("arbitrary",), vmem_limit_bytes=limit
            ),
            cost_estimate=pl.CostEstimate(flops=work, bytes_accessed=100000, transcendentals=0),
        )(self.pos, *ins, *before, *deps)
        self.token = res[-1]
        return list(res[:-1])

    def sums(self, wanted, deps=()):
        arrays, place = [], {}
        for _, terms in wanted:
            for a, _ in terms:
                if id(a) not in place:
                    place[id(a)] = len(arrays)
                    arrays.append(a)
        outs = []
        for dtype, terms in wanted:
            a, index = terms[0]
            outs.append((jax.eval_shape(lambda v, index=index: v[index], a).shape, dtype))

        def kernel(pos, *refs):
            for n, (dtype, terms) in enumerate(wanted):
                total = None
                for a, index in terms:
                    v = refs[place[id(a)]][index].astype(F32)
                    total = v if total is None else total + v
                refs[len(arrays) + n][...] = total.astype(dtype)

        return self.run(kernel, outs, arrays, deps=deps, work=SMALL)


ALL = (Ellipsis,)


def query_kernel(pos, lat, gain, wq, wk, gcol, out, scr, *, scale):
    chans = wk.shape[0]
    x = lat[...].astype(F32)
    n, _ = stats(x.reshape(out.shape[1], x.shape[-1]))
    rounded = (n * gain[...]).astype(BF)
    query = nn(rounded, wq[...]).astype(BF)
    t = nt(wk[...], query) * gcol[...]
    t = (t - jnp.sum(t, axis=0, keepdims=True) / chans) * (scale * LOG2E)
    scr[...] = jnp.zeros(scr.shape, F32)
    scr[0:chans, :] = t
    out[...] = scr[...].astype(BF)


def stack_kernel(pos, *refs, images):
    *level, out = refs
    z = pos[2]
    feat = out.shape[0] // images
    wide = [v[...].astype(F32) for v in level]
    lat_rows = out.shape[1] // images
    slot = lax.broadcasted_iota(jnp.int32, wide[0].shape, 1) // lat_rows
    for r in range(images):
        im = lax.rem(z + r, images)
        total = None
        for rz in range(images):
            s = lax.rem(z + rz, images)
            v = pltpu.roll(wide[rz], lax.rem(s - im + images, images) * lat_rows, 1)
            total = v if total is None else jnp.where(slot == s, v, total)
        out[r * feat : (r + 1) * feat, :] = total.astype(BF)


def share_kernel(pos, lat, cot, *outs):
    n = len(outs)
    lat_rows = lat.shape[1]
    for r in range(n):
        im = lax.rem(pos[2] + r, n)
        outs[r][0:lat_rows, :] = lat[im]
        outs[r][lat_rows : 2 * lat_rows, :] = cot[im]


def gather_kernel(pos, *refs):
    *pieces, out = refs
    n = len(pieces)
    lat_rows = pieces[0].shape[0] // 2
    for r in range(n):
        src = lax.rem(pos[2] - r + n, n)
        for half in range(2):
            at = pl.multiple_of(half * n * lat_rows + src * lat_rows, lat_rows)
            out[pl.ds(at, lat_rows), :] = pieces[r][half * lat_rows : (half + 1) * lat_rows, :]


def column_kernel(pos, row, out):
    n = row.shape[1]
    same = lax.broadcasted_iota(jnp.int32, (n, n), 0) == lax.broadcasted_iota(jnp.int32, (n, n), 1)
    out[...] = jnp.sum(jnp.where(same, row[...], 0.0), axis=1, keepdims=True)


def pixel_norm_kernel(pos, ids, pix, *refs, tile, start, total):
    out, wide, tail = refs[-3:]
    t = pl.program_id(0) + start
    chans, images = pix.shape[:2]
    feat = out.shape[1]
    base = feat - 16
    wide[...] = pix[...].astype(F32)
    row = lax.broadcasted_iota(jnp.int32, (16, tile), 0) + base
    lane = lax.broadcasted_iota(jnp.int32, (1, tile), 1) + t * tile
    for i in range(images):
        x = wide[:, i, :]
        x = x - jnp.sum(x, axis=0, keepdims=True) / chans
        var = jnp.sum(x * x, axis=0, keepdims=True) / chans
        size = jnp.where(ids[i] == 0, 25, jnp.where(ids[i] == 1, 49, 81))
        count = lax.div(total * size, 81) - pos[6]
        valid = jnp.where(lane < count, 1.0, 0.0)
        inv = lax.rsqrt(var + EPS) * valid
        inv_high = inv.astype(BF).astype(F32)
        x = x * inv
        out[i, 0:base, :] = x[0:base].astype(BF)
        tail[...] = jnp.zeros(tail.shape, F32)
        tail[0 : chans - base, :] = x[base:chans]
        high = tail[...]
        high = jnp.where((row == chans) | (row == chans + 1), valid, high)
        high = jnp.where(row == chans + 2, inv_high, high)
        high = jnp.where(row == chans + 3, inv - inv_high, high)
        out[i, base:feat, :] = high.astype(BF)


def cross_kernel(pos, *refs, at):
    pieces, refs = refs[:4], refs[4:]
    nt_ref, p_out, mine, send, qkt, qk, acc = refs
    t = pl.program_id(0)
    lpos, core = pos[0], pos[1]
    group = pieces[0].shape[1]
    feat = qkt.shape[0]
    row = at

    @pl.when(t == 0)
    def _():
        for rl in range(4):
            at = pl.multiple_of(group * (lpos ^ rl), group)
            qkt[:, pl.ds(at, group)] = pieces[rl][row : row + feat, :]
        qk[...] = jnp.transpose(qkt[...].astype(F32), (1, 0)).astype(BF)

    n = nt_ref[0]
    p = jnp.exp2(nn(qk[...], n)).astype(BF)
    p_out[...] = p
    part = nt(n, p)

    @pl.when(t == 0)
    def _():
        acc[...] = part

    @pl.when(t != 0)
    def _():
        acc[...] = acc[...] + part

    @pl.when(t == pl.num_programs(0) - 1)
    def _():
        split_halves(acc, mine, send, core, group)


def split_halves(acc, mine, send, core, group):
    for y in range(2):
        a = pl.multiple_of(2 * group * y + group * core, group)
        b = pl.multiple_of(2 * group * y + group * (1 - core), group)
        mine[:, group * y : group * (y + 1)] = acc[:, pl.ds(a, group)].astype(BF)
        send[:, group * y : group * (y + 1)] = acc[:, pl.ds(b, group)].astype(BF)


def pixel_back_kernel(pos, *refs, chans):
    gv_mine, gv_other, nt_ref, p_ref, qkt_ref = refs[:5]
    refs = refs[-7:]
    grad, mine, send, gvt, gv, qktb, acc = refs
    t = pl.program_id(0)
    core = pos[1]
    feat, lats = gv.shape[1], gv.shape[0]
    group = lats // 4
    base = feat - 16

    @pl.when(t == 0)
    def _():
        for ref, c in ((gv_mine, core), (gv_other, 1 - core)):
            for y in range(2):
                at = pl.multiple_of(2 * group * y + group * c, group)
                gvt[:, pl.ds(at, group)] = ref[:, group * y : group * (y + 1)]
        gv[...] = jnp.transpose(gvt[...].astype(F32), (1, 0)).astype(BF)
        qktb[...] = (qkt_ref[...].astype(F32) * LN2).astype(BF)

    n = nt_ref[0]
    p = p_ref[...]
    ds = (p.astype(F32) * nn(gv[...], n)).astype(BF)
    part = nt(n, ds)
    dn = nn(qktb[...], ds) + nn(gvt[...], p)
    nf = n.astype(F32)
    low, high = nf[0:base], nf[base:feat]
    row = lax.broadcasted_iota(jnp.int32, high.shape, 0) + base
    inv = jnp.sum(
        jnp.where((row == chans + 2) | (row == chans + 3), high, 0.0), axis=0, keepdims=True
    )
    high = jnp.where(row < chans, high, 0.0)
    m2 = (
        jnp.sum(dn[0:base] * low, axis=0, keepdims=True)
        + jnp.sum(dn[base:feat] * high, axis=0, keepdims=True)
    ) / chans
    grad[0, 0:base, :] = (inv * (dn[0:base] - low * m2)).astype(BF)
    grad[0, base:feat, :] = (inv * (dn[base:feat] - high * m2)).astype(BF)

    @pl.when(t == 0)
    def _():
        acc[...] = part

    @pl.when(t != 0)
    def _():
        acc[...] = acc[...] + part

    @pl.when(t == pl.num_programs(0) - 1)
    def _():
        split_halves(acc, mine, send, core, group)


def interleave_kernel(pos, src, out, wide):
    chans, images = out.shape[:2]
    for i in range(images):
        wide[:, i, :] = src[i, 0:chans, :].astype(F32)
    out[...] = wide[...].astype(BF)


def matrix_kernel(pos, *refs, groups, items, pix):
    z, y, core, it = pos[2], pos[3], pos[1], pos[4]
    scr, sel = refs[-2:]
    n_ins = 2 * sum(groups)
    ins, outs = refs[:n_ins], refs[n_ins:-2]
    width = scr.shape[0]
    part = width // items
    quarter = part // 4
    each = quarter // pix
    at = 0
    for g, units in enumerate(groups):
        at_col = 0
        for u in range(units):
            left, right = ins[2 * at], ins[2 * at + 1]
            at += 1
            cols = right.shape[1]
            scr[...] = jnp.transpose(left[...].astype(F32), (1, 0))
            for cc in range(2):
                for k in range(items):
                    for n, kp in enumerate((0, 2, 1, 3)):
                        off = (
                            lax.rem(it + k, items) * part
                            + (2 * y + (core ^ cc)) * quarter
                            + (z ^ kp) * each
                        )
                        to = k * quarter + n * each
                        sel[to : to + each, :] = scr[pl.ds(pl.multiple_of(off, each), each), :]
                res = nn(sel[...].astype(BF), right[...]).astype(BF)
                outs[2 * g + cc][:, at_col : at_col + cols] = res
            at_col += cols


def first_kernel(pos, a_mine, a_recv, lc_mine, lc_recv, gcol, wv, co, g1, fu, fd, gs, si,
                 att_out, tot_out, res1_out, nt2_out, hid1_out, act1_out, res2_out, nt3_out, q_out, kv_out, lat):
    get = (wv, co, fu, fd, si).__getitem__
    y = pos[3]
    half = lc_mine.shape[0] // 2
    width = lat.shape[1]
    chans = wv.shape[0]
    lat[pl.ds(pl.multiple_of(half * y, half), half), :] = lc_mine[0:half, :]
    lat[pl.ds(pl.multiple_of(half * (1 - y), half), half), :] = lc_recv[0:half, :]
    a = a_mine[...].astype(F32) + a_recv[...].astype(F32)
    tot = a[chans : chans + 1, :]
    att = a[0:chans, :] / tot
    att_out[...] = att
    tot_out[...] = tot
    mixed = tn((att * gcol[...]).astype(BF), get(0)[...]).astype(BF)
    res1 = lat[...].astype(F32) + nn(mixed, get(1)[...])
    res1_out[...] = res1
    n2, _ = stats(res1)
    nt2 = (n2 * g1[...]).astype(BF)
    nt2_out[...] = nt2
    hid = nn(nt2, get(2)[...])
    hid1_out[...] = hid
    act = gelu(hid).astype(BF)
    act1_out[...] = act
    res2 = res1 + nn(act, get(3)[...])
    res2_out[...] = res2
    n3, _ = stats(res2)
    nt3 = (n3 * gs[...]).astype(BF)
    nt3_out[...] = nt3
    proj = get(4)
    kv_out[...] = nn(nt3, proj[:, width : 3 * width]).astype(BF)
    q_out[...] = nn(nt3, proj[:, 0:width]).astype(BF)


def second_kernel(pos, q, kv, kv2, res2, lc_mine, lc_recv, so, g2, su, sd,
                  out0, out1, out2, out3, selfr_out, sent3_out, back3_out, nt4_out, act2_out, hg2_out, gain_out, dq_out, dkv_out, dkv2_out, cot,
                  prob, mixed_scr, tots, mixed_out):
    y = pos[3]
    half = lc_mine.shape[0] // 2
    rows, width = res2.shape
    hd = width // HEADS
    hs = 1.0 / math.sqrt(hd)
    cot[pl.ds(pl.multiple_of(half * y, half), half), :] = lc_mine[half : 2 * half, :]
    cot[pl.ds(pl.multiple_of(half * (1 - y), half), half), :] = lc_recv[half : 2 * half, :]
    for h in range(HEADS):
        cols = slice(h * hd, (h + 1) * hd)
        vcols = slice(width + h * hd, width + (h + 1) * hd)
        qh = q[:, cols]
        pa = jnp.exp2(nt(qh, kv[:, cols]) * (hs * LOG2E))
        pb = jnp.exp2(nt(qh, kv2[:, cols]) * (hs * LOG2E))
        tot = jnp.sum(pa, axis=1, keepdims=True) + jnp.sum(pb, axis=1, keepdims=True)
        pa, pb = pa.astype(BF), pb.astype(BF)
        prob[h, :, 0:rows] = pa
        prob[h, :, rows : 2 * rows] = pb
        rt = 1.0 / tot
        tots[h] = rt
        mixed_scr[:, cols] = (nn(pa, kv[:, vcols]) + nn(pb, kv2[:, vcols])) * rt
    selfr = mixed_scr[...].astype(BF)
    selfr_out[...] = selfr
    res3 = res2[...] + nn(selfr, so[...])
    n4, r4 = stats(res3)
    nt4 = (n4 * g2[...]).astype(BF)
    nt4_out[...] = nt4
    hid = nn(nt4, su[...])
    act = gelu(hid).astype(BF)
    act2_out[...] = act
    mixed_out[...] = res3 + nn(act, sd[...])
    each = out0.shape[0]
    for r, out in enumerate((out0, out1, out2, out3)):
        at = half * y + lax.rem(pos[2] + r, 4) * each
        out[...] = mixed_out[pl.ds(pl.multiple_of(at, each), each), :].astype(BF)
    hg = (nt(cot[...], sd[...]) * gelu_grad(hid)).astype(BF)
    hg2_out[...] = hg
    ng = nt(hg, su[...])
    gain_out[...] = jnp.sum(ng * n4, axis=0, keepdims=True)
    back3 = cot[...].astype(F32) + norm_back(ng * g2[...], n4, r4)
    back3_out[...] = back3
    sent3 = back3.astype(BF)
    sent3_out[...] = sent3
    mg_all = nt(sent3, so[...]).astype(BF)
    for h in range(HEADS):
        cols = slice(h * hd, (h + 1) * hd)
        vcols = slice(width + h * hd, width + (h + 1) * hd)
        mg = mg_all[:, cols].astype(F32)
        rt = tots[h]
        ng_h = (mg * rt).astype(BF)
        tg = -jnp.sum(mg * mixed_scr[:, cols], axis=1, keepdims=True) * rt
        qh = q[:, cols]
        dq = None
        for src, dst, at in ((kv, dkv_out, 0), (kv2, dkv2_out, rows)):
            p = prob[h, :, at : at + rows]
            sg = (p.astype(F32) * (nt(ng_h, src[:, vcols]) + tg)).astype(BF)
            d = nn(sg, src[:, cols])
            dq = d if dq is None else dq + d
            dst[:, cols] = (tn(sg, qh) * hs).astype(dst.dtype)
            dst[:, vcols] = tn(p, ng_h).astype(dst.dtype)
        dq_out[:, cols] = (dq * hs).astype(BF)


def third_kernel(pos, dq, dkv, dkv2, back3, res2, res1, hid1, att, tot, gcol, wv, co, g1, fu, fd, gs, si, gain2,
                 pg_out, sent2_out, hg1_out, back1_out, gv_out, ht_give, ht_keep, scr, back1_scr, *, items):
    get = (si, fd, fu, co, wv).__getitem__
    rows, width = back3.shape
    chans = wv.shape[0]
    feat = scr.shape[0]
    base = feat - 16
    pg_out[:, 0:width] = dq[...]
    pg_out[:, width : 3 * width] = (dkv[...] + dkv2[...].astype(F32)).astype(BF)
    ng = nt(pg_out[...], get(0)[...])
    n3, r3 = stats(res2[...])
    gain_self = jnp.sum(ng * n3, axis=0, keepdims=True)
    back2 = back3[...] + norm_back(ng * gs[...], n3, r3)
    sent2 = back2.astype(BF)
    sent2_out[...] = sent2
    hg = (nt(sent2, get(1)[...]) * gelu_grad(hid1[...])).astype(BF)
    hg1_out[...] = hg
    ng = nt(hg, get(2)[...])
    n2, r2 = stats(res1[...])
    gain_first = jnp.sum(ng * n2, axis=0, keepdims=True)
    back1 = back2 + norm_back(ng * g1[...], n2, r2)
    back1_scr[...] = back1
    half = rows // 2
    back1_out[...] = back1_scr[pl.ds(pl.multiple_of(half * pos[3], half), half), :]
    sent1 = back1.astype(BF)
    ag = nt(sent1, get(3)[...]).astype(BF)
    rt = 1.0 / tot[...]
    raw = nt(get(4)[...], ag) * (rt * gcol[...])
    tg = -jnp.sum(att[...] * raw, axis=0, keepdims=True)
    raw = raw - jnp.sum(raw, axis=0, keepdims=True) / chans
    scr[...] = jnp.zeros(scr.shape, F32)
    scr[0:chans, :] = raw
    gv_out[0:base, :] = scr[0:base, :].astype(BF)
    row = lax.broadcasted_iota(jnp.int32, (16, rows), 0) + base
    tg_high = tg.astype(BF).astype(F32)
    high = jnp.where(row == chans, tg_high, scr[base:feat, :])
    high = jnp.where(row == chans + 1, tg - tg_high, high)
    gv_out[base:feat, :] = high.astype(BF)
    scr[0:chans, :] = att[...]
    ht = nn(scr[...].astype(BF), sent1)
    row = lax.broadcasted_iota(jnp.int32, (16, width), 0) + base
    high = ht[base:feat]
    for k, v in enumerate((gain_first, gain_self, gain2[...])):
        v_high = v.astype(BF).astype(F32)
        high = jnp.where(row == chans + 2 * k, v_high, high)
        high = jnp.where(row == chans + 2 * k + 1, v - v_high, high)
    lanes = width // (4 * items)
    for i in range(items):
        for q in range(4):
            k = lax.rem(i - pos[4] + items, items)
            cut = slice(i * 4 * lanes + q * lanes, i * 4 * lanes + (q + 1) * lanes)

            @pl.when((q // 2 == pos[3]) & (q % 2 == pos[1]))
            def _():
                ht_keep[k, 0:base, :] = ht[0:base, cut].astype(BF)
                ht_keep[k, base:feat, :] = high[:, cut].astype(BF)

            @pl.when((q // 2 == pos[3]) & (q % 2 != pos[1]))
            def _():
                ht_give[k, 0:base, :] = ht[0:base, cut].astype(BF)
                ht_give[k, base:feat, :] = high[:, cut].astype(BF)


def last_kernel(pos, b_mine, b_recv, lat, back1, gain, gcol, wq, wk, out, gt_keep, gt_give, scr, *, scale, items):
    chans, width = wk.shape
    feat = scr.shape[0]
    base = feat - 16
    b = (b_mine[...].astype(F32) + b_recv[...].astype(F32)) * scale
    bs = b[0:chans, :]
    rows_grad = tn((bs * gcol[...]).astype(BF), wk[...]).astype(BF)
    ng = nt(rows_grad, wq[...])
    n, r = stats(lat[0 : back1.shape[0], :].astype(F32))
    rounded = (n * gain[...]).astype(BF)
    gain_grad = jnp.sum(ng * n, axis=0, keepdims=True)
    out[...] = (back1[...] + norm_back(ng * gain[...], n, r)).astype(BF).reshape(out.shape)
    scr[...] = jnp.zeros(scr.shape, F32)
    scr[0:chans, :] = bs
    gt = nn(scr[...].astype(BF), rounded)
    row = lax.broadcasted_iota(jnp.int32, (16, width), 0) + base
    high = gt[base:feat]
    g_high = gain_grad.astype(BF).astype(F32)
    high = jnp.where(row == chans, g_high, high)
    high = jnp.where(row == chans + 1, gain_grad - g_high, high)
    lanes = width // (4 * items)
    for i in range(items):
        for q in range(4):
            k = lax.rem(i - pos[4] + items, items)
            yr = (q // 2) ^ pos[3]
            cut = slice(i * 4 * lanes + q * lanes, i * 4 * lanes + (q + 1) * lanes)

            @pl.when(q % 2 == pos[1])
            def _():
                gt_keep[yr, k, 0:base, :] = gt[0:base, cut].astype(BF)
                gt_keep[yr, k, base:feat, :] = high[:, cut].astype(BF)

            @pl.when(q % 2 != pos[1])
            def _():
                gt_give[yr, k, 0:base, :] = gt[0:base, cut].astype(BF)
                gt_give[yr, k, base:feat, :] = high[:, cut].astype(BF)


def columns(pos, width, items):
    lanes = width // (4 * items)
    at = []
    for lr in range(4):
        for k in range(items):
            start = lax.rem(pos[4] + k, items) * 4 * lanes + (pos[0] ^ lr) * lanes
            at.append(pl.multiple_of(start, lanes))
    return at, lanes


def join(full, parts, at, lanes):
    if lanes % 128 == 0:
        for off, part in zip(at, parts):
            full[:, pl.ds(off, lanes)] = part[...].astype(F32)
        return
    r = lax.broadcasted_iota(jnp.int32, (lanes, full.shape[1]), 0)
    c = lax.broadcasted_iota(jnp.int32, (lanes, full.shape[1]), 1)
    full[...] = jnp.zeros(full.shape, F32)
    for off, part in zip(at, parts):
        full[...] = full[...] + nn(part[...], (c == r + off).astype(F32).astype(BF))


def row_sums(prod):
    ones = jnp.ones((8, prod.shape[1]), BF)
    return nt(ones, prod.astype(BF))[0:1]


def value_kernel(pos, *refs, items):
    parts, refs = refs[: 4 * items], refs[4 * items :]
    gcol, wv, co, value_out, cross_out, vsum_out, *gains, full = refs
    feat = full.shape[0]
    parts = [p[feat : 2 * feat, :] for p in parts]
    chans, width = wv.shape
    rows = cross_out.shape[0]
    at, lanes = columns(pos, width, items)
    join(full, parts, at, lanes)
    hb = full[0:chans, :].astype(BF)
    for k in range(3):
        lo = chans + 2 * k
        gains[k][...] = full[lo : lo + 1, :] + full[lo + 1 : lo + 2, :]
    one = own_columns(width, rows, pos[5])
    wsel = (nn(wv[...], one) * gcol[...]).astype(BF)
    cross_out[...] = tn(wsel, hb)
    v = nt(hb, co[...])
    vsum_out[...] = row_sums(v * wv[...].astype(F32))
    value_out[...] = v * gcol[...]


def own_columns(width, rows, index):
    r = lax.broadcasted_iota(jnp.int32, (width, rows), 0)
    c = lax.broadcasted_iota(jnp.int32, (width, rows), 1)
    return (r == c + index * rows).astype(F32).astype(BF)


def key_kernel(pos, *refs, items):
    parts, refs = refs[: 4 * items], refs[4 * items :]
    gcol, wk, wq, vsum, *refs = refs
    key_out, query_out, psum_out, gain_out, full = refs
    feat = full.shape[0]
    parts = [p[0:feat, :] for p in parts]
    chans, width = wk.shape
    rows = query_out.shape[0]
    at, lanes = columns(pos, width, items)
    join(full, parts, at, lanes)
    gb = full[0:chans, :].astype(BF)
    gain_out[...] = full[chans : chans + 1, :] + full[chans + 1 : chans + 2, :]
    one = own_columns(lanes, rows, pos[2])
    sel = (nn(parts[0][0:chans, :], one) * gcol[...]).astype(BF)
    query_out[...] = tn(sel, wk[...])
    k = nn(gb, wq[...])
    psum_out[...] = row_sums(k * wk[...].astype(F32)) + vsum[...]
    key_out[...] = k * gcol[...]


def swap(x, kind, lat):
    if kind == "core":
        perm = [(s, s ^ 1) for s in range(lat)]
    else:
        perm = [(s, s ^ 2) for s in range(lat)]
    return lax.ppermute(x, "lat", perm)


def fetch(x, axis, n, r):
    return lax.ppermute(x, axis, [((d + r) % n, d) for d in range(n)])


def send(x, axis, n, r):
    return lax.ppermute(x, axis, [(d, (d + r) % n) for d in range(n)])


def near_first(n):
    return sorted(range(1, n), key=lambda r: min(r, n - r))


def plane(x, items, lat, y, k, back=False):
    perm = []
    for i in range(items):
        for l in range(lat):
            far = ((i + k) % items) * lat + (l ^ (2 * y))
            near = i * lat + l
            perm.append((far, near) if back else (near, far))
    return lax.ppermute(x, ("item", "lat"), perm)


class AllSum:
    def __init__(self, keep, give, items, pix, lat):
        self.sizes = items, pix, lat
        self.both = keep, swap(give, "core", lat)
        self.part = (lambda y, k: (y, k)) if keep.ndim == 4 else (lambda y, k: (k,))
        ys = 2 if keep.ndim == 4 else 1
        self.spots = [(y, k) for y in range(ys) for k in range(items)]

    def first(self):
        return [(BF, [(v, self.part(*at)) for v in self.both]) for at in self.spots]

    def after_first(self, res):
        items, _, lat = self.sizes
        self.terms = [res[0]] + [
            plane(v, items, lat, *at) for at, v in zip(self.spots[1:], res[1:])
        ]

    def now(self):
        return [(BF, [(v, ALL) for v in self.terms])]

    def all_pix(self, own):
        pix = self.sizes[1]
        self.terms = [own] + [fetch(own, "pix", pix, r) for r in near_first(pix)]

    def pix_pair(self, own, bit):
        pix = self.sizes[1]
        self.terms = [own, lax.ppermute(own, "pix", [(d, d ^ bit) for d in range(pix)])]

    def spread(self, total):
        items, _, lat = self.sizes
        near = [
            total if not (y or k) else plane(total, items, lat, y, k, back=True)
            for y in range(2)
            for k in range(items)
        ]
        far = [swap(v, "core", lat) for v in near]
        self.parts = near[:items] + far[:items] + near[items:] + far[items:]

    def spread_items(self, total):
        items = self.sizes[0]
        self.pieces = [total] + [fetch(total, "item", items, k) for k in range(1, items)]


def join_kernel(pos, *refs):
    *terms, rows, total, out0, out1, out2, out3 = refs
    value = terms[0][...].astype(F32)
    for t in terms[1:]:
        value = value + t[...].astype(F32)
    total[...] = value.astype(BF)
    for r, out in enumerate((out0, out1, out2, out3)):
        out[...] = rows[lax.rem(pos[2] + r, 4)]


def home_kernel(pos, *refs):
    *pieces, out = refs
    for r, p in enumerate(pieces):
        out[lax.rem(pos[2] - r + 4, 4)] = p[...]


def both_kernel(pos, *refs):
    *terms, other, out = refs
    feat = other.shape[0]
    value = terms[0][...].astype(F32)
    for t in terms[1:]:
        value = value + t[...].astype(F32)
    out[0:feat, :] = value.astype(BF)
    out[feat : 2 * feat, :] = other[...]


class Units:
    def __init__(self, mine, give, cols, items, pix, lat):
        self.sizes, self.cols = (items, pix, lat), cols
        self.both = mine, swap(give, "core", lat)

    def over_core(self):
        items = self.sizes[0]
        n = self.both[0].shape[0] // items
        return [(BF, [(v, (slice(k * n, (k + 1) * n),)) for v in self.both]) for k in range(items)]

    def hold(self, res):
        self.held = res

    def copies(self, first=0):
        return [(BF, [(v, ALL)]) for v in self.held[first:]]

    def over_items(self, res):
        items = self.sizes[0]
        self.terms = [self.held[0]] + [send(v, "item", items, k + 1) for k, v in enumerate(res)]

    def halves(self):
        n = self.terms[0].shape[0] // 2
        return [(BF, [(v, (slice(h * n, (h + 1) * n),)) for v in self.terms]) for h in range(2)]

    def over_pix(self, res, bit):
        pix = self.sizes[1]
        got = lax.ppermute(res[1], "pix", [(d, d ^ bit) for d in range(pix)])
        self.terms = [res[0], got]

    def grads(self):
        at, wanted = 0, []
        for c in self.cols:
            wanted.append((F32, [(v, (slice(None), slice(at, at + c))) for v in self.terms]))
            at += c
        return wanted


def make_units(chain, groups, items, pix, lat, deps=()):
    rows, width = groups[0][0][0].shape
    outs, ins, cols = [], [], []
    for pairs in groups:
        cols.append([right.shape[1] for _, right in pairs])
        outs += [((width // 4, sum(cols[-1])), BF)] * 2
        ins += [v for pair in pairs for v in pair]
    res = chain.run(
        lambda *r: matrix_kernel(*r, groups=[len(g) for g in groups], items=items, pix=pix),
        outs,
        ins,
        [pltpu.VMEM((width, rows), F32), pltpu.VMEM((width // 4, rows), F32)],
        deps=deps,
    )
    return [Units(res[2 * g], res[2 * g + 1], c, items, pix, lat) for g, c in enumerate(cols)]


def body(
    latents,
    pixels,
    size_ids,
    cross_gain,
    pixel_gain,
    query_weight,
    key_weight,
    value_weight,
    cross_output,
    first_gain,
    first_up,
    first_down,
    self_gain,
    self_inputs,
    self_output,
    second_gain,
    second_up,
    second_down,
    cotangent,
):
    images, lat_rows, width = latents.shape
    pix_rows, chans = pixels.shape[1:]
    lat, pix, items = lax.axis_size("lat"), lax.axis_size("pix"), lax.axis_size("item")
    assert lat == 4 and pix == 4 and images == pix
    feat = -(-(chans + 4) // 16) * 16
    l, z, it = lax.axis_index("lat"), lax.axis_index("pix"), lax.axis_index("item")
    core, yy = l % 2, l // 2
    block = l * pix + z
    pos = jnp.stack(
        [l, core, z, yy, it, it * (lat * pix) + block, block * pix_rows]
    ).astype(jnp.int32)
    chain = Chain(pos)
    rows = images * lat_rows
    lats = lat * rows
    lanes = width // (4 * items)
    scale = 1.0 / math.sqrt(width)
    row = lambda v: v.reshape(1, -1)
    (gcol,) = chain.run(column_kernel, [((chans, 1), F32)], [row(pixel_gain)])

    piece = ((2 * lat_rows, width), BF)
    shares = chain.run(share_kernel, [piece] * pix, [latents, cotangent])
    shares = [shares[0]] + [send(shares[k], "pix", pix, k) for k in range(1, pix)]
    ptile = min(512, pix_rows // 2)
    steps = pix_rows // ptile // 2
    feats = jnp.transpose(pixels, (2, 0, 1))

    def norm_half(part, before):
        start = part * steps
        (res,) = chain.run(
            lambda *r: pixel_norm_kernel(
                *r, tile=ptile, start=start, total=pix_rows * lat * pix
            ),
            [((images, feat, pix_rows), BF)],
            [size_ids, feats] + before,
            [pltpu.VMEM((chans, images, ptile), F32), pltpu.VMEM((16, ptile), F32)],
            grid=steps,
            in_specs=[SM, pl.BlockSpec((chans, images, ptile), lambda t, pos: (0, 0, t + start))]
            + [ANY] * part,
            out_specs=[pl.BlockSpec((images, feat, ptile), lambda t, pos: (0, 0, t + start))],
            aliases={3: 0} if part else {},
        )
        return res

    normed = norm_half(0, [])
    (qkt,) = chain.run(
        lambda *r: query_kernel(*r, scale=scale),
        [((feat, rows), BF)],
        [latents, row(cross_gain), query_weight, key_weight, gcol],
        [pltpu.VMEM((feat, rows), F32)],
    )
    level = [qkt] + [fetch(qkt, "pix", pix, r) for r in range(1, pix)]
    normed = norm_half(1, [normed])
    (stack,) = chain.run(
        lambda *r: stack_kernel(*r, images=images), [((images * feat, rows), BF)], level
    )
    stack_y = swap(stack, "y", lat)
    query = [stack, swap(stack, "core", lat), stack_y, swap(stack_y, "core", lat)]
    order = [1, 3, 2, 0]

    image_of = lambda r: lambda t, pos: (lax.rem(pos[2] + r, images), 0, 0)
    image_spec = lambda r: pl.BlockSpec((1, feat, pix_rows), image_of(r))
    half = ((feat, lats // 2), BF)
    full = ((feat, lats), BF)
    powered, query_all, part, from_z = {}, {}, {}, []

    def cross(r):
        powered[r], mine, give, query_all[r] = chain.run(
            lambda *a: cross_kernel(*a, at=r * feat),
            [((lats, pix_rows), BF), half, half, full],
            [*query, normed],
            [pltpu.VMEM((lats, feat), BF), pltpu.VMEM((feat, lats), F32)],
            in_specs=[None] * 4 + [image_spec(r)],
            limit=WIDE_LIMIT,
        )
        part[r] = mine, swap(give, "core", lat)

    def halves(*which):
        return [(BF, [(v, ALL) for v in part[r]]) for r in which]

    def pass_on(which, res):
        from_z.extend(send(v, "pix", pix, r) for r, v in zip(which, res))

    cross(order[0])
    cross(order[1])
    pass_on(order[:1], chain.sums(halves(order[0])))
    cross(order[2])
    (lc_mine,) = chain.run(gather_kernel, [((2 * rows, width), BF)], shares)
    lc_recv = swap(lc_mine, "y", lat)
    pass_on(order[1:3], chain.sums(halves(*order[1:3])))
    cross(order[3])
    (a_mine,) = chain.sums([(BF, [(v, ALL) for v in [*part[0], *from_z]])])
    a_recv = swap(a_mine, "y", lat)
    r2 = 2 * rows
    sq = (r2, width)
    att, tot, res1, nt2, hid1, act1, res2, nt3, q, kv = chain.run(
        first_kernel,
        [((chans, r2), F32), ((1, r2), F32), (sq, F32), (sq, BF), (sq, F32), (sq, BF), (sq, F32), (sq, BF), (sq, BF), ((r2, 2 * width), BF)],
        [a_mine, a_recv, lc_mine, lc_recv, gcol, value_weight, cross_output, row(first_gain), first_up, first_down, row(self_gain), self_inputs],
        [pltpu.VMEM(sq, BF)],
        limit=WIDE_LIMIT,
    )
    kv2 = swap(kv, "core", lat)
    image_rows = ((images, lat_rows, width), BF)
    rows_piece = ((lat_rows, width), BF)
    deal = lambda v: [v[0]] + [send(v[r], "pix", pix, r) for r in range(1, pix)]
    *out, selfr, sent3, back3, nt4, act2, hg2, gain2, dq, dkv, dkv_send, cot = chain.run(
        second_kernel,
        [rows_piece] * 4 + [(sq, BF), (sq, BF), (sq, F32), (sq, BF), (sq, BF), (sq, BF), ((1, width), F32), (sq, BF), ((r2, 2 * width), F32), ((r2, 2 * width), BF), (sq, BF)],
        [q, kv, kv2, res2, lc_mine, lc_recv, self_output, row(second_gain), second_up, second_down],
        [
            pltpu.VMEM((HEADS, r2, 2 * r2), BF),
            pltpu.VMEM(sq, F32),
            pltpu.VMEM((HEADS, r2, 1), F32),
            pltpu.VMEM(sq, F32),
        ],
        limit=WIDE_LIMIT,
    )
    dkv2 = swap(dkv_send, "core", lat)
    (units_two,) = make_units(
        chain, [[(nt4, hg2), (act2, cot), (selfr, sent3)]], items, pix, lat
    )
    pg, sent2, hg1, back1, gvt, ht_give, ht_keep = chain.run(
        lambda *r: third_kernel(*r, items=items),
        [((r2, 3 * width), BF), (sq, BF), (sq, BF), ((rows, width), F32), ((feat, r2), BF)]
        + [((items, feat, lanes), BF)] * 2,
        [dq, dkv, dkv2, back3, res2, res1, hid1, att, tot, gcol, value_weight, cross_output, row(first_gain), first_up, first_down, row(self_gain), self_inputs, gain2],
        [pltpu.VMEM((feat, r2), F32), pltpu.VMEM(sq, F32)],
        limit=WIDE_LIMIT,
    )
    gv_at = {r: (fetch(gvt, "pix", pix, r) if r else gvt) for r in order}
    gv_both = {r: (v, swap(v, "core", lat)) for r, v in gv_at.items()}
    ht = AllSum(ht_keep, ht_give, items, pix, lat)
    units_two.hold(chain.sums(units_two.over_core()))
    units_two.over_items(units_two.held[1:])
    (latents_out,) = chain.run(home_kernel, [image_rows], deal(out), work=SMALL)
    (units_rest,) = make_units(
        chain, [[(nt3, pg), (nt2, hg1), (act1, sent2)]], items, pix, lat
    )
    first = ht.first()
    res = chain.sums(first + units_rest.over_core() + [(BF, [(gv_at[1], ALL)])])
    ht.after_first(res[: len(first)])
    units_rest.hold(res[len(first) : -1])
    gv_both[1] = gv_at[1], swap(res[-1], "core", lat)
    res = chain.sums(units_rest.copies(1) + units_two.halves())
    units_rest.over_items(res[: items - 1])
    units_two.hold(res[items - 1 :])

    grad, part, from_z = None, {}, []

    def back(r, deps=()):
        nonlocal grad
        ins = [*gv_both[r], normed, powered[r], query_all[r]]
        grad, mine, give = chain.run(
            lambda *a: pixel_back_kernel(*a, chans=chans),
            [((images, feat, pix_rows), BF), half, half],
            ins + ([] if grad is None else [grad]),
            [
                pltpu.VMEM((feat, lats), BF),
                pltpu.VMEM((lats, feat), BF),
                pltpu.VMEM((feat, lats), BF),
                pltpu.VMEM((feat, lats), F32),
            ],
            in_specs=[None, None, image_spec(r), None, None] + ([] if grad is None else [ANY]),
            out_specs=[image_spec(r), None, None],
            aliases={} if grad is None else {6: 0},
            limit=WIDE_LIMIT,
            deps=deps,
        )
        part[r] = mine, swap(give, "core", lat)

    back(order[0], [gv_at[r] for r in order])
    res = chain.sums(ht.now() + units_two.copies())
    ht.pix_pair(res[0], 1)
    units_two.over_pix(res[1:], 1)
    back(order[1], [v[1] for v in gv_both.values()])
    res = chain.sums(halves(order[0]) + ht.now() + units_two.halves())
    pass_on(order[:1], res[:1])
    ht.pix_pair(res[1], 2)
    units_two.over_pix(res[2:], 2)
    back(order[2])
    res = chain.sums(halves(*order[1:3]) + ht.now() + units_two.grads())
    pass_on(order[1:3], res[:2])
    ht_total, second_up_grad, second_down_grad, self_out_grad = res[2:]
    back(order[3])
    (pixel_grad,) = chain.run(
        interleave_kernel,
        [((chans, images, pix_rows), BF)],
        [grad],
        [pltpu.VMEM((chans, images, ptile), F32)],
        grid=pix_rows // ptile,
        in_specs=[pl.BlockSpec((images, feat, ptile), lambda t, pos: (0, 0, t))],
        out_specs=[pl.BlockSpec((chans, images, ptile), lambda t, pos: (0, 0, t))],
    )

    def y_halves(pos, *refs):
        *terms, mine, give = refs
        for out, y in ((mine, pos[3]), (give, 1 - pos[3])):
            total = None
            for v in terms:
                v = v[:, pl.ds(pl.multiple_of(y * rows, rows), rows)].astype(F32)
                total = v if total is None else total + v
            out[...] = total.astype(out.dtype)

    quarter = (feat, rows)
    b_mine, b_give = chain.run(y_halves, [(quarter, F32), (quarter, BF)], [*part[0], *from_z])
    b_recv = swap(b_give, "y", lat)
    units_rest.over_pix(chain.sums(units_rest.halves()), 1)
    latent_grad, gt_keep, gt_give = chain.run(
        lambda *r: last_kernel(*r, scale=scale, items=items),
        [image_rows] + [((2, items, feat, lanes), BF)] * 2,
        [b_mine, b_recv, lc_mine, back1, row(cross_gain), gcol, query_weight, key_weight],
        [pltpu.VMEM((feat, rows), F32)],
    )
    gt = AllSum(gt_keep, gt_give, items, pix, lat)
    gt.after_first(chain.sums(gt.first()))
    own, *pieces = chain.run(
        join_kernel, [((feat, lanes), BF)] + [rows_piece] * pix, [*gt.terms, latent_grad]
    )
    gt.all_pix(own)
    gt.spread(
        *chain.run(both_kernel, [((2 * feat, lanes), BF)], [*gt.terms, ht_total])
    )
    units_rest.over_pix(chain.sums(units_rest.halves()), 2)
    pieces = deal(pieces)
    own_rows = width // (items * lat * pix)
    results = [((chans, width), F32), ((own_rows, width), F32), ((1, chans), F32)]
    value_grad, cross_out_grad, vsum, gain_first, gain_self, gain_second = chain.run(
        lambda *r: value_kernel(*r, items=items),
        results + [((1, width), F32)] * 3,
        [*gt.parts, gcol, value_weight, cross_output],
        [pltpu.VMEM((feat, width), F32)],
    )
    key_grad, query_grad, psum, cross_gain_grad = chain.run(
        lambda *r: key_kernel(*r, items=items),
        results + [((1, width), F32)],
        [*gt.parts, gcol, key_weight, query_weight, vsum],
        [pltpu.VMEM((feat, width), F32)],
    )
    self_in_grad, first_up_grad, first_down_grad = chain.sums(units_rest.grads())
    (latent_grad,) = chain.run(home_kernel, [image_rows], pieces)
    flat = lambda v: v.reshape(v.shape[1])
    return (
        latents_out,
        latent_grad,
        jnp.transpose(pixel_grad, (1, 2, 0)),
        query_grad,
        cross_out_grad,
        first_up_grad,
        first_down_grad,
        self_in_grad,
        self_out_grad,
        second_up_grad,
        second_down_grad,
        key_grad,
        value_grad,
        flat(cross_gain_grad),
        flat(psum),
        flat(gain_first),
        flat(gain_self),
        flat(gain_second),
    )


def solution(mesh):
    split = P("item", ("lat", "pix"), None)
    in_specs = (split, split, P("item")) + (P(),) * 15 + (split,)
    grads = P(("item", "lat", "pix"), None)
    out_specs = (split, split, split) + (grads,) * 8 + (P(),) * 7
    return jax.shard_map(body, mesh=mesh, in_specs=in_specs, out_specs=out_specs, check_vma=False)
```

```python
import math

import jax
import jax.numpy as jnp
from jax import lax
from jax.experimental import pallas as pl
from jax.experimental.pallas import tpu as pltpu
from jax.sharding import PartitionSpec as P

HEADS = 8
EPS = 1e-05
LOG2E = 1.4426950408889634
LN2 = 0.6931471805599453
BF = jnp.bfloat16
F32 = jnp.float32
VM = pl.BlockSpec(memory_space=pltpu.VMEM)
SM = pl.BlockSpec(memory_space=pltpu.SMEM)
ANY = pl.BlockSpec(memory_space=pl.ANY)
WORK = 5 * 10**9
SMALL = 10**9
LIMIT = 12 * 1024 * 1024
WIDE_LIMIT = 16 * 1024 * 1024


def nn(a, b):
    return lax.dot_general(a, b, (((1,), (0,)), ((), ())), preferred_element_type=F32)


def nt(a, b):
    return lax.dot_general(a, b, (((1,), (1,)), ((), ())), preferred_element_type=F32)


def tn(a, b):
    return lax.dot_general(a, b, (((0,), (0,)), ((), ())), preferred_element_type=F32)


def stats(v):
    c = v - jnp.mean(v, axis=-1, keepdims=True)
    r = lax.rsqrt(jnp.mean(c * c, axis=-1, keepdims=True) + EPS)
    return c * r, r


def norm_back(scaled, n, r):
    return r * (
        scaled
        - jnp.mean(scaled, axis=-1, keepdims=True)
        - n * jnp.mean(scaled * n, axis=-1, keepdims=True)
    )


K0 = math.sqrt(2.0 / math.pi)
K1 = 0.044715


def gelu(v):
    return 0.5 * v * (1.0 + jnp.tanh(K0 * (v + K1 * v * v * v)))


def gelu_grad(v):
    t = jnp.tanh(K0 * (v + K1 * v * v * v))
    return 0.5 * (1.0 + t) + 0.5 * v * (1.0 - t * t) * (K0 * (1.0 + 3.0 * K1 * v * v))


class Chain:
    def __init__(self, pos):
        self.pos = pos
        self.token = None

    def run(self, kernel, outs, ins, scratch=(), grid=None, in_specs=None, out_specs=None,
            deps=(), aliases=None, limit=LIMIT, work=WORK):
        before = [] if self.token is None else [self.token]
        n_ins, n_extra, n_outs = len(ins), len(before) + len(deps), len(outs)

        def body(pos, *refs):
            given = refs[:n_ins]
            results = refs[n_ins + n_extra : n_ins + n_extra + n_outs]
            refs[n_ins + n_extra + n_outs][...] = jnp.zeros((8, 128), F32)
            rest = refs[n_ins + n_extra + n_outs + 1 :]
            kernel(pos, *given, *results, *rest)

        fixed = lambda v: pl.BlockSpec(v.shape, lambda t, pos: (0,) * len(v.shape))
        shapes = [jax.ShapeDtypeStruct(*o) for o in outs]
        small = jax.ShapeDtypeStruct((8, 128), F32)
        where = lambda a: SM if a.dtype == jnp.int32 else fixed(a)
        specs = in_specs or [None] * n_ins
        specs = [s if s is not None else where(a) for s, a in zip(specs, ins)]
        o_specs = out_specs or [None] * n_outs
        o_specs = [s if s is not None else fixed(o) for s, o in zip(o_specs, shapes)]
        res = pl.pallas_call(
            body,
            grid_spec=pltpu.PrefetchScalarGridSpec(
                num_scalar_prefetch=1,
                grid=(grid or 1,),
                in_specs=specs + [fixed(v) for v in before] + [ANY] * len(deps),
                out_specs=tuple(o_specs + [fixed(small)]),
                scratch_shapes=list(scratch),
            ),
            out_shape=tuple(shapes + [small]),
            input_output_aliases=aliases or {},
            compiler_params=pltpu.CompilerParams(
                dimension_semantics=("arbitrary",), vmem_limit_bytes=limit
            ),
            cost_estimate=pl.CostEstimate(flops=work, bytes_accessed=100000, transcendentals=0),
        )(self.pos, *ins, *before, *deps)
        self.token = res[-1]
        return list(res[:-1])

    def sums(self, wanted, deps=()):
        arrays, place = [], {}
        for _, terms in wanted:
            for a, _ in terms:
                if id(a) not in place:
                    place[id(a)] = len(arrays)
                    arrays.append(a)
        outs = []
        for dtype, terms in wanted:
            a, index = terms[0]
            outs.append((jax.eval_shape(lambda v, index=index: v[index], a).shape, dtype))

        def kernel(pos, *refs):
            for n, (dtype, terms) in enumerate(wanted):
                total = None
                for a, index in terms:
                    v = refs[place[id(a)]][index].astype(F32)
                    total = v if total is None else total + v
                refs[len(arrays) + n][...] = total.astype(dtype)

        return self.run(kernel, outs, arrays, deps=deps, work=SMALL)


ALL = (Ellipsis,)


def query_kernel(pos, lat, gain, wq, wk, gcol, out, scr, *, scale):
    chans = wk.shape[0]
    x = lat[...].astype(F32)
    n, _ = stats(x.reshape(out.shape[1], x.shape[-1]))
    rounded = (n * gain[...]).astype(BF)
    query = nn(rounded, wq[...]).astype(BF)
    t = nt(wk[...], query) * gcol[...]
    t = (t - jnp.sum(t, axis=0, keepdims=True) / chans) * (scale * LOG2E)
    scr[...] = jnp.zeros(scr.shape, F32)
    scr[0:chans, :] = t
    out[...] = scr[...].astype(BF)


def stack_kernel(pos, *refs, images):
    *level, out = refs
    z = pos[2]
    feat = out.shape[0] // images
    wide = [v[...].astype(F32) for v in level]
    lat_rows = out.shape[1] // images
    slot = lax.broadcasted_iota(jnp.int32, wide[0].shape, 1) // lat_rows
    for r in range(images):
        im = lax.rem(z + r, images)
        total = None
        for rz in range(images):
            s = lax.rem(z + rz, images)
            v = pltpu.roll(wide[rz], lax.rem(s - im + images, images) * lat_rows, 1)
            total = v if total is None else jnp.where(slot == s, v, total)
        out[r * feat : (r + 1) * feat, :] = total.astype(BF)


def share_kernel(pos, lat, cot, *outs):
    n = len(outs)
    lat_rows = lat.shape[1]
    for r in range(n):
        im = lax.rem(pos[2] + r, n)
        outs[r][0:lat_rows, :] = lat[im]
        outs[r][lat_rows : 2 * lat_rows, :] = cot[im]


def gather_kernel(pos, *refs):
    *pieces, out = refs
    n = len(pieces)
    lat_rows = pieces[0].shape[0] // 2
    for r in range(n):
        src = lax.rem(pos[2] - r + n, n)
        for half in range(2):
            at = pl.multiple_of(half * n * lat_rows + src * lat_rows, lat_rows)
            out[pl.ds(at, lat_rows), :] = pieces[r][half * lat_rows : (half + 1) * lat_rows, :]


def column_kernel(pos, row, out):
    n = row.shape[1]
    same = lax.broadcasted_iota(jnp.int32, (n, n), 0) == lax.broadcasted_iota(jnp.int32, (n, n), 1)
    out[...] = jnp.sum(jnp.where(same, row[...], 0.0), axis=1, keepdims=True)


def pixel_norm_kernel(pos, ids, pix, *refs, tile, start, total):
    out, wide, tail = refs[-3:]
    t = pl.program_id(0) + start
    chans, images = pix.shape[:2]
    feat = out.shape[1]
    base = feat - 16
    wide[...] = pix[...].astype(F32)
    row = lax.broadcasted_iota(jnp.int32, (16, tile), 0) + base
    lane = lax.broadcasted_iota(jnp.int32, (1, tile), 1) + t * tile
    for i in range(images):
        x = wide[:, i, :]
        x = x - jnp.sum(x, axis=0, keepdims=True) / chans
        var = jnp.sum(x * x, axis=0, keepdims=True) / chans
        size = jnp.where(ids[i] == 0, 25, jnp.where(ids[i] == 1, 49, 81))
        count = lax.div(total * size, 81) - pos[6]
        valid = jnp.where(lane < count, 1.0, 0.0)
        inv = lax.rsqrt(var + EPS) * valid
        inv_high = inv.astype(BF).astype(F32)
        x = x * inv
        out[i, 0:base, :] = x[0:base].astype(BF)
        tail[...] = jnp.zeros(tail.shape, F32)
        tail[0 : chans - base, :] = x[base:chans]
        high = tail[...]
        high = jnp.where((row == chans) | (row == chans + 1), valid, high)
        high = jnp.where(row == chans + 2, inv_high, high)
        high = jnp.where(row == chans + 3, inv - inv_high, high)
        out[i, base:feat, :] = high.astype(BF)


def cross_kernel(pos, *refs, at):
    pieces, refs = refs[:4], refs[4:]
    nt_ref, p_out, mine, send, qkt, qk, acc = refs
    t = pl.program_id(0)
    lpos, core = pos[0], pos[1]
    group = pieces[0].shape[1]
    feat = qkt.shape[0]
    row = at

    @pl.when(t == 0)
    def _():
        for rl in range(4):
            at = pl.multiple_of(group * (lpos ^ rl), group)
            qkt[:, pl.ds(at, group)] = pieces[rl][row : row + feat, :]
        qk[...] = jnp.transpose(qkt[...].astype(F32), (1, 0)).astype(BF)

    n = nt_ref[0]
    p = jnp.exp2(nn(qk[...], n)).astype(BF)
    p_out[...] = p
    part = nt(n, p)

    @pl.when(t == 0)
    def _():
        acc[...] = part

    @pl.when(t != 0)
    def _():
        acc[...] = acc[...] + part

    @pl.when(t == pl.num_programs(0) - 1)
    def _():
        split_halves(acc, mine, send, core, group)


def split_halves(acc, mine, send, core, group):
    for y in range(2):
        a = pl.multiple_of(2 * group * y + group * core, group)
        b = pl.multiple_of(2 * group * y + group * (1 - core), group)
        mine[:, group * y : group * (y + 1)] = acc[:, pl.ds(a, group)].astype(BF)
        send[:, group * y : group * (y + 1)] = acc[:, pl.ds(b, group)].astype(BF)


def pixel_back_kernel(pos, *refs, chans):
    gv_mine, gv_other, nt_ref, p_ref, qkt_ref = refs[:5]
    refs = refs[-7:]
    grad, mine, send, gvt, gv, qktb, acc = refs
    t = pl.program_id(0)
    core = pos[1]
    feat, lats = gv.shape[1], gv.shape[0]
    group = lats // 4
    base = feat - 16

    @pl.when(t == 0)
    def _():
        for ref, c in ((gv_mine, core), (gv_other, 1 - core)):
            for y in range(2):
                at = pl.multiple_of(2 * group * y + group * c, group)
                gvt[:, pl.ds(at, group)] = ref[:, group * y : group * (y + 1)]
        gv[...] = jnp.transpose(gvt[...].astype(F32), (1, 0)).astype(BF)
        qktb[...] = (qkt_ref[...].astype(F32) * LN2).astype(BF)

    n = nt_ref[0]
    p = p_ref[...]
    ds = (p.astype(F32) * nn(gv[...], n)).astype(BF)
    part = nt(n, ds)
    dn = nn(qktb[...], ds) + nn(gvt[...], p)
    nf = n.astype(F32)
    low, high = nf[0:base], nf[base:feat]
    row = lax.broadcasted_iota(jnp.int32, high.shape, 0) + base
    inv = jnp.sum(
        jnp.where((row == chans + 2) | (row == chans + 3), high, 0.0), axis=0, keepdims=True
    )
    high = jnp.where(row < chans, high, 0.0)
    m2 = (
        jnp.sum(dn[0:base] * low, axis=0, keepdims=True)
        + jnp.sum(dn[base:feat] * high, axis=0, keepdims=True)
    ) / chans
    grad[0, 0:base, :] = (inv * (dn[0:base] - low * m2)).astype(BF)
    grad[0, base:feat, :] = (inv * (dn[base:feat] - high * m2)).astype(BF)

    @pl.when(t == 0)
    def _():
        acc[...] = part

    @pl.when(t != 0)
    def _():
        acc[...] = acc[...] + part

    @pl.when(t == pl.num_programs(0) - 1)
    def _():
        split_halves(acc, mine, send, core, group)


def interleave_kernel(pos, src, out, wide):
    chans, images = out.shape[:2]
    for i in range(images):
        wide[:, i, :] = src[i, 0:chans, :].astype(F32)
    out[...] = wide[...].astype(BF)


def matrix_kernel(pos, *refs, groups, items, pix):
    z, y, core, it = pos[2], pos[3], pos[1], pos[4]
    scr, sel = refs[-2:]
    n_ins = 2 * sum(groups)
    ins, outs = refs[:n_ins], refs[n_ins:-2]
    width = scr.shape[0]
    part = width // items
    quarter = part // 4
    each = quarter // pix
    at = 0
    for g, units in enumerate(groups):
        at_col = 0
        for u in range(units):
            left, right = ins[2 * at], ins[2 * at + 1]
            at += 1
            cols = right.shape[1]
            scr[...] = jnp.transpose(left[...].astype(F32), (1, 0))
            for cc in range(2):
                for k in range(items):
                    for n, kp in enumerate((0, 2, 1, 3)):
                        off = (
                            lax.rem(it + k, items) * part
                            + (2 * y + (core ^ cc)) * quarter
                            + (z ^ kp) * each
                        )
                        to = k * quarter + n * each
                        sel[to : to + each, :] = scr[pl.ds(pl.multiple_of(off, each), each), :]
                res = nn(sel[...].astype(BF), right[...]).astype(BF)
                outs[2 * g + cc][:, at_col : at_col + cols] = res
            at_col += cols


def first_kernel(pos, a_mine, a_recv, lc_mine, lc_recv, gcol, wv, co, g1, fu, fd, gs, si,
                 att_out, tot_out, res1_out, nt2_out, hid1_out, act1_out, res2_out, nt3_out, q_out, kv_out, lat):
    get = (wv, co, fu, fd, si).__getitem__
    y = pos[3]
    half = lc_mine.shape[0] // 2
    width = lat.shape[1]
    chans = wv.shape[0]
    lat[pl.ds(pl.multiple_of(half * y, half), half), :] = lc_mine[0:half, :]
    lat[pl.ds(pl.multiple_of(half * (1 - y), half), half), :] = lc_recv[0:half, :]
    a = a_mine[...].astype(F32) + a_recv[...].astype(F32)
    tot = a[chans : chans + 1, :]
    att = a[0:chans, :] / tot
    att_out[...] = att
    tot_out[...] = tot
    mixed = tn((att * gcol[...]).astype(BF), get(0)[...]).astype(BF)
    res1 = lat[...].astype(F32) + nn(mixed, get(1)[...])
    res1_out[...] = res1
    n2, _ = stats(res1)
    nt2 = (n2 * g1[...]).astype(BF)
    nt2_out[...] = nt2
    hid = nn(nt2, get(2)[...])
    hid1_out[...] = hid
    act = gelu(hid).astype(BF)
    act1_out[...] = act
    res2 = res1 + nn(act, get(3)[...])
    res2_out[...] = res2
    n3, _ = stats(res2)
    nt3 = (n3 * gs[...]).astype(BF)
    nt3_out[...] = nt3
    proj = get(4)
    kv_out[...] = nn(nt3, proj[:, width : 3 * width]).astype(BF)
    q_out[...] = nn(nt3, proj[:, 0:width]).astype(BF)


def second_kernel(pos, q, kv, kv2, res2, lc_mine, lc_recv, so, g2, su, sd,
                  out0, out1, out2, out3, selfr_out, sent3_out, back3_out, nt4_out, act2_out, hg2_out, gain_out, dq_out, dkv_out, dkv2_out, cot,
                  prob, mixed_scr, tots, mixed_out):
    y = pos[3]
    half = lc_mine.shape[0] // 2
    rows, width = res2.shape
    hd = width // HEADS
    hs = 1.0 / math.sqrt(hd)
    cot[pl.ds(pl.multiple_of(half * y, half), half), :] = lc_mine[half : 2 * half, :]
    cot[pl.ds(pl.multiple_of(half * (1 - y), half), half), :] = lc_recv[half : 2 * half, :]
    for h in range(HEADS):
        cols = slice(h * hd, (h + 1) * hd)
        vcols = slice(width + h * hd, width + (h + 1) * hd)
        qh = q[:, cols]
        pa = jnp.exp2(nt(qh, kv[:, cols]) * (hs * LOG2E))
        pb = jnp.exp2(nt(qh, kv2[:, cols]) * (hs * LOG2E))
        tot = jnp.sum(pa, axis=1, keepdims=True) + jnp.sum(pb, axis=1, keepdims=True)
        pa, pb = pa.astype(BF), pb.astype(BF)
        prob[h, :, 0:rows] = pa
        prob[h, :, rows : 2 * rows] = pb
        rt = 1.0 / tot
        tots[:, h : h + 1] = rt
        mixed_scr[:, cols] = (nn(pa, kv[:, vcols]) + nn(pb, kv2[:, vcols])) * rt
    selfr = mixed_scr[...].astype(BF)
    selfr_out[...] = selfr
    res3 = res2[...] + nn(selfr, so[...])
    n4, r4 = stats(res3)
    nt4 = (n4 * g2[...]).astype(BF)
    nt4_out[...] = nt4
    hid = nn(nt4, su[...])
    act = gelu(hid).astype(BF)
    act2_out[...] = act
    mixed_out[...] = res3 + nn(act, sd[...])
    each = out0.shape[0]
    for r, out in enumerate((out0, out1, out2, out3)):
        at = half * y + lax.rem(pos[2] + r, 4) * each
        out[...] = mixed_out[pl.ds(pl.multiple_of(at, each), each), :].astype(BF)
    hg = (nt(cot[...], sd[...]) * gelu_grad(hid)).astype(BF)
    hg2_out[...] = hg
    ng = nt(hg, su[...])
    gain_out[...] = jnp.sum(ng * n4, axis=0, keepdims=True)
    back3 = cot[...].astype(F32) + norm_back(ng * g2[...], n4, r4)
    back3_out[...] = back3
    sent3 = back3.astype(BF)
    sent3_out[...] = sent3
    mg_all = nt(sent3, so[...]).astype(BF)
    for h in range(HEADS):
        cols = slice(h * hd, (h + 1) * hd)
        vcols = slice(width + h * hd, width + (h + 1) * hd)
        mg = mg_all[:, cols].astype(F32)
        rt = tots[:, h : h + 1]
        ng_h = (mg * rt).astype(BF)
        tg = -jnp.sum(mg * mixed_scr[:, cols], axis=1, keepdims=True) * rt
        qh = q[:, cols]
        dq = None
        for src, dst, at in ((kv, dkv_out, 0), (kv2, dkv2_out, rows)):
            p = prob[h, :, at : at + rows]
            sg = (p.astype(F32) * (nt(ng_h, src[:, vcols]) + tg)).astype(BF)
            d = nn(sg, src[:, cols])
            dq = d if dq is None else dq + d
            dst[:, cols] = (tn(sg, qh) * hs).astype(dst.dtype)
            dst[:, vcols] = tn(p, ng_h).astype(dst.dtype)
        dq_out[:, cols] = (dq * hs).astype(BF)


def third_kernel(pos, dq, dkv, dkv2, back3, res2, res1, hid1, att, tot, gcol, wv, co, g1, fu, fd, gs, si, gain2,
                 pg_out, sent2_out, hg1_out, back1_out, gv_out, ht_give, ht_keep, scr, back1_scr, *, items):
    get = (si, fd, fu, co, wv).__getitem__
    rows, width = back3.shape
    chans = wv.shape[0]
    feat = scr.shape[0]
    base = feat - 16
    pg_out[:, 0:width] = dq[...]
    pg_out[:, width : 3 * width] = (dkv[...].astype(F32) + dkv2[...].astype(F32)).astype(BF)
    ng = nt(pg_out[...], get(0)[...])
    n3, r3 = stats(res2[...])
    gain_self = jnp.sum(ng * n3, axis=0, keepdims=True)
    back2 = back3[...] + norm_back(ng * gs[...], n3, r3)
    sent2 = back2.astype(BF)
    sent2_out[...] = sent2
    hg = (nt(sent2, get(1)[...]) * gelu_grad(hid1[...])).astype(BF)
    hg1_out[...] = hg
    ng = nt(hg, get(2)[...])
    n2, r2 = stats(res1[...])
    gain_first = jnp.sum(ng * n2, axis=0, keepdims=True)
    back1 = back2 + norm_back(ng * g1[...], n2, r2)
    back1_scr[...] = back1
    half = rows // 2
    back1_out[...] = back1_scr[pl.ds(pl.multiple_of(half * pos[3], half), half), :]
    sent1 = back1.astype(BF)
    ag = nt(sent1, get(3)[...]).astype(BF)
    rt = 1.0 / tot[...]
    raw = nt(get(4)[...], ag) * (rt * gcol[...])
    tg = -jnp.sum(att[...] * raw, axis=0, keepdims=True)
    raw = raw - jnp.sum(raw, axis=0, keepdims=True) / chans
    scr[...] = jnp.zeros(scr.shape, F32)
    scr[0:chans, :] = raw
    gv_out[0:base, :] = scr[0:base, :].astype(BF)
    row = lax.broadcasted_iota(jnp.int32, (16, rows), 0) + base
    tg_high = tg.astype(BF).astype(F32)
    high = jnp.where(row == chans, tg_high, scr[base:feat, :])
    high = jnp.where(row == chans + 1, tg - tg_high, high)
    gv_out[base:feat, :] = high.astype(BF)
    scr[0:chans, :] = att[...]
    ht = nn(scr[...].astype(BF), sent1)
    row = lax.broadcasted_iota(jnp.int32, (16, width), 0) + base
    high = ht[base:feat]
    for k, v in enumerate((gain_first, gain_self, gain2[...])):
        v_high = v.astype(BF).astype(F32)
        high = jnp.where(row == chans + 2 * k, v_high, high)
        high = jnp.where(row == chans + 2 * k + 1, v - v_high, high)
    lanes = width // (4 * items)
    for i in range(items):
        for q in range(4):
            k = lax.rem(i - pos[4] + items, items)
            cut = slice(i * 4 * lanes + q * lanes, i * 4 * lanes + (q + 1) * lanes)

            @pl.when((q // 2 == pos[3]) & (q % 2 == pos[1]))
            def _():
                ht_keep[k, 0:base, :] = ht[0:base, cut].astype(BF)
                ht_keep[k, base:feat, :] = high[:, cut].astype(BF)

            @pl.when((q // 2 == pos[3]) & (q % 2 != pos[1]))
            def _():
                ht_give[k, 0:base, :] = ht[0:base, cut].astype(BF)
                ht_give[k, base:feat, :] = high[:, cut].astype(BF)


def last_kernel(pos, b_mine, b_recv, lat, back1, gain, gcol, wq, wk, out, gt_keep, gt_give, scr, *, scale, items):
    chans, width = wk.shape
    feat = scr.shape[0]
    base = feat - 16
    b = (b_mine[...].astype(F32) + b_recv[...].astype(F32)) * scale
    bs = b[0:chans, :]
    rows_grad = tn((bs * gcol[...]).astype(BF), wk[...]).astype(BF)
    ng = nt(rows_grad, wq[...])
    n, r = stats(lat[0 : back1.shape[0], :].astype(F32))
    rounded = (n * gain[...]).astype(BF)
    gain_grad = jnp.sum(ng * n, axis=0, keepdims=True)
    out[...] = (back1[...] + norm_back(ng * gain[...], n, r)).astype(BF).reshape(out.shape)
    scr[...] = jnp.zeros(scr.shape, F32)
    scr[0:chans, :] = bs
    gt = nn(scr[...].astype(BF), rounded)
    row = lax.broadcasted_iota(jnp.int32, (16, width), 0) + base
    high = gt[base:feat]
    g_high = gain_grad.astype(BF).astype(F32)
    high = jnp.where(row == chans, g_high, high)
    high = jnp.where(row == chans + 1, gain_grad - g_high, high)
    lanes = width // (4 * items)
    for i in range(items):
        for q in range(4):
            k = lax.rem(i - pos[4] + items, items)
            yr = (q // 2) ^ pos[3]
            cut = slice(i * 4 * lanes + q * lanes, i * 4 * lanes + (q + 1) * lanes)

            @pl.when(q % 2 == pos[1])
            def _():
                gt_keep[yr, k, 0:base, :] = gt[0:base, cut].astype(BF)
                gt_keep[yr, k, base:feat, :] = high[:, cut].astype(BF)

            @pl.when(q % 2 != pos[1])
            def _():
                gt_give[yr, k, 0:base, :] = gt[0:base, cut].astype(BF)
                gt_give[yr, k, base:feat, :] = high[:, cut].astype(BF)


def columns(pos, width, items):
    lanes = width // (4 * items)
    at = []
    for lr in range(4):
        for k in range(items):
            start = lax.rem(pos[4] + k, items) * 4 * lanes + (pos[0] ^ lr) * lanes
            at.append(pl.multiple_of(start, lanes))
    return at, lanes


def join(full, parts, at, lanes):
    if lanes % 128 == 0:
        for off, part in zip(at, parts):
            full[:, pl.ds(off, lanes)] = part[...].astype(F32)
        return
    r = lax.broadcasted_iota(jnp.int32, (lanes, full.shape[1]), 0)
    c = lax.broadcasted_iota(jnp.int32, (lanes, full.shape[1]), 1)
    full[...] = jnp.zeros(full.shape, F32)
    for off, part in zip(at, parts):
        full[...] = full[...] + nn(part[...], (c == r + off).astype(F32).astype(BF))


def row_sums(prod):
    ones = jnp.ones((8, prod.shape[1]), BF)
    return nt(ones, prod.astype(BF))[0:1]


def value_kernel(pos, *refs, items):
    parts, refs = refs[: 4 * items], refs[4 * items :]
    gcol, wv, co, value_out, cross_out, vsum_out, *gains, full = refs
    feat = full.shape[0]
    parts = [p[feat : 2 * feat, :] for p in parts]
    chans, width = wv.shape
    rows = cross_out.shape[0]
    at, lanes = columns(pos, width, items)
    join(full, parts, at, lanes)
    hb = full[0:chans, :].astype(BF)
    for k in range(3):
        lo = chans + 2 * k
        gains[k][...] = full[lo : lo + 1, :] + full[lo + 1 : lo + 2, :]
    one = own_columns(width, rows, pos[5])
    wsel = (nn(wv[...], one) * gcol[...]).astype(BF)
    cross_out[...] = tn(wsel, hb)
    v = nt(hb, co[...])
    vsum_out[...] = row_sums(v * wv[...].astype(F32))
    value_out[...] = v * gcol[...]


def own_columns(width, rows, index):
    r = lax.broadcasted_iota(jnp.int32, (width, rows), 0)
    c = lax.broadcasted_iota(jnp.int32, (width, rows), 1)
    return (r == c + index * rows).astype(F32).astype(BF)


def key_kernel(pos, *refs, items):
    parts, refs = refs[: 4 * items], refs[4 * items :]
    gcol, wk, wq, vsum, *refs = refs
    key_out, query_out, psum_out, gain_out, full = refs
    feat = full.shape[0]
    parts = [p[0:feat, :] for p in parts]
    chans, width = wk.shape
    rows = query_out.shape[0]
    at, lanes = columns(pos, width, items)
    join(full, parts, at, lanes)
    gb = full[0:chans, :].astype(BF)
    gain_out[...] = full[chans : chans + 1, :] + full[chans + 1 : chans + 2, :]
    one = own_columns(lanes, rows, pos[2])
    sel = (nn(parts[0][0:chans, :], one) * gcol[...]).astype(BF)
    query_out[...] = tn(sel, wk[...])
    k = nn(gb, wq[...])
    psum_out[...] = row_sums(k * wk[...].astype(F32)) + vsum[...]
    key_out[...] = k * gcol[...]


def swap(x, kind, lat):
    if kind == "core":
        perm = [(s, s ^ 1) for s in range(lat)]
    else:
        perm = [(s, s ^ 2) for s in range(lat)]
    return lax.ppermute(x, "lat", perm)


def fetch(x, axis, n, r):
    return lax.ppermute(x, axis, [((d + r) % n, d) for d in range(n)])


def send(x, axis, n, r):
    return lax.ppermute(x, axis, [(d, (d + r) % n) for d in range(n)])


def near_first(n):
    return sorted(range(1, n), key=lambda r: min(r, n - r))


def plane(x, items, lat, y, k, back=False):
    perm = []
    for i in range(items):
        for l in range(lat):
            far = ((i + k) % items) * lat + (l ^ (2 * y))
            near = i * lat + l
            perm.append((far, near) if back else (near, far))
    return lax.ppermute(x, ("item", "lat"), perm)


class AllSum:
    def __init__(self, keep, give, items, pix, lat):
        self.sizes = items, pix, lat
        self.both = keep, swap(give, "core", lat)
        self.part = (lambda y, k: (y, k)) if keep.ndim == 4 else (lambda y, k: (k,))
        ys = 2 if keep.ndim == 4 else 1
        self.spots = [(y, k) for y in range(ys) for k in range(items)]

    def first(self):
        return [(BF, [(v, self.part(*at)) for v in self.both]) for at in self.spots]

    def after_first(self, res):
        items, _, lat = self.sizes
        self.terms = [res[0]] + [
            plane(v, items, lat, *at) for at, v in zip(self.spots[1:], res[1:])
        ]

    def now(self):
        return [(BF, [(v, ALL) for v in self.terms])]

    def all_pix(self, own):
        pix = self.sizes[1]
        self.terms = [own] + [fetch(own, "pix", pix, r) for r in near_first(pix)]

    def pix_pair(self, own, bit):
        pix = self.sizes[1]
        self.terms = [own, lax.ppermute(own, "pix", [(d, d ^ bit) for d in range(pix)])]

    def spread(self, total):
        items, _, lat = self.sizes
        near = [
            total if not (y or k) else plane(total, items, lat, y, k, back=True)
            for y in range(2)
            for k in range(items)
        ]
        far = [swap(v, "core", lat) for v in near]
        self.parts = near[:items] + far[:items] + near[items:] + far[items:]

    def spread_items(self, total):
        items = self.sizes[0]
        self.pieces = [total] + [fetch(total, "item", items, k) for k in range(1, items)]


def join_kernel(pos, *refs):
    *terms, rows, total, out0, out1, out2, out3 = refs
    value = terms[0][...].astype(F32)
    for t in terms[1:]:
        value = value + t[...].astype(F32)
    total[...] = value.astype(BF)
    for r, out in enumerate((out0, out1, out2, out3)):
        out[...] = rows[lax.rem(pos[2] + r, 4)]


def home_kernel(pos, *refs):
    *pieces, out = refs
    for r, p in enumerate(pieces):
        out[lax.rem(pos[2] - r + 4, 4)] = p[...]


def both_kernel(pos, *refs):
    *terms, other, out = refs
    feat = other.shape[0]
    value = terms[0][...].astype(F32)
    for t in terms[1:]:
        value = value + t[...].astype(F32)
    out[0:feat, :] = value.astype(BF)
    out[feat : 2 * feat, :] = other[...]


class Units:
    def __init__(self, mine, give, cols, items, pix, lat):
        self.sizes, self.cols = (items, pix, lat), cols
        self.both = mine, swap(give, "core", lat)

    def over_core(self):
        items = self.sizes[0]
        n = self.both[0].shape[0] // items
        return [(BF, [(v, (slice(k * n, (k + 1) * n),)) for v in self.both]) for k in range(items)]

    def hold(self, res):
        self.held = res

    def copies(self, first=0):
        return [(BF, [(v, ALL)]) for v in self.held[first:]]

    def over_items(self, res):
        items = self.sizes[0]
        self.terms = [self.held[0]] + [send(v, "item", items, k + 1) for k, v in enumerate(res)]

    def halves(self):
        n = self.terms[0].shape[0] // 2
        return [(BF, [(v, (slice(h * n, (h + 1) * n),)) for v in self.terms]) for h in range(2)]

    def over_pix(self, res, bit):
        pix = self.sizes[1]
        got = lax.ppermute(res[1], "pix", [(d, d ^ bit) for d in range(pix)])
        self.terms = [res[0], got]

    def grads(self):
        at, wanted = 0, []
        for c in self.cols:
            wanted.append((F32, [(v, (slice(None), slice(at, at + c))) for v in self.terms]))
            at += c
        return wanted


def make_units(chain, groups, items, pix, lat, deps=()):
    rows, width = groups[0][0][0].shape
    outs, ins, cols = [], [], []
    for pairs in groups:
        cols.append([right.shape[1] for _, right in pairs])
        outs += [((width // 4, sum(cols[-1])), BF)] * 2
        ins += [v for pair in pairs for v in pair]
    res = chain.run(
        lambda *r: matrix_kernel(*r, groups=[len(g) for g in groups], items=items, pix=pix),
        outs,
        ins,
        [pltpu.VMEM((width, rows), F32), pltpu.VMEM((width // 4, rows), F32)],
        deps=deps,
    )
    return [Units(res[2 * g], res[2 * g + 1], c, items, pix, lat) for g, c in enumerate(cols)]


def body(
    latents,
    pixels,
    size_ids,
    cross_gain,
    pixel_gain,
    query_weight,
    key_weight,
    value_weight,
    cross_output,
    first_gain,
    first_up,
    first_down,
    self_gain,
    self_inputs,
    self_output,
    second_gain,
    second_up,
    second_down,
    cotangent,
):
    images, lat_rows, width = latents.shape
    pix_rows, chans = pixels.shape[1:]
    lat, pix, items = lax.axis_size("lat"), lax.axis_size("pix"), lax.axis_size("item")
    assert lat == 4 and pix == 4 and images == pix
    feat = -(-(chans + 4) // 16) * 16
    l, z, it = lax.axis_index("lat"), lax.axis_index("pix"), lax.axis_index("item")
    core, yy = l % 2, l // 2
    block = l * pix + z
    pos = jnp.stack(
        [l, core, z, yy, it, it * (lat * pix) + block, block * pix_rows]
    ).astype(jnp.int32)
    chain = Chain(pos)
    rows = images * lat_rows
    lats = lat * rows
    lanes = width // (4 * items)
    scale = 1.0 / math.sqrt(width)
    row = lambda v: v.reshape(1, -1)
    (gcol,) = chain.run(column_kernel, [((chans, 1), F32)], [row(pixel_gain)])

    piece = ((2 * lat_rows, width), BF)
    shares = chain.run(share_kernel, [piece] * pix, [latents, cotangent])
    shares = [shares[0]] + [send(shares[k], "pix", pix, k) for k in range(1, pix)]
    ptile = min(512, pix_rows // 2)
    steps = pix_rows // ptile // 2
    feats = jnp.transpose(pixels, (2, 0, 1))

    def norm_half(part, before):
        start = part * steps
        (res,) = chain.run(
            lambda *r: pixel_norm_kernel(
                *r, tile=ptile, start=start, total=pix_rows * lat * pix
            ),
            [((images, feat, pix_rows), BF)],
            [size_ids, feats] + before,
            [pltpu.VMEM((chans, images, ptile), F32), pltpu.VMEM((16, ptile), F32)],
            grid=steps,
            in_specs=[SM, pl.BlockSpec((chans, images, ptile), lambda t, pos: (0, 0, t + start))]
            + [ANY] * part,
            out_specs=[pl.BlockSpec((images, feat, ptile), lambda t, pos: (0, 0, t + start))],
            aliases={3: 0} if part else {},
        )
        return res

    normed = norm_half(0, [])
    (qkt,) = chain.run(
        lambda *r: query_kernel(*r, scale=scale),
        [((feat, rows), BF)],
        [latents, row(cross_gain), query_weight, key_weight, gcol],
        [pltpu.VMEM((feat, rows), F32)],
    )
    level = [qkt] + [fetch(qkt, "pix", pix, r) for r in range(1, pix)]
    normed = norm_half(1, [normed])
    (stack,) = chain.run(
        lambda *r: stack_kernel(*r, images=images), [((images * feat, rows), BF)], level
    )
    stack_y = swap(stack, "y", lat)
    query = [stack, swap(stack, "core", lat), stack_y, swap(stack_y, "core", lat)]
    order = [1, 3, 2, 0]

    image_of = lambda r: lambda t, pos: (lax.rem(pos[2] + r, images), 0, 0)
    image_spec = lambda r: pl.BlockSpec((1, feat, pix_rows), image_of(r))
    half = ((feat, lats // 2), BF)
    full = ((feat, lats), BF)
    powered, query_all, part, from_z = {}, {}, {}, []

    def cross(r):
        powered[r], mine, give, query_all[r] = chain.run(
            lambda *a: cross_kernel(*a, at=r * feat),
            [((lats, pix_rows), BF), half, half, full],
            [*query, normed],
            [pltpu.VMEM((lats, feat), BF), pltpu.VMEM((feat, lats), F32)],
            in_specs=[None] * 4 + [image_spec(r)],
            limit=WIDE_LIMIT,
        )
        part[r] = mine, swap(give, "core", lat)

    def halves(*which):
        return [(BF, [(v, ALL) for v in part[r]]) for r in which]

    def pass_on(which, res):
        from_z.extend(send(v, "pix", pix, r) for r, v in zip(which, res))

    cross(order[0])
    cross(order[1])
    pass_on(order[:1], chain.sums(halves(order[0])))
    cross(order[2])
    (lc_mine,) = chain.run(gather_kernel, [((2 * rows, width), BF)], shares)
    lc_recv = swap(lc_mine, "y", lat)
    pass_on(order[1:3], chain.sums(halves(*order[1:3])))
    cross(order[3])
    (a_mine,) = chain.sums([(BF, [(v, ALL) for v in [*part[0], *from_z]])])
    a_recv = swap(a_mine, "y", lat)
    r2 = 2 * rows
    sq = (r2, width)
    att, tot, res1, nt2, hid1, act1, res2, nt3, q, kv = chain.run(
        first_kernel,
        [((chans, r2), F32), ((1, r2), F32), (sq, F32), (sq, BF), (sq, F32), (sq, BF), (sq, F32), (sq, BF), (sq, BF), ((r2, 2 * width), BF)],
        [a_mine, a_recv, lc_mine, lc_recv, gcol, value_weight, cross_output, row(first_gain), first_up, first_down, row(self_gain), self_inputs],
        [pltpu.VMEM(sq, BF)],
        limit=WIDE_LIMIT,
    )
    kv2 = swap(kv, "core", lat)
    image_rows = ((images, lat_rows, width), BF)
    rows_piece = ((lat_rows, width), BF)
    deal = lambda v: [v[0]] + [send(v[r], "pix", pix, r) for r in range(1, pix)]
    *out, selfr, sent3, back3, nt4, act2, hg2, gain2, dq, dkv, dkv_send, cot = chain.run(
        second_kernel,
        [rows_piece] * 4 + [(sq, BF), (sq, BF), (sq, F32), (sq, BF), (sq, BF), (sq, BF), ((1, width), F32), (sq, BF), ((r2, 2 * width), BF), ((r2, 2 * width), BF), (sq, BF)],
        [q, kv, kv2, res2, lc_mine, lc_recv, self_output, row(second_gain), second_up, second_down],
        [
            pltpu.VMEM((HEADS, r2, 2 * r2), BF),
            pltpu.VMEM(sq, F32),
            pltpu.VMEM((r2, 128), F32),
            pltpu.VMEM(sq, F32),
        ],
        limit=WIDE_LIMIT,
    )
    dkv2 = swap(dkv_send, "core", lat)
    (units_two,) = make_units(
        chain, [[(nt4, hg2), (act2, cot), (selfr, sent3)]], items, pix, lat
    )
    pg, sent2, hg1, back1, gvt, ht_give, ht_keep = chain.run(
        lambda *r: third_kernel(*r, items=items),
        [((r2, 3 * width), BF), (sq, BF), (sq, BF), ((rows, width), F32), ((feat, r2), BF)]
        + [((items, feat, lanes), BF)] * 2,
        [dq, dkv, dkv2, back3, res2, res1, hid1, att, tot, gcol, value_weight, cross_output, row(first_gain), first_up, first_down, row(self_gain), self_inputs, gain2],
        [pltpu.VMEM((feat, r2), F32), pltpu.VMEM(sq, F32)],
        limit=WIDE_LIMIT,
    )
    gv_at = {r: (fetch(gvt, "pix", pix, r) if r else gvt) for r in order}
    gv_both = {r: (v, swap(v, "core", lat)) for r, v in gv_at.items()}
    ht = AllSum(ht_keep, ht_give, items, pix, lat)
    units_two.hold(chain.sums(units_two.over_core()))
    units_two.over_items(units_two.held[1:])
    (latents_out,) = chain.run(home_kernel, [image_rows], deal(out), work=SMALL)
    (units_rest,) = make_units(
        chain, [[(nt3, pg), (nt2, hg1), (act1, sent2)]], items, pix, lat
    )
    first = ht.first()
    res = chain.sums(first + units_rest.over_core() + [(BF, [(gv_at[1], ALL)])])
    ht.after_first(res[: len(first)])
    units_rest.hold(res[len(first) : -1])
    gv_both[1] = gv_at[1], swap(res[-1], "core", lat)
    res = chain.sums(units_rest.copies(1) + units_two.halves())
    units_rest.over_items(res[: items - 1])
    units_two.over_pix(res[items - 1 :], 1)

    grad, part, from_z = None, {}, []

    def back(r, deps=()):
        nonlocal grad
        ins = [*gv_both[r], normed, powered[r], query_all[r]]
        grad, mine, give = chain.run(
            lambda *a: pixel_back_kernel(*a, chans=chans),
            [((images, feat, pix_rows), BF), half, half],
            ins + ([] if grad is None else [grad]),
            [
                pltpu.VMEM((feat, lats), BF),
                pltpu.VMEM((lats, feat), BF),
                pltpu.VMEM((feat, lats), BF),
                pltpu.VMEM((feat, lats), F32),
            ],
            in_specs=[None, None, image_spec(r), None, None] + ([] if grad is None else [ANY]),
            out_specs=[image_spec(r), None, None],
            aliases={} if grad is None else {6: 0},
            limit=WIDE_LIMIT,
            deps=deps,
        )
        part[r] = mine, swap(give, "core", lat)

    back(order[0], [gv_at[r] for r in order])
    ht.pix_pair(*chain.sums(ht.now()), 1)
    back(order[1], [v[1] for v in gv_both.values()])
    res = chain.sums(halves(order[0]) + ht.now() + units_two.halves())
    pass_on(order[:1], res[:1])
    ht.pix_pair(res[1], 2)
    units_two.over_pix(res[2:], 2)
    back(order[2])
    pass_on(order[1:3], chain.sums(halves(*order[1:3])))
    back(order[3])
    (pixel_grad,) = chain.run(
        interleave_kernel,
        [((chans, images, pix_rows), BF)],
        [grad],
        [pltpu.VMEM((chans, images, ptile), F32)],
        grid=pix_rows // ptile,
        in_specs=[pl.BlockSpec((images, feat, ptile), lambda t, pos: (0, 0, t))],
        out_specs=[pl.BlockSpec((chans, images, ptile), lambda t, pos: (0, 0, t))],
    )

    (ht_total,) = chain.sums(ht.now())

    def y_halves(pos, *refs):
        *terms, mine, give = refs
        for out, y in ((mine, pos[3]), (give, 1 - pos[3])):
            total = None
            for v in terms:
                v = v[:, pl.ds(pl.multiple_of(y * rows, rows), rows)].astype(F32)
                total = v if total is None else total + v
            out[...] = total.astype(out.dtype)

    quarter = (feat, rows)
    b_mine, b_give = chain.run(y_halves, [(quarter, F32), (quarter, BF)], [*part[0], *from_z])
    b_recv = swap(b_give, "y", lat)
    latent_grad, gt_keep, gt_give = chain.run(
        lambda *r: last_kernel(*r, scale=scale, items=items),
        [image_rows] + [((2, items, feat, lanes), BF)] * 2,
        [b_mine, b_recv, lc_mine, back1, row(cross_gain), gcol, query_weight, key_weight],
        [pltpu.VMEM((feat, rows), F32)],
    )
    gt = AllSum(gt_keep, gt_give, items, pix, lat)
    res = chain.sums(units_rest.halves() + units_two.grads())
    units_rest.over_pix(res[:2], 1)
    second_up_grad, second_down_grad, self_out_grad = res[2:]
    gt.after_first(chain.sums(gt.first()))
    own, *pieces = chain.run(
        join_kernel, [((feat, lanes), BF)] + [rows_piece] * pix, [*gt.terms, latent_grad]
    )
    gt.all_pix(own)
    gt.spread(
        *chain.run(both_kernel, [((2 * feat, lanes), BF)], [*gt.terms, ht_total])
    )
    own_rows = width // (items * lat * pix)
    results = [((chans, width), F32), ((own_rows, width), F32), ((1, chans), F32)]
    value_grad, cross_out_grad, vsum, gain_first, gain_self, gain_second = chain.run(
        lambda *r: value_kernel(*r, items=items),
        results + [((1, width), F32)] * 3,
        [*gt.parts, gcol, value_weight, cross_output],
        [pltpu.VMEM((feat, width), F32)],
    )
    units_rest.over_pix(chain.sums(units_rest.halves()), 2)
    key_grad, query_grad, psum, cross_gain_grad = chain.run(
        lambda *r: key_kernel(*r, items=items),
        results + [((1, width), F32)],
        [*gt.parts, gcol, key_weight, query_weight, vsum],
        [pltpu.VMEM((feat, width), F32)],
    )
    (latent_grad,) = chain.run(home_kernel, [image_rows], deal(pieces))
    self_in_grad, first_up_grad, first_down_grad = chain.sums(units_rest.grads())
    flat = lambda v: v.reshape(v.shape[1])
    return (
        latents_out,
        latent_grad,
        jnp.transpose(pixel_grad, (1, 2, 0)),
        query_grad,
        cross_out_grad,
        first_up_grad,
        first_down_grad,
        self_in_grad,
        self_out_grad,
        second_up_grad,
        second_down_grad,
        key_grad,
        value_grad,
        flat(cross_gain_grad),
        flat(psum),
        flat(gain_first),
        flat(gain_self),
        flat(gain_second),
    )


def solution(mesh):
    split = P("item", ("lat", "pix"), None)
    in_specs = (split, split, P("item")) + (P(),) * 15 + (split,)
    grads = P(("item", "lat", "pix"), None)
    out_specs = (split, split, split) + (grads,) * 8 + (P(),) * 7
    return jax.shard_map(body, mesh=mesh, in_specs=in_specs, out_specs=out_specs, check_vma=False)
```

```python
import math

import jax
import jax.numpy as jnp
from jax import lax
from jax.experimental import pallas as pl
from jax.experimental.pallas import tpu as pltpu
from jax.sharding import PartitionSpec as P

HEADS = 8
EPS = 1e-05
LOG2E = 1.4426950408889634
LN2 = 0.6931471805599453
BF = jnp.bfloat16
F32 = jnp.float32
VM = pl.BlockSpec(memory_space=pltpu.VMEM)
SM = pl.BlockSpec(memory_space=pltpu.SMEM)
ANY = pl.BlockSpec(memory_space=pl.ANY)
WORK = 5 * 10**9
SMALL = 10**9
LIMIT = 12 * 1024 * 1024
WIDE_LIMIT = 16 * 1024 * 1024


def nn(a, b):
    return lax.dot_general(a, b, (((1,), (0,)), ((), ())), preferred_element_type=F32)


def nt(a, b):
    return lax.dot_general(a, b, (((1,), (1,)), ((), ())), preferred_element_type=F32)


def tn(a, b):
    return lax.dot_general(a, b, (((0,), (0,)), ((), ())), preferred_element_type=F32)


def stats(v):
    c = v - jnp.mean(v, axis=-1, keepdims=True)
    r = lax.rsqrt(jnp.mean(c * c, axis=-1, keepdims=True) + EPS)
    return c * r, r


def norm_back(scaled, n, r):
    return r * (
        scaled
        - jnp.mean(scaled, axis=-1, keepdims=True)
        - n * jnp.mean(scaled * n, axis=-1, keepdims=True)
    )


K0 = math.sqrt(2.0 / math.pi)
K1 = 0.044715


def gelu(v):
    return 0.5 * v * (1.0 + jnp.tanh(K0 * (v + K1 * v * v * v)))


def gelu_grad(v):
    t = jnp.tanh(K0 * (v + K1 * v * v * v))
    return 0.5 * (1.0 + t) + 0.5 * v * (1.0 - t * t) * (K0 * (1.0 + 3.0 * K1 * v * v))


class Chain:
    def __init__(self, pos):
        self.pos = pos
        self.token = None

    def run(self, kernel, outs, ins, scratch=(), grid=None, in_specs=None, out_specs=None,
            deps=(), aliases=None, limit=LIMIT, work=WORK):
        before = [] if self.token is None else [self.token]
        n_ins, n_extra, n_outs = len(ins), len(before) + len(deps), len(outs)

        def body(pos, *refs):
            given = refs[:n_ins]
            results = refs[n_ins + n_extra : n_ins + n_extra + n_outs]
            refs[n_ins + n_extra + n_outs][...] = jnp.zeros((8, 128), F32)
            rest = refs[n_ins + n_extra + n_outs + 1 :]
            kernel(pos, *given, *results, *rest)

        fixed = lambda v: pl.BlockSpec(v.shape, lambda t, pos: (0,) * len(v.shape))
        shapes = [jax.ShapeDtypeStruct(*o) for o in outs]
        small = jax.ShapeDtypeStruct((8, 128), F32)
        where = lambda a: SM if a.dtype == jnp.int32 else fixed(a)
        specs = in_specs or [None] * n_ins
        specs = [s if s is not None else where(a) for s, a in zip(specs, ins)]
        o_specs = out_specs or [None] * n_outs
        o_specs = [s if s is not None else fixed(o) for s, o in zip(o_specs, shapes)]
        res = pl.pallas_call(
            body,
            grid_spec=pltpu.PrefetchScalarGridSpec(
                num_scalar_prefetch=1,
                grid=(grid or 1,),
                in_specs=specs + [fixed(v) for v in before] + [ANY] * len(deps),
                out_specs=tuple(o_specs + [fixed(small)]),
                scratch_shapes=list(scratch),
            ),
            out_shape=tuple(shapes + [small]),
            input_output_aliases=aliases or {},
            compiler_params=pltpu.CompilerParams(
                dimension_semantics=("arbitrary",), vmem_limit_bytes=limit
            ),
            cost_estimate=pl.CostEstimate(flops=work, bytes_accessed=100000, transcendentals=0),
        )(self.pos, *ins, *before, *deps)
        self.token = res[-1]
        return list(res[:-1])

    def sums(self, wanted, deps=()):
        arrays, place = [], {}
        for _, terms in wanted:
            for a, _ in terms:
                if id(a) not in place:
                    place[id(a)] = len(arrays)
                    arrays.append(a)
        outs = []
        for dtype, terms in wanted:
            a, index = terms[0]
            outs.append((jax.eval_shape(lambda v, index=index: v[index], a).shape, dtype))

        def kernel(pos, *refs):
            for n, (dtype, terms) in enumerate(wanted):
                total = None
                for a, index in terms:
                    v = refs[place[id(a)]][index].astype(F32)
                    total = v if total is None else total + v
                refs[len(arrays) + n][...] = total.astype(dtype)

        return self.run(kernel, outs, arrays, deps=deps, work=SMALL)


ALL = (Ellipsis,)


def query_kernel(pos, lat, gain, wq, wk, gcol, out, scr, *, scale):
    chans = wk.shape[0]
    x = lat[...].astype(F32)
    n, _ = stats(x.reshape(out.shape[1], x.shape[-1]))
    rounded = (n * gain[...]).astype(BF)
    query = nn(rounded, wq[...]).astype(BF)
    t = nt(wk[...], query) * gcol[...]
    t = (t - jnp.sum(t, axis=0, keepdims=True) / chans) * (scale * LOG2E)
    scr[...] = jnp.zeros(scr.shape, F32)
    scr[0:chans, :] = t
    out[...] = scr[...].astype(BF)


def stack_kernel(pos, *refs, images):
    *level, out = refs
    z = pos[2]
    feat = out.shape[0] // images
    wide = [v[...].astype(F32) for v in level]
    lat_rows = out.shape[1] // images
    slot = lax.broadcasted_iota(jnp.int32, wide[0].shape, 1) // lat_rows
    for r in range(images):
        im = lax.rem(z + r, images)
        total = None
        for rz in range(images):
            s = lax.rem(z + rz, images)
            v = pltpu.roll(wide[rz], lax.rem(s - im + images, images) * lat_rows, 1)
            total = v if total is None else jnp.where(slot == s, v, total)
        out[r * feat : (r + 1) * feat, :] = total.astype(BF)


def share_kernel(pos, lat, cot, *outs):
    n = len(outs)
    lat_rows = lat.shape[1]
    for r in range(n):
        im = lax.rem(pos[2] + r, n)
        outs[r][0:lat_rows, :] = lat[im]
        outs[r][lat_rows : 2 * lat_rows, :] = cot[im]


def gather_kernel(pos, *refs):
    *pieces, out = refs
    n = len(pieces)
    lat_rows = pieces[0].shape[0] // 2
    for r in range(n):
        src = lax.rem(pos[2] - r + n, n)
        for half in range(2):
            at = pl.multiple_of(half * n * lat_rows + src * lat_rows, lat_rows)
            out[pl.ds(at, lat_rows), :] = pieces[r][half * lat_rows : (half + 1) * lat_rows, :]


def column_kernel(pos, row, out):
    n = row.shape[1]
    same = lax.broadcasted_iota(jnp.int32, (n, n), 0) == lax.broadcasted_iota(jnp.int32, (n, n), 1)
    out[...] = jnp.sum(jnp.where(same, row[...], 0.0), axis=1, keepdims=True)


def pixel_norm_kernel(pos, ids, pix, *refs, tile, start, total):
    out, wide, tail = refs[-3:]
    t = pl.program_id(0) + start
    chans, images = pix.shape[:2]
    feat = out.shape[1]
    base = feat - 16
    wide[...] = pix[...].astype(F32)
    row = lax.broadcasted_iota(jnp.int32, (16, tile), 0) + base
    lane = lax.broadcasted_iota(jnp.int32, (1, tile), 1) + t * tile
    for i in range(images):
        x = wide[:, i, :]
        x = x - jnp.sum(x, axis=0, keepdims=True) / chans
        var = jnp.sum(x * x, axis=0, keepdims=True) / chans
        size = jnp.where(ids[i] == 0, 25, jnp.where(ids[i] == 1, 49, 81))
        count = lax.div(total * size, 81) - pos[6]
        valid = jnp.where(lane < count, 1.0, 0.0)
        inv = lax.rsqrt(var + EPS) * valid
        inv_high = inv.astype(BF).astype(F32)
        x = x * inv
        out[i, 0:base, :] = x[0:base].astype(BF)
        tail[...] = jnp.zeros(tail.shape, F32)
        tail[0 : chans - base, :] = x[base:chans]
        high = tail[...]
        high = jnp.where((row == chans) | (row == chans + 1), valid, high)
        high = jnp.where(row == chans + 2, inv_high, high)
        high = jnp.where(row == chans + 3, inv - inv_high, high)
        out[i, base:feat, :] = high.astype(BF)


def cross_kernel(pos, *refs, at):
    pieces, refs = refs[:4], refs[4:]
    nt_ref, p_out, mine, send, qkt, qk, acc = refs
    t = pl.program_id(0)
    lpos, core = pos[0], pos[1]
    group = pieces[0].shape[1]
    feat = qkt.shape[0]
    row = at

    @pl.when(t == 0)
    def _():
        for rl in range(4):
            at = pl.multiple_of(group * (lpos ^ rl), group)
            qkt[:, pl.ds(at, group)] = pieces[rl][row : row + feat, :]
        qk[...] = jnp.transpose(qkt[...].astype(F32), (1, 0)).astype(BF)

    n = nt_ref[0]
    p = jnp.exp2(nn(qk[...], n)).astype(BF)
    p_out[...] = p
    part = nt(n, p)

    @pl.when(t == 0)
    def _():
        acc[...] = part

    @pl.when(t != 0)
    def _():
        acc[...] = acc[...] + part

    @pl.when(t == pl.num_programs(0) - 1)
    def _():
        split_halves(acc, mine, send, core, group)


def split_halves(acc, mine, send, core, group):
    for y in range(2):
        a = pl.multiple_of(2 * group * y + group * core, group)
        b = pl.multiple_of(2 * group * y + group * (1 - core), group)
        mine[:, group * y : group * (y + 1)] = acc[:, pl.ds(a, group)].astype(BF)
        send[:, group * y : group * (y + 1)] = acc[:, pl.ds(b, group)].astype(BF)


def pixel_back_kernel(pos, *refs, chans):
    gv_mine, gv_other, nt_ref, p_ref, qkt_ref = refs[:5]
    refs = refs[-7:]
    grad, mine, send, gvt, gv, qktb, acc = refs
    t = pl.program_id(0)
    core = pos[1]
    feat, lats = gv.shape[1], gv.shape[0]
    group = lats // 4
    base = feat - 16

    @pl.when(t == 0)
    def _():
        for ref, c in ((gv_mine, core), (gv_other, 1 - core)):
            for y in range(2):
                at = pl.multiple_of(2 * group * y + group * c, group)
                gvt[:, pl.ds(at, group)] = ref[:, group * y : group * (y + 1)]
        gv[...] = jnp.transpose(gvt[...].astype(F32), (1, 0)).astype(BF)
        qktb[...] = (qkt_ref[...].astype(F32) * LN2).astype(BF)

    n = nt_ref[0]
    p = p_ref[...]
    ds = (p.astype(F32) * nn(gv[...], n)).astype(BF)
    part = nt(n, ds)
    dn = nn(qktb[...], ds) + nn(gvt[...], p)
    nf = n.astype(F32)
    low, high = nf[0:base], nf[base:feat]
    row = lax.broadcasted_iota(jnp.int32, high.shape, 0) + base
    inv = jnp.sum(
        jnp.where((row == chans + 2) | (row == chans + 3), high, 0.0), axis=0, keepdims=True
    )
    high = jnp.where(row < chans, high, 0.0)
    m2 = (
        jnp.sum(dn[0:base] * low, axis=0, keepdims=True)
        + jnp.sum(dn[base:feat] * high, axis=0, keepdims=True)
    ) / chans
    grad[0, 0:base, :] = (inv * (dn[0:base] - low * m2)).astype(BF)
    grad[0, base:feat, :] = (inv * (dn[base:feat] - high * m2)).astype(BF)

    @pl.when(t == 0)
    def _():
        acc[...] = part

    @pl.when(t != 0)
    def _():
        acc[...] = acc[...] + part

    @pl.when(t == pl.num_programs(0) - 1)
    def _():
        split_halves(acc, mine, send, core, group)


def interleave_kernel(pos, src, out, wide):
    chans, images = out.shape[:2]
    for i in range(images):
        wide[:, i, :] = src[i, 0:chans, :].astype(F32)
    out[...] = wide[...].astype(BF)


def matrix_kernel(pos, *refs, groups, items, pix):
    z, y, core, it = pos[2], pos[3], pos[1], pos[4]
    scr, sel = refs[-2:]
    n_ins = 2 * sum(groups)
    ins, outs = refs[:n_ins], refs[n_ins:-2]
    width = scr.shape[0]
    part = width // items
    quarter = part // 4
    each = quarter // pix
    at = 0
    for g, units in enumerate(groups):
        at_col = 0
        for u in range(units):
            left, right = ins[2 * at], ins[2 * at + 1]
            at += 1
            cols = right.shape[1]
            scr[...] = jnp.transpose(left[...].astype(F32), (1, 0))
            for cc in range(2):
                for k in range(items):
                    for n, kp in enumerate((0, 2, 1, 3)):
                        off = (
                            lax.rem(it + k, items) * part
                            + (2 * y + (core ^ cc)) * quarter
                            + (z ^ kp) * each
                        )
                        to = k * quarter + n * each
                        sel[to : to + each, :] = scr[pl.ds(pl.multiple_of(off, each), each), :]
                res = nn(sel[...].astype(BF), right[...]).astype(BF)
                outs[2 * g + cc][:, at_col : at_col + cols] = res
            at_col += cols


def first_kernel(pos, a_mine, a_recv, lc_mine, lc_recv, gcol, wv, co, g1, fu, fd, gs, si,
                 att_out, tot_out, res1_out, nt2_out, hid1_out, act1_out, res2_out, nt3_out, q_out, kv_out, lat):
    get = (wv, co, fu, fd, si).__getitem__
    y = pos[3]
    half = lc_mine.shape[0] // 2
    width = lat.shape[1]
    chans = wv.shape[0]
    lat[pl.ds(pl.multiple_of(half * y, half), half), :] = lc_mine[0:half, :]
    lat[pl.ds(pl.multiple_of(half * (1 - y), half), half), :] = lc_recv[0:half, :]
    a = a_mine[...].astype(F32) + a_recv[...].astype(F32)
    tot = a[chans : chans + 1, :]
    att = a[0:chans, :] / tot
    att_out[...] = att
    tot_out[...] = tot
    mixed = tn((att * gcol[...]).astype(BF), get(0)[...]).astype(BF)
    res1 = lat[...].astype(F32) + nn(mixed, get(1)[...])
    res1_out[...] = res1
    n2, _ = stats(res1)
    nt2 = (n2 * g1[...]).astype(BF)
    nt2_out[...] = nt2
    hid = nn(nt2, get(2)[...])
    hid1_out[...] = hid
    act = gelu(hid).astype(BF)
    act1_out[...] = act
    res2 = res1 + nn(act, get(3)[...])
    res2_out[...] = res2
    n3, _ = stats(res2)
    nt3 = (n3 * gs[...]).astype(BF)
    nt3_out[...] = nt3
    proj = get(4)
    kv_out[...] = nn(nt3, proj[:, width : 3 * width]).astype(BF)
    q_out[...] = nn(nt3, proj[:, 0:width]).astype(BF)


def second_kernel(pos, q, kv, kv2, res2, lc_mine, lc_recv, so, g2, su, sd,
                  out0, out1, out2, out3, selfr_out, sent3_out, back3_out, nt4_out, act2_out, hg2_out, gain_out, dq_out, dkv_out, dkv2_out, cot,
                  prob, mixed_scr, tots, mixed_out):
    y = pos[3]
    half = lc_mine.shape[0] // 2
    rows, width = res2.shape
    hd = width // HEADS
    hs = 1.0 / math.sqrt(hd)
    cot[pl.ds(pl.multiple_of(half * y, half), half), :] = lc_mine[half : 2 * half, :]
    cot[pl.ds(pl.multiple_of(half * (1 - y), half), half), :] = lc_recv[half : 2 * half, :]
    for h in range(HEADS):
        cols = slice(h * hd, (h + 1) * hd)
        vcols = slice(width + h * hd, width + (h + 1) * hd)
        qh = q[:, cols]
        pa = jnp.exp2(nt(qh, kv[:, cols]) * (hs * LOG2E))
        pb = jnp.exp2(nt(qh, kv2[:, cols]) * (hs * LOG2E))
        tot = jnp.sum(pa, axis=1, keepdims=True) + jnp.sum(pb, axis=1, keepdims=True)
        pa, pb = pa.astype(BF), pb.astype(BF)
        prob[h, :, 0:rows] = pa
        prob[h, :, rows : 2 * rows] = pb
        rt = 1.0 / tot
        tots[:, h : h + 1] = rt
        mixed_scr[:, cols] = (nn(pa, kv[:, vcols]) + nn(pb, kv2[:, vcols])) * rt
    selfr = mixed_scr[...].astype(BF)
    selfr_out[...] = selfr
    res3 = res2[...] + nn(selfr, so[...])
    n4, r4 = stats(res3)
    nt4 = (n4 * g2[...]).astype(BF)
    nt4_out[...] = nt4
    hid = nn(nt4, su[...])
    act = gelu(hid).astype(BF)
    act2_out[...] = act
    mixed_out[...] = res3 + nn(act, sd[...])
    each = out0.shape[0]
    for r, out in enumerate((out0, out1, out2, out3)):
        at = half * y + lax.rem(pos[2] + r, 4) * each
        out[...] = mixed_out[pl.ds(pl.multiple_of(at, each), each), :].astype(BF)
    hg = (nt(cot[...], sd[...]) * gelu_grad(hid)).astype(BF)
    hg2_out[...] = hg
    ng = nt(hg, su[...])
    gain_out[...] = jnp.sum(ng * n4, axis=0, keepdims=True)
    back3 = cot[...].astype(F32) + norm_back(ng * g2[...], n4, r4)
    back3_out[...] = back3
    sent3 = back3.astype(BF)
    sent3_out[...] = sent3
    mg_all = nt(sent3, so[...]).astype(BF)
    for h in range(HEADS):
        cols = slice(h * hd, (h + 1) * hd)
        vcols = slice(width + h * hd, width + (h + 1) * hd)
        mg = mg_all[:, cols].astype(F32)
        rt = tots[:, h : h + 1]
        ng_h = (mg * rt).astype(BF)
        tg = -jnp.sum(mg * mixed_scr[:, cols], axis=1, keepdims=True) * rt
        qh = q[:, cols]
        dq = None
        for src, dst, at in ((kv, dkv_out, 0), (kv2, dkv2_out, rows)):
            p = prob[h, :, at : at + rows]
            sg = (p.astype(F32) * (nt(ng_h, src[:, vcols]) + tg)).astype(BF)
            d = nn(sg, src[:, cols])
            dq = d if dq is None else dq + d
            dst[:, cols] = (tn(sg, qh) * hs).astype(dst.dtype)
            dst[:, vcols] = tn(p, ng_h).astype(dst.dtype)
        dq_out[:, cols] = (dq * hs).astype(BF)


def third_kernel(pos, dq, dkv, dkv2, back3, res2, res1, hid1, att, tot, gcol, wv, co, g1, fu, fd, gs, si, gain2,
                 pg_out, sent2_out, hg1_out, back1_out, gv_out, ht_give, ht_keep, scr, back1_scr, *, items):
    get = (si, fd, fu, co, wv).__getitem__
    rows, width = back3.shape
    chans = wv.shape[0]
    feat = scr.shape[0]
    base = feat - 16
    pg_out[:, 0:width] = dq[...]
    pg_out[:, width : 3 * width] = (dkv[...].astype(F32) + dkv2[...].astype(F32)).astype(BF)
    ng = nt(pg_out[...], get(0)[...])
    n3, r3 = stats(res2[...])
    gain_self = jnp.sum(ng * n3, axis=0, keepdims=True)
    back2 = back3[...] + norm_back(ng * gs[...], n3, r3)
    sent2 = back2.astype(BF)
    sent2_out[...] = sent2
    hg = (nt(sent2, get(1)[...]) * gelu_grad(hid1[...])).astype(BF)
    hg1_out[...] = hg
    ng = nt(hg, get(2)[...])
    n2, r2 = stats(res1[...])
    gain_first = jnp.sum(ng * n2, axis=0, keepdims=True)
    back1 = back2 + norm_back(ng * g1[...], n2, r2)
    back1_scr[...] = back1
    half = rows // 2
    back1_out[...] = back1_scr[pl.ds(pl.multiple_of(half * pos[3], half), half), :]
    sent1 = back1.astype(BF)
    ag = nt(sent1, get(3)[...]).astype(BF)
    rt = 1.0 / tot[...]
    raw = nt(get(4)[...], ag) * (rt * gcol[...])
    tg = -jnp.sum(att[...] * raw, axis=0, keepdims=True)
    raw = raw - jnp.sum(raw, axis=0, keepdims=True) / chans
    scr[...] = jnp.zeros(scr.shape, F32)
    scr[0:chans, :] = raw
    gv_out[0:base, :] = scr[0:base, :].astype(BF)
    row = lax.broadcasted_iota(jnp.int32, (16, rows), 0) + base
    tg_high = tg.astype(BF).astype(F32)
    high = jnp.where(row == chans, tg_high, scr[base:feat, :])
    high = jnp.where(row == chans + 1, tg - tg_high, high)
    gv_out[base:feat, :] = high.astype(BF)
    scr[0:chans, :] = att[...]
    ht = nn(scr[...].astype(BF), sent1)
    row = lax.broadcasted_iota(jnp.int32, (16, width), 0) + base
    high = ht[base:feat]
    for k, v in enumerate((gain_first, gain_self, gain2[...])):
        v_high = v.astype(BF).astype(F32)
        high = jnp.where(row == chans + 2 * k, v_high, high)
        high = jnp.where(row == chans + 2 * k + 1, v - v_high, high)
    lanes = width // (4 * items)
    for i in range(items):
        for q in range(4):
            k = lax.rem(i - pos[4] + items, items)
            cut = slice(i * 4 * lanes + q * lanes, i * 4 * lanes + (q + 1) * lanes)

            @pl.when((q // 2 == pos[3]) & (q % 2 == pos[1]))
            def _():
                ht_keep[k, 0:base, :] = ht[0:base, cut].astype(BF)
                ht_keep[k, base:feat, :] = high[:, cut].astype(BF)

            @pl.when((q // 2 == pos[3]) & (q % 2 != pos[1]))
            def _():
                ht_give[k, 0:base, :] = ht[0:base, cut].astype(BF)
                ht_give[k, base:feat, :] = high[:, cut].astype(BF)


def last_kernel(pos, b_mine, b_recv, lat, back1, gain, gcol, wq, wk, out, gt_keep, gt_give, scr, *, scale, items):
    chans, width = wk.shape
    feat = scr.shape[0]
    base = feat - 16
    b = (b_mine[...].astype(F32) + b_recv[...].astype(F32)) * scale
    bs = b[0:chans, :]
    rows_grad = tn((bs * gcol[...]).astype(BF), wk[...]).astype(BF)
    ng = nt(rows_grad, wq[...])
    n, r = stats(lat[0 : back1.shape[0], :].astype(F32))
    rounded = (n * gain[...]).astype(BF)
    gain_grad = jnp.sum(ng * n, axis=0, keepdims=True)
    out[...] = (back1[...] + norm_back(ng * gain[...], n, r)).astype(BF).reshape(out.shape)
    scr[...] = jnp.zeros(scr.shape, F32)
    scr[0:chans, :] = bs
    gt = nn(scr[...].astype(BF), rounded)
    row = lax.broadcasted_iota(jnp.int32, (16, width), 0) + base
    high = gt[base:feat]
    g_high = gain_grad.astype(BF).astype(F32)
    high = jnp.where(row == chans, g_high, high)
    high = jnp.where(row == chans + 1, gain_grad - g_high, high)
    lanes = width // (4 * items)
    for i in range(items):
        for q in range(4):
            k = lax.rem(i - pos[4] + items, items)
            yr = (q // 2) ^ pos[3]
            cut = slice(i * 4 * lanes + q * lanes, i * 4 * lanes + (q + 1) * lanes)

            @pl.when(q % 2 == pos[1])
            def _():
                gt_keep[yr, k, 0:base, :] = gt[0:base, cut].astype(BF)
                gt_keep[yr, k, base:feat, :] = high[:, cut].astype(BF)

            @pl.when(q % 2 != pos[1])
            def _():
                gt_give[yr, k, 0:base, :] = gt[0:base, cut].astype(BF)
                gt_give[yr, k, base:feat, :] = high[:, cut].astype(BF)


def columns(pos, width, items):
    lanes = width // (4 * items)
    at = []
    for lr in range(4):
        for k in range(items):
            start = lax.rem(pos[4] + k, items) * 4 * lanes + (pos[0] ^ lr) * lanes
            at.append(pl.multiple_of(start, lanes))
    return at, lanes


def join(full, parts, at, lanes):
    if lanes % 128 == 0:
        for off, part in zip(at, parts):
            full[:, pl.ds(off, lanes)] = part[...].astype(F32)
        return
    r = lax.broadcasted_iota(jnp.int32, (lanes, full.shape[1]), 0)
    c = lax.broadcasted_iota(jnp.int32, (lanes, full.shape[1]), 1)
    full[...] = jnp.zeros(full.shape, F32)
    for off, part in zip(at, parts):
        full[...] = full[...] + nn(part[...], (c == r + off).astype(F32).astype(BF))


def row_sums(prod):
    ones = jnp.ones((8, prod.shape[1]), BF)
    return nt(ones, prod.astype(BF))[0:1]


def value_kernel(pos, *refs, items):
    parts, refs = refs[: 4 * items], refs[4 * items :]
    gcol, wv, co, value_out, cross_out, vsum_out, *gains, full = refs
    feat = full.shape[0]
    parts = [p[feat : 2 * feat, :] for p in parts]
    chans, width = wv.shape
    rows = cross_out.shape[0]
    at, lanes = columns(pos, width, items)
    join(full, parts, at, lanes)
    hb = full[0:chans, :].astype(BF)
    for k in range(3):
        lo = chans + 2 * k
        gains[k][...] = full[lo : lo + 1, :] + full[lo + 1 : lo + 2, :]
    one = own_columns(width, rows, pos[5])
    wsel = (nn(wv[...], one) * gcol[...]).astype(BF)
    cross_out[...] = tn(wsel, hb)
    v = nt(hb, co[...])
    vsum_out[...] = row_sums(v * wv[...].astype(F32))
    value_out[...] = v * gcol[...]


def own_columns(width, rows, index):
    r = lax.broadcasted_iota(jnp.int32, (width, rows), 0)
    c = lax.broadcasted_iota(jnp.int32, (width, rows), 1)
    return (r == c + index * rows).astype(F32).astype(BF)


def key_kernel(pos, *refs, items):
    parts, refs = refs[: 4 * items], refs[4 * items :]
    gcol, wk, wq, vsum, *refs = refs
    key_out, query_out, psum_out, gain_out, full = refs
    feat = full.shape[0]
    parts = [p[0:feat, :] for p in parts]
    chans, width = wk.shape
    rows = query_out.shape[0]
    at, lanes = columns(pos, width, items)
    join(full, parts, at, lanes)
    gb = full[0:chans, :].astype(BF)
    gain_out[...] = full[chans : chans + 1, :] + full[chans + 1 : chans + 2, :]
    one = own_columns(lanes, rows, pos[2])
    sel = (nn(parts[0][0:chans, :], one) * gcol[...]).astype(BF)
    query_out[...] = tn(sel, wk[...])
    k = nn(gb, wq[...])
    psum_out[...] = row_sums(k * wk[...].astype(F32)) + vsum[...]
    key_out[...] = k * gcol[...]


def swap(x, kind, lat):
    if kind == "core":
        perm = [(s, s ^ 1) for s in range(lat)]
    else:
        perm = [(s, s ^ 2) for s in range(lat)]
    return lax.ppermute(x, "lat", perm)


def fetch(x, axis, n, r):
    return lax.ppermute(x, axis, [((d + r) % n, d) for d in range(n)])


def send(x, axis, n, r):
    return lax.ppermute(x, axis, [(d, (d + r) % n) for d in range(n)])


def near_first(n):
    return sorted(range(1, n), key=lambda r: min(r, n - r))


def plane(x, items, lat, y, k, back=False):
    perm = []
    for i in range(items):
        for l in range(lat):
            far = ((i + k) % items) * lat + (l ^ (2 * y))
            near = i * lat + l
            perm.append((far, near) if back else (near, far))
    return lax.ppermute(x, ("item", "lat"), perm)


class AllSum:
    def __init__(self, keep, give, items, pix, lat):
        self.sizes = items, pix, lat
        self.both = keep, swap(give, "core", lat)
        self.part = (lambda y, k: (y, k)) if keep.ndim == 4 else (lambda y, k: (k,))
        ys = 2 if keep.ndim == 4 else 1
        self.spots = [(y, k) for y in range(ys) for k in range(items)]

    def first(self):
        return [(BF, [(v, self.part(*at)) for v in self.both]) for at in self.spots]

    def after_first(self, res):
        items, _, lat = self.sizes
        self.terms = [res[0]] + [
            plane(v, items, lat, *at) for at, v in zip(self.spots[1:], res[1:])
        ]

    def now(self):
        return [(BF, [(v, ALL) for v in self.terms])]

    def all_pix(self, own):
        pix = self.sizes[1]
        self.terms = [own] + [fetch(own, "pix", pix, r) for r in near_first(pix)]

    def pix_pair(self, own, bit):
        pix = self.sizes[1]
        self.terms = [own, lax.ppermute(own, "pix", [(d, d ^ bit) for d in range(pix)])]

    def spread(self, total):
        items, _, lat = self.sizes
        near = [
            total if not (y or k) else plane(total, items, lat, y, k, back=True)
            for y in range(2)
            for k in range(items)
        ]
        far = [swap(v, "core", lat) for v in near]
        self.parts = near[:items] + far[:items] + near[items:] + far[items:]

    def spread_items(self, total):
        items = self.sizes[0]
        self.pieces = [total] + [fetch(total, "item", items, k) for k in range(1, items)]


def join_kernel(pos, *refs):
    *terms, rows, total, out0, out1, out2, out3 = refs
    value = terms[0][...].astype(F32)
    for t in terms[1:]:
        value = value + t[...].astype(F32)
    total[...] = value.astype(BF)
    for r, out in enumerate((out0, out1, out2, out3)):
        out[...] = rows[lax.rem(pos[2] + r, 4)]


def home_kernel(pos, *refs):
    *pieces, out = refs
    for r, p in enumerate(pieces):
        out[lax.rem(pos[2] - r + 4, 4)] = p[...]


def both_kernel(pos, *refs):
    *terms, other, out = refs
    feat = other.shape[0]
    value = terms[0][...].astype(F32)
    for t in terms[1:]:
        value = value + t[...].astype(F32)
    out[0:feat, :] = value.astype(BF)
    out[feat : 2 * feat, :] = other[...]


class Units:
    def __init__(self, mine, give, cols, items, pix, lat):
        self.sizes, self.cols = (items, pix, lat), cols
        self.both = mine, swap(give, "core", lat)

    def over_core(self):
        items = self.sizes[0]
        n = self.both[0].shape[0] // items
        return [(BF, [(v, (slice(k * n, (k + 1) * n),)) for v in self.both]) for k in range(items)]

    def hold(self, res):
        self.held = res

    def copies(self, first=0):
        return [(BF, [(v, ALL)]) for v in self.held[first:]]

    def over_items(self, res):
        items = self.sizes[0]
        self.terms = [self.held[0]] + [send(v, "item", items, k + 1) for k, v in enumerate(res)]

    def halves(self):
        n = self.terms[0].shape[0] // 2
        return [(BF, [(v, (slice(h * n, (h + 1) * n),)) for v in self.terms]) for h in range(2)]

    def over_pix(self, res, bit):
        pix = self.sizes[1]
        got = lax.ppermute(res[1], "pix", [(d, d ^ bit) for d in range(pix)])
        self.terms = [res[0], got]

    def grads(self):
        at, wanted = 0, []
        for c in self.cols:
            wanted.append((F32, [(v, (slice(None), slice(at, at + c))) for v in self.terms]))
            at += c
        return wanted


def make_units(chain, groups, items, pix, lat, deps=()):
    rows, width = groups[0][0][0].shape
    outs, ins, cols = [], [], []
    for pairs in groups:
        cols.append([right.shape[1] for _, right in pairs])
        outs += [((width // 4, sum(cols[-1])), BF)] * 2
        ins += [v for pair in pairs for v in pair]
    res = chain.run(
        lambda *r: matrix_kernel(*r, groups=[len(g) for g in groups], items=items, pix=pix),
        outs,
        ins,
        [pltpu.VMEM((width, rows), F32), pltpu.VMEM((width // 4, rows), F32)],
        deps=deps,
    )
    return [Units(res[2 * g], res[2 * g + 1], c, items, pix, lat) for g, c in enumerate(cols)]


def body(
    latents,
    pixels,
    size_ids,
    cross_gain,
    pixel_gain,
    query_weight,
    key_weight,
    value_weight,
    cross_output,
    first_gain,
    first_up,
    first_down,
    self_gain,
    self_inputs,
    self_output,
    second_gain,
    second_up,
    second_down,
    cotangent,
):
    images, lat_rows, width = latents.shape
    pix_rows, chans = pixels.shape[1:]
    lat, pix, items = lax.axis_size("lat"), lax.axis_size("pix"), lax.axis_size("item")
    assert lat == 4 and pix == 4 and images == pix
    feat = -(-(chans + 4) // 16) * 16
    l, z, it = lax.axis_index("lat"), lax.axis_index("pix"), lax.axis_index("item")
    core, yy = l % 2, l // 2
    block = l * pix + z
    pos = jnp.stack(
        [l, core, z, yy, it, it * (lat * pix) + block, block * pix_rows]
    ).astype(jnp.int32)
    chain = Chain(pos)
    rows = images * lat_rows
    lats = lat * rows
    lanes = width // (4 * items)
    scale = 1.0 / math.sqrt(width)
    row = lambda v: v.reshape(1, -1)
    (gcol,) = chain.run(column_kernel, [((chans, 1), F32)], [row(pixel_gain)])

    piece = ((2 * lat_rows, width), BF)
    shares = chain.run(share_kernel, [piece] * pix, [latents, cotangent])
    shares = [shares[0]] + [send(shares[k], "pix", pix, k) for k in range(1, pix)]
    ptile = min(512, pix_rows // 2)
    steps = pix_rows // ptile // 2
    feats = jnp.transpose(pixels, (2, 0, 1))

    def norm_half(part, before):
        start = part * steps
        (res,) = chain.run(
            lambda *r: pixel_norm_kernel(
                *r, tile=ptile, start=start, total=pix_rows * lat * pix
            ),
            [((images, feat, pix_rows), BF)],
            [size_ids, feats] + before,
            [pltpu.VMEM((chans, images, ptile), F32), pltpu.VMEM((16, ptile), F32)],
            grid=steps,
            in_specs=[SM, pl.BlockSpec((chans, images, ptile), lambda t, pos: (0, 0, t + start))]
            + [ANY] * part,
            out_specs=[pl.BlockSpec((images, feat, ptile), lambda t, pos: (0, 0, t + start))],
            aliases={3: 0} if part else {},
        )
        return res

    normed = norm_half(0, [])
    (qkt,) = chain.run(
        lambda *r: query_kernel(*r, scale=scale),
        [((feat, rows), BF)],
        [latents, row(cross_gain), query_weight, key_weight, gcol],
        [pltpu.VMEM((feat, rows), F32)],
    )
    level = [qkt] + [fetch(qkt, "pix", pix, r) for r in range(1, pix)]
    (stack,) = chain.run(
        lambda *r: stack_kernel(*r, images=images), [((images * feat, rows), BF)], level
    )
    normed = norm_half(1, [normed])
    stack_y = swap(stack, "y", lat)
    query = [stack, swap(stack, "core", lat), stack_y, swap(stack_y, "core", lat)]
    order = [1, 3, 2, 0]

    image_of = lambda r: lambda t, pos: (lax.rem(pos[2] + r, images), 0, 0)
    image_spec = lambda r: pl.BlockSpec((1, feat, pix_rows), image_of(r))
    half = ((feat, lats // 2), BF)
    full = ((feat, lats), BF)
    powered, query_all, part, from_z = {}, {}, {}, []

    def cross(r):
        powered[r], mine, give, query_all[r] = chain.run(
            lambda *a: cross_kernel(*a, at=r * feat),
            [((lats, pix_rows), BF), half, half, full],
            [*query, normed],
            [pltpu.VMEM((lats, feat), BF), pltpu.VMEM((feat, lats), F32)],
            in_specs=[None] * 4 + [image_spec(r)],
            work=3 * 10**9,
            limit=WIDE_LIMIT,
        )
        part[r] = mine, swap(give, "core", lat)

    def halves(*which):
        return [(BF, [(v, ALL) for v in part[r]]) for r in which]

    def pass_on(which, res):
        from_z.extend(send(v, "pix", pix, r) for r, v in zip(which, res))

    cross(order[0])
    cross(order[1])
    pass_on(order[:1], chain.sums(halves(order[0])))
    cross(order[2])
    (lc_mine,) = chain.run(gather_kernel, [((2 * rows, width), BF)], shares)
    lc_recv = swap(lc_mine, "y", lat)
    pass_on(order[1:3], chain.sums(halves(*order[1:3])))
    cross(order[3])
    (a_mine,) = chain.sums([(BF, [(v, ALL) for v in [*part[0], *from_z]])])
    a_recv = swap(a_mine, "y", lat)
    r2 = 2 * rows
    sq = (r2, width)
    att, tot, res1, nt2, hid1, act1, res2, nt3, q, kv = chain.run(
        first_kernel,
        [((chans, r2), F32), ((1, r2), F32), (sq, F32), (sq, BF), (sq, F32), (sq, BF), (sq, F32), (sq, BF), (sq, BF), ((r2, 2 * width), BF)],
        [a_mine, a_recv, lc_mine, lc_recv, gcol, value_weight, cross_output, row(first_gain), first_up, first_down, row(self_gain), self_inputs],
        [pltpu.VMEM(sq, BF)],
        limit=WIDE_LIMIT,
    )
    kv2 = swap(kv, "core", lat)
    image_rows = ((images, lat_rows, width), BF)
    rows_piece = ((lat_rows, width), BF)
    deal = lambda v: [v[0]] + [send(v[r], "pix", pix, r) for r in range(1, pix)]
    *out, selfr, sent3, back3, nt4, act2, hg2, gain2, dq, dkv, dkv_send, cot = chain.run(
        second_kernel,
        [rows_piece] * 4 + [(sq, BF), (sq, BF), (sq, F32), (sq, BF), (sq, BF), (sq, BF), ((1, width), F32), (sq, BF), ((r2, 2 * width), BF), ((r2, 2 * width), BF), (sq, BF)],
        [q, kv, kv2, res2, lc_mine, lc_recv, self_output, row(second_gain), second_up, second_down],
        [
            pltpu.VMEM((HEADS, r2, 2 * r2), BF),
            pltpu.VMEM(sq, F32),
            pltpu.VMEM((r2, 128), F32),
            pltpu.VMEM(sq, F32),
        ],
        limit=WIDE_LIMIT,
    )
    dkv2 = swap(dkv_send, "core", lat)
    (units_two,) = make_units(
        chain, [[(nt4, hg2), (act2, cot), (selfr, sent3)]], items, pix, lat
    )
    pg, sent2, hg1, back1, gvt, ht_give, ht_keep = chain.run(
        lambda *r: third_kernel(*r, items=items),
        [((r2, 3 * width), BF), (sq, BF), (sq, BF), ((rows, width), F32), ((feat, r2), BF)]
        + [((items, feat, lanes), BF)] * 2,
        [dq, dkv, dkv2, back3, res2, res1, hid1, att, tot, gcol, value_weight, cross_output, row(first_gain), first_up, first_down, row(self_gain), self_inputs, gain2],
        [pltpu.VMEM((feat, r2), F32), pltpu.VMEM(sq, F32)],
        limit=WIDE_LIMIT,
    )
    gv_at = {r: (fetch(gvt, "pix", pix, r) if r else gvt) for r in order}
    gv_both = {r: (v, swap(v, "core", lat)) for r, v in gv_at.items()}
    ht = AllSum(ht_keep, ht_give, items, pix, lat)
    units_two.hold(chain.sums(units_two.over_core()))
    units_two.over_items(units_two.held[1:])
    (latents_out,) = chain.run(home_kernel, [image_rows], deal(out), work=SMALL)
    (units_rest,) = make_units(
        chain, [[(nt3, pg), (nt2, hg1), (act1, sent2)]], items, pix, lat
    )
    first = ht.first()
    res = chain.sums(first + units_rest.over_core() + [(BF, [(gv_at[1], ALL)])])
    ht.after_first(res[: len(first)])
    units_rest.hold(res[len(first) : -1])
    gv_both[1] = gv_at[1], swap(res[-1], "core", lat)
    res = chain.sums(units_rest.copies(1) + units_two.halves())
    units_rest.over_items(res[: items - 1])
    units_two.over_pix(res[items - 1 :], 1)

    grad, part, from_z = None, {}, []

    def back(r, deps=()):
        nonlocal grad
        ins = [*gv_both[r], normed, powered[r], query_all[r]]
        grad, mine, give = chain.run(
            lambda *a: pixel_back_kernel(*a, chans=chans),
            [((images, feat, pix_rows), BF), half, half],
            ins + ([] if grad is None else [grad]),
            [
                pltpu.VMEM((feat, lats), BF),
                pltpu.VMEM((lats, feat), BF),
                pltpu.VMEM((feat, lats), BF),
                pltpu.VMEM((feat, lats), F32),
            ],
            in_specs=[None, None, image_spec(r), None, None] + ([] if grad is None else [ANY]),
            out_specs=[image_spec(r), None, None],
            aliases={} if grad is None else {6: 0},
            limit=WIDE_LIMIT,
            deps=deps,
        )
        part[r] = mine, swap(give, "core", lat)

    back(order[0], [gv_at[r] for r in order])
    ht.pix_pair(*chain.sums(ht.now()), 1)
    back(order[1], [v[1] for v in gv_both.values()])
    res = chain.sums(halves(order[0]) + ht.now() + units_two.halves())
    pass_on(order[:1], res[:1])
    ht.pix_pair(res[1], 2)
    units_two.over_pix(res[2:], 2)
    back(order[2])
    pass_on(order[1:3], chain.sums(halves(*order[1:3])))
    back(order[3])
    (pixel_grad,) = chain.run(
        interleave_kernel,
        [((chans, images, pix_rows), BF)],
        [grad],
        [pltpu.VMEM((chans, images, ptile), F32)],
        grid=pix_rows // ptile,
        in_specs=[pl.BlockSpec((images, feat, ptile), lambda t, pos: (0, 0, t))],
        out_specs=[pl.BlockSpec((chans, images, ptile), lambda t, pos: (0, 0, t))],
    )

    (ht_total,) = chain.sums(ht.now())

    def y_halves(pos, *refs):
        *terms, mine, give = refs
        for out, y in ((mine, pos[3]), (give, 1 - pos[3])):
            total = None
            for v in terms:
                v = v[:, pl.ds(pl.multiple_of(y * rows, rows), rows)].astype(F32)
                total = v if total is None else total + v
            out[...] = total.astype(out.dtype)

    quarter = (feat, rows)
    b_mine, b_give = chain.run(y_halves, [(quarter, F32), (quarter, BF)], [*part[0], *from_z])
    b_recv = swap(b_give, "y", lat)
    latent_grad, gt_keep, gt_give = chain.run(
        lambda *r: last_kernel(*r, scale=scale, items=items),
        [image_rows] + [((2, items, feat, lanes), BF)] * 2,
        [b_mine, b_recv, lc_mine, back1, row(cross_gain), gcol, query_weight, key_weight],
        [pltpu.VMEM((feat, rows), F32)],
    )
    gt = AllSum(gt_keep, gt_give, items, pix, lat)
    res = chain.sums(units_rest.halves() + units_two.grads())
    units_rest.over_pix(res[:2], 1)
    second_up_grad, second_down_grad, self_out_grad = res[2:]
    gt.after_first(chain.sums(gt.first()))
    own, *pieces = chain.run(
        join_kernel, [((feat, lanes), BF)] + [rows_piece] * pix, [*gt.terms, latent_grad]
    )
    gt.all_pix(own)
    gt.spread(
        *chain.run(both_kernel, [((2 * feat, lanes), BF)], [*gt.terms, ht_total])
    )
    own_rows = width // (items * lat * pix)
    results = [((chans, width), F32), ((own_rows, width), F32), ((1, chans), F32)]
    value_grad, cross_out_grad, vsum, gain_first, gain_self, gain_second = chain.run(
        lambda *r: value_kernel(*r, items=items),
        results + [((1, width), F32)] * 3,
        [*gt.parts, gcol, value_weight, cross_output],
        [pltpu.VMEM((feat, width), F32)],
    )
    units_rest.over_pix(chain.sums(units_rest.halves()), 2)
    key_grad, query_grad, psum, cross_gain_grad = chain.run(
        lambda *r: key_kernel(*r, items=items),
        results + [((1, width), F32)],
        [*gt.parts, gcol, key_weight, query_weight, vsum],
        [pltpu.VMEM((feat, width), F32)],
    )
    (latent_grad,) = chain.run(home_kernel, [image_rows], deal(pieces))
    self_in_grad, first_up_grad, first_down_grad = chain.sums(units_rest.grads())
    flat = lambda v: v.reshape(v.shape[1])
    return (
        latents_out,
        latent_grad,
        jnp.transpose(pixel_grad, (1, 2, 0)),
        query_grad,
        cross_out_grad,
        first_up_grad,
        first_down_grad,
        self_in_grad,
        self_out_grad,
        second_up_grad,
        second_down_grad,
        key_grad,
        value_grad,
        flat(cross_gain_grad),
        flat(psum),
        flat(gain_first),
        flat(gain_self),
        flat(gain_second),
    )


def solution(mesh):
    split = P("item", ("lat", "pix"), None)
    in_specs = (split, split, P("item")) + (P(),) * 15 + (split,)
    grads = P(("item", "lat", "pix"), None)
    out_specs = (split, split, split) + (grads,) * 8 + (P(),) * 7
    return jax.shard_map(body, mesh=mesh, in_specs=in_specs, out_specs=out_specs, check_vma=False)
```

```python
import math

import jax
import jax.numpy as jnp
from jax import lax
from jax.experimental import pallas as pl
from jax.experimental.pallas import tpu as pltpu
from jax.sharding import PartitionSpec as P

HEADS = 8
EPS = 1e-05
LOG2E = 1.4426950408889634
LN2 = 0.6931471805599453
BF = jnp.bfloat16
F32 = jnp.float32
VM = pl.BlockSpec(memory_space=pltpu.VMEM)
SM = pl.BlockSpec(memory_space=pltpu.SMEM)
ANY = pl.BlockSpec(memory_space=pl.ANY)
WORK = 5 * 10**9
SMALL = 10**9
LIMIT = 12 * 1024 * 1024
WIDE_LIMIT = 16 * 1024 * 1024


def nn(a, b):
    return lax.dot_general(a, b, (((1,), (0,)), ((), ())), preferred_element_type=F32)


def nt(a, b):
    return lax.dot_general(a, b, (((1,), (1,)), ((), ())), preferred_element_type=F32)


def tn(a, b):
    return lax.dot_general(a, b, (((0,), (0,)), ((), ())), preferred_element_type=F32)


def stats(v):
    c = v - jnp.mean(v, axis=-1, keepdims=True)
    r = lax.rsqrt(jnp.mean(c * c, axis=-1, keepdims=True) + EPS)
    return c * r, r


def norm_back(scaled, n, r):
    return r * (
        scaled
        - jnp.mean(scaled, axis=-1, keepdims=True)
        - n * jnp.mean(scaled * n, axis=-1, keepdims=True)
    )


K0 = math.sqrt(2.0 / math.pi)
K1 = 0.044715


def gelu(v):
    return 0.5 * v * (1.0 + jnp.tanh(K0 * (v + K1 * v * v * v)))


def gelu_grad(v):
    t = jnp.tanh(K0 * (v + K1 * v * v * v))
    return 0.5 * (1.0 + t) + 0.5 * v * (1.0 - t * t) * (K0 * (1.0 + 3.0 * K1 * v * v))


class Chain:
    def __init__(self, pos):
        self.pos = pos
        self.token = None

    def run(self, kernel, outs, ins, scratch=(), grid=None, in_specs=None, out_specs=None,
            deps=(), aliases=None, limit=LIMIT, work=WORK):
        before = [] if self.token is None else [self.token]
        n_ins, n_extra, n_outs = len(ins), len(before) + len(deps), len(outs)

        def body(pos, *refs):
            given = refs[:n_ins]
            results = refs[n_ins + n_extra : n_ins + n_extra + n_outs]
            refs[n_ins + n_extra + n_outs][...] = jnp.zeros((8, 128), F32)
            rest = refs[n_ins + n_extra + n_outs + 1 :]
            kernel(pos, *given, *results, *rest)

        fixed = lambda v: pl.BlockSpec(v.shape, lambda t, pos: (0,) * len(v.shape))
        shapes = [jax.ShapeDtypeStruct(*o) for o in outs]
        small = jax.ShapeDtypeStruct((8, 128), F32)
        where = lambda a: SM if a.dtype == jnp.int32 else fixed(a)
        specs = in_specs or [None] * n_ins
        specs = [s if s is not None else where(a) for s, a in zip(specs, ins)]
        o_specs = out_specs or [None] * n_outs
        o_specs = [s if s is not None else fixed(o) for s, o in zip(o_specs, shapes)]
        res = pl.pallas_call(
            body,
            grid_spec=pltpu.PrefetchScalarGridSpec(
                num_scalar_prefetch=1,
                grid=(grid or 1,),
                in_specs=specs + [fixed(v) for v in before] + [ANY] * len(deps),
                out_specs=tuple(o_specs + [fixed(small)]),
                scratch_shapes=list(scratch),
            ),
            out_shape=tuple(shapes + [small]),
            input_output_aliases=aliases or {},
            compiler_params=pltpu.CompilerParams(
                dimension_semantics=("arbitrary",), vmem_limit_bytes=limit
            ),
            cost_estimate=pl.CostEstimate(flops=work, bytes_accessed=100000, transcendentals=0),
        )(self.pos, *ins, *before, *deps)
        self.token = res[-1]
        return list(res[:-1])

    def sums(self, wanted, deps=()):
        arrays, place = [], {}
        for _, terms in wanted:
            for a, _ in terms:
                if id(a) not in place:
                    place[id(a)] = len(arrays)
                    arrays.append(a)
        outs = []
        for dtype, terms in wanted:
            a, index = terms[0]
            outs.append((jax.eval_shape(lambda v, index=index: v[index], a).shape, dtype))

        def kernel(pos, *refs):
            for n, (dtype, terms) in enumerate(wanted):
                total = None
                for a, index in terms:
                    v = refs[place[id(a)]][index].astype(F32)
                    total = v if total is None else total + v
                refs[len(arrays) + n][...] = total.astype(dtype)

        return self.run(kernel, outs, arrays, deps=deps, work=SMALL)


ALL = (Ellipsis,)


def query_kernel(pos, lat, gain, wq, wk, gcol, out, scr, *, scale):
    chans = wk.shape[0]
    x = lat[...].astype(F32)
    n, _ = stats(x.reshape(out.shape[1], x.shape[-1]))
    rounded = (n * gain[...]).astype(BF)
    query = nn(rounded, wq[...]).astype(BF)
    t = nt(wk[...], query) * gcol[...]
    t = (t - jnp.sum(t, axis=0, keepdims=True) / chans) * (scale * LOG2E)
    scr[...] = jnp.zeros(scr.shape, F32)
    scr[0:chans, :] = t
    out[...] = scr[...].astype(BF)


def stack_kernel(pos, *refs, images):
    *level, out = refs
    z = pos[2]
    feat = out.shape[0] // images
    wide = [v[...].astype(F32) for v in level]
    lat_rows = out.shape[1] // images
    slot = lax.broadcasted_iota(jnp.int32, wide[0].shape, 1) // lat_rows
    for r in range(images):
        im = lax.rem(z + r, images)
        total = None
        for rz in range(images):
            s = lax.rem(z + rz, images)
            v = pltpu.roll(wide[rz], lax.rem(s - im + images, images) * lat_rows, 1)
            total = v if total is None else jnp.where(slot == s, v, total)
        out[r * feat : (r + 1) * feat, :] = total.astype(BF)


def share_kernel(pos, lat, cot, *outs):
    n = len(outs)
    lat_rows = lat.shape[1]
    for r in range(n):
        im = lax.rem(pos[2] + r, n)
        outs[r][0:lat_rows, :] = lat[im]
        outs[r][lat_rows : 2 * lat_rows, :] = cot[im]


def gather_kernel(pos, *refs):
    *pieces, out = refs
    n = len(pieces)
    lat_rows = pieces[0].shape[0] // 2
    for r in range(n):
        src = lax.rem(pos[2] - r + n, n)
        for half in range(2):
            at = pl.multiple_of(half * n * lat_rows + src * lat_rows, lat_rows)
            out[pl.ds(at, lat_rows), :] = pieces[r][half * lat_rows : (half + 1) * lat_rows, :]


def column_kernel(pos, row, out):
    n = row.shape[1]
    same = lax.broadcasted_iota(jnp.int32, (n, n), 0) == lax.broadcasted_iota(jnp.int32, (n, n), 1)
    out[...] = jnp.sum(jnp.where(same, row[...], 0.0), axis=1, keepdims=True)


def pixel_norm_kernel(pos, ids, pix, *refs, tile, start, total):
    out, wide, tail = refs[-3:]
    t = pl.program_id(0) + start
    chans, images = pix.shape[:2]
    feat = out.shape[1]
    base = feat - 16
    wide[...] = pix[...].astype(F32)
    row = lax.broadcasted_iota(jnp.int32, (16, tile), 0) + base
    lane = lax.broadcasted_iota(jnp.int32, (1, tile), 1) + t * tile
    for i in range(images):
        x = wide[:, i, :]
        x = x - jnp.sum(x, axis=0, keepdims=True) / chans
        var = jnp.sum(x * x, axis=0, keepdims=True) / chans
        size = jnp.where(ids[i] == 0, 25, jnp.where(ids[i] == 1, 49, 81))
        count = lax.div(total * size, 81) - pos[6]
        valid = jnp.where(lane < count, 1.0, 0.0)
        inv = lax.rsqrt(var + EPS) * valid
        inv_high = inv.astype(BF).astype(F32)
        x = x * inv
        out[i, 0:base, :] = x[0:base].astype(BF)
        tail[...] = jnp.zeros(tail.shape, F32)
        tail[0 : chans - base, :] = x[base:chans]
        high = tail[...]
        high = jnp.where((row == chans) | (row == chans + 1), valid, high)
        high = jnp.where(row == chans + 2, inv_high, high)
        high = jnp.where(row == chans + 3, inv - inv_high, high)
        out[i, base:feat, :] = high.astype(BF)


def cross_kernel(pos, *refs, at):
    pieces, refs = refs[:4], refs[4:]
    nt_ref, p_out, mine, send, qkt, qk, acc = refs
    t = pl.program_id(0)
    lpos, core = pos[0], pos[1]
    group = pieces[0].shape[1]
    feat = qkt.shape[0]
    row = at

    @pl.when(t == 0)
    def _():
        for rl in range(4):
            at = pl.multiple_of(group * (lpos ^ rl), group)
            qkt[:, pl.ds(at, group)] = pieces[rl][row : row + feat, :]
        qk[...] = jnp.transpose(qkt[...].astype(F32), (1, 0)).astype(BF)

    n = nt_ref[0]
    p = jnp.exp2(nn(qk[...], n)).astype(BF)
    p_out[...] = p
    part = nt(n, p)

    @pl.when(t == 0)
    def _():
        acc[...] = part

    @pl.when(t != 0)
    def _():
        acc[...] = acc[...] + part

    @pl.when(t == pl.num_programs(0) - 1)
    def _():
        split_halves(acc, mine, send, core, group)


def split_halves(acc, mine, send, core, group):
    for y in range(2):
        a = pl.multiple_of(2 * group * y + group * core, group)
        b = pl.multiple_of(2 * group * y + group * (1 - core), group)
        mine[:, group * y : group * (y + 1)] = acc[:, pl.ds(a, group)].astype(BF)
        send[:, group * y : group * (y + 1)] = acc[:, pl.ds(b, group)].astype(BF)


def pixel_back_kernel(pos, *refs, chans):
    gv_mine, gv_other, nt_ref, p_ref, qkt_ref = refs[:5]
    refs = refs[-7:]
    grad, mine, send, gvt, gv, qktb, acc = refs
    t = pl.program_id(0)
    core = pos[1]
    feat, lats = gv.shape[1], gv.shape[0]
    group = lats // 4
    base = feat - 16

    @pl.when(t == 0)
    def _():
        for ref, c in ((gv_mine, core), (gv_other, 1 - core)):
            for y in range(2):
                at = pl.multiple_of(2 * group * y + group * c, group)
                gvt[:, pl.ds(at, group)] = ref[:, group * y : group * (y + 1)]
        gv[...] = jnp.transpose(gvt[...].astype(F32), (1, 0)).astype(BF)
        qktb[...] = (qkt_ref[...].astype(F32) * LN2).astype(BF)

    n = nt_ref[0]
    p = p_ref[...]
    ds = (p.astype(F32) * nn(gv[...], n)).astype(BF)
    part = nt(n, ds)
    dn = nn(qktb[...], ds) + nn(gvt[...], p)
    nf = n.astype(F32)
    low, high = nf[0:base], nf[base:feat]
    row = lax.broadcasted_iota(jnp.int32, high.shape, 0) + base
    inv = jnp.sum(
        jnp.where((row == chans + 2) | (row == chans + 3), high, 0.0), axis=0, keepdims=True
    )
    high = jnp.where(row < chans, high, 0.0)
    m2 = (
        jnp.sum(dn[0:base] * low, axis=0, keepdims=True)
        + jnp.sum(dn[base:feat] * high, axis=0, keepdims=True)
    ) / chans
    grad[0, 0:base, :] = (inv * (dn[0:base] - low * m2)).astype(BF)
    grad[0, base:feat, :] = (inv * (dn[base:feat] - high * m2)).astype(BF)

    @pl.when(t == 0)
    def _():
        acc[...] = part

    @pl.when(t != 0)
    def _():
        acc[...] = acc[...] + part

    @pl.when(t == pl.num_programs(0) - 1)
    def _():
        split_halves(acc, mine, send, core, group)


def interleave_kernel(pos, src, out, wide):
    chans, images = out.shape[:2]
    for i in range(images):
        wide[:, i, :] = src[i, 0:chans, :].astype(F32)
    out[...] = wide[...].astype(BF)


def matrix_kernel(pos, *refs, groups, items, pix):
    z, y, core, it = pos[2], pos[3], pos[1], pos[4]
    scr, sel = refs[-2:]
    n_ins = 2 * sum(groups)
    ins, outs = refs[:n_ins], refs[n_ins:-2]
    width = scr.shape[0]
    part = width // items
    quarter = part // 4
    each = quarter // pix
    at = 0
    for g, units in enumerate(groups):
        at_col = 0
        for u in range(units):
            left, right = ins[2 * at], ins[2 * at + 1]
            at += 1
            cols = right.shape[1]
            scr[...] = jnp.transpose(left[...].astype(F32), (1, 0))
            for cc in range(2):
                for k in range(items):
                    for n, kp in enumerate((0, 2, 1, 3)):
                        off = (
                            lax.rem(it + k, items) * part
                            + (2 * y + (core ^ cc)) * quarter
                            + (z ^ kp) * each
                        )
                        to = k * quarter + n * each
                        sel[to : to + each, :] = scr[pl.ds(pl.multiple_of(off, each), each), :]
                res = nn(sel[...].astype(BF), right[...]).astype(BF)
                outs[2 * g + cc][:, at_col : at_col + cols] = res
            at_col += cols


def first_kernel(pos, a_mine, a_recv, lc_mine, lc_recv, gcol, wv, co, g1, fu, fd, gs, si,
                 att_out, tot_out, res1_out, nt2_out, hid1_out, act1_out, res2_out, nt3_out, q_out, kv_out, lat):
    get = (wv, co, fu, fd, si).__getitem__
    y = pos[3]
    half = lc_mine.shape[0] // 2
    width = lat.shape[1]
    chans = wv.shape[0]
    lat[pl.ds(pl.multiple_of(half * y, half), half), :] = lc_mine[0:half, :]
    lat[pl.ds(pl.multiple_of(half * (1 - y), half), half), :] = lc_recv[0:half, :]
    a = a_mine[...].astype(F32) + a_recv[...].astype(F32)
    tot = a[chans : chans + 1, :]
    att = a[0:chans, :] / tot
    att_out[...] = att
    tot_out[...] = tot
    mixed = tn((att * gcol[...]).astype(BF), get(0)[...]).astype(BF)
    res1 = lat[...].astype(F32) + nn(mixed, get(1)[...])
    res1_out[...] = res1
    n2, _ = stats(res1)
    nt2 = (n2 * g1[...]).astype(BF)
    nt2_out[...] = nt2
    hid = nn(nt2, get(2)[...])
    hid1_out[...] = hid
    act = gelu(hid).astype(BF)
    act1_out[...] = act
    res2 = res1 + nn(act, get(3)[...])
    res2_out[...] = res2
    n3, _ = stats(res2)
    nt3 = (n3 * gs[...]).astype(BF)
    nt3_out[...] = nt3
    proj = get(4)
    kv_out[...] = nn(nt3, proj[:, width : 3 * width]).astype(BF)
    q_out[...] = nn(nt3, proj[:, 0:width]).astype(BF)


def second_kernel(pos, q, kv, kv2, res2, lc_mine, lc_recv, so, g2, su, sd,
                  out0, out1, out2, out3, selfr_out, sent3_out, back3_out, nt4_out, act2_out, hg2_out, gain_out, dq_out, dkv_out, dkv2_out, cot,
                  prob, mixed_scr, tots, mixed_out):
    y = pos[3]
    half = lc_mine.shape[0] // 2
    rows, width = res2.shape
    hd = width // HEADS
    hs = 1.0 / math.sqrt(hd)
    cot[pl.ds(pl.multiple_of(half * y, half), half), :] = lc_mine[half : 2 * half, :]
    cot[pl.ds(pl.multiple_of(half * (1 - y), half), half), :] = lc_recv[half : 2 * half, :]
    for h in range(HEADS):
        cols = slice(h * hd, (h + 1) * hd)
        vcols = slice(width + h * hd, width + (h + 1) * hd)
        qh = q[:, cols]
        pa = jnp.exp2(nt(qh, kv[:, cols]) * (hs * LOG2E))
        pb = jnp.exp2(nt(qh, kv2[:, cols]) * (hs * LOG2E))
        tot = jnp.sum(pa, axis=1, keepdims=True) + jnp.sum(pb, axis=1, keepdims=True)
        pa, pb = pa.astype(BF), pb.astype(BF)
        prob[h, :, 0:rows] = pa
        prob[h, :, rows : 2 * rows] = pb
        rt = 1.0 / tot
        tots[:, h : h + 1] = rt
        mixed_scr[:, cols] = (nn(pa, kv[:, vcols]) + nn(pb, kv2[:, vcols])) * rt
    selfr = mixed_scr[...].astype(BF)
    selfr_out[...] = selfr
    res3 = res2[...] + nn(selfr, so[...])
    n4, r4 = stats(res3)
    nt4 = (n4 * g2[...]).astype(BF)
    nt4_out[...] = nt4
    hid = nn(nt4, su[...])
    act = gelu(hid).astype(BF)
    act2_out[...] = act
    mixed_out[...] = res3 + nn(act, sd[...])
    each = out0.shape[0]
    for r, out in enumerate((out0, out1, out2, out3)):
        at = half * y + lax.rem(pos[2] + r, 4) * each
        out[...] = mixed_out[pl.ds(pl.multiple_of(at, each), each), :].astype(BF)
    hg = (nt(cot[...], sd[...]) * gelu_grad(hid)).astype(BF)
    hg2_out[...] = hg
    ng = nt(hg, su[...])
    gain_out[...] = jnp.sum(ng * n4, axis=0, keepdims=True)
    back3 = cot[...].astype(F32) + norm_back(ng * g2[...], n4, r4)
    back3_out[...] = back3
    sent3 = back3.astype(BF)
    sent3_out[...] = sent3
    mg_all = nt(sent3, so[...]).astype(BF)
    for h in range(HEADS):
        cols = slice(h * hd, (h + 1) * hd)
        vcols = slice(width + h * hd, width + (h + 1) * hd)
        mg = mg_all[:, cols].astype(F32)
        rt = tots[:, h : h + 1]
        ng_h = (mg * rt).astype(BF)
        tg = -jnp.sum(mg * mixed_scr[:, cols], axis=1, keepdims=True) * rt
        qh = q[:, cols]
        dq = None
        for src, dst, at in ((kv, dkv_out, 0), (kv2, dkv2_out, rows)):
            p = prob[h, :, at : at + rows]
            sg = (p.astype(F32) * (nt(ng_h, src[:, vcols]) + tg)).astype(BF)
            d = nn(sg, src[:, cols])
            dq = d if dq is None else dq + d
            dst[:, cols] = (tn(sg, qh) * hs).astype(dst.dtype)
            dst[:, vcols] = tn(p, ng_h).astype(dst.dtype)
        dq_out[:, cols] = (dq * hs).astype(BF)


def third_kernel(pos, dq, dkv, dkv2, back3, res2, res1, hid1, att, tot, gcol, wv, co, g1, fu, fd, gs, si, gain2,
                 pg_out, sent2_out, hg1_out, back1_out, gv_out, ht_give, ht_keep, scr, back1_scr, *, items):
    get = (si, fd, fu, co, wv).__getitem__
    rows, width = back3.shape
    chans = wv.shape[0]
    feat = scr.shape[0]
    base = feat - 16
    pg_out[:, 0:width] = dq[...]
    pg_out[:, width : 3 * width] = (dkv[...].astype(F32) + dkv2[...].astype(F32)).astype(BF)
    ng = nt(pg_out[...], get(0)[...])
    n3, r3 = stats(res2[...])
    gain_self = jnp.sum(ng * n3, axis=0, keepdims=True)
    back2 = back3[...] + norm_back(ng * gs[...], n3, r3)
    sent2 = back2.astype(BF)
    sent2_out[...] = sent2
    hg = (nt(sent2, get(1)[...]) * gelu_grad(hid1[...])).astype(BF)
    hg1_out[...] = hg
    ng = nt(hg, get(2)[...])
    n2, r2 = stats(res1[...])
    gain_first = jnp.sum(ng * n2, axis=0, keepdims=True)
    back1 = back2 + norm_back(ng * g1[...], n2, r2)
    back1_scr[...] = back1
    half = rows // 2
    back1_out[...] = back1_scr[pl.ds(pl.multiple_of(half * pos[3], half), half), :]
    sent1 = back1.astype(BF)
    ag = nt(sent1, get(3)[...]).astype(BF)
    rt = 1.0 / tot[...]
    raw = nt(get(4)[...], ag) * (rt * gcol[...])
    tg = -jnp.sum(att[...] * raw, axis=0, keepdims=True)
    raw = raw - jnp.sum(raw, axis=0, keepdims=True) / chans
    scr[...] = jnp.zeros(scr.shape, F32)
    scr[0:chans, :] = raw
    gv_out[0:base, :] = scr[0:base, :].astype(BF)
    row = lax.broadcasted_iota(jnp.int32, (16, rows), 0) + base
    tg_high = tg.astype(BF).astype(F32)
    high = jnp.where(row == chans, tg_high, scr[base:feat, :])
    high = jnp.where(row == chans + 1, tg - tg_high, high)
    gv_out[base:feat, :] = high.astype(BF)
    scr[0:chans, :] = att[...]
    ht = nn(scr[...].astype(BF), sent1)
    row = lax.broadcasted_iota(jnp.int32, (16, width), 0) + base
    high = ht[base:feat]
    for k, v in enumerate((gain_first, gain_self, gain2[...])):
        v_high = v.astype(BF).astype(F32)
        high = jnp.where(row == chans + 2 * k, v_high, high)
        high = jnp.where(row == chans + 2 * k + 1, v - v_high, high)
    lanes = width // (4 * items)
    for i in range(items):
        for q in range(4):
            k = lax.rem(i - pos[4] + items, items)
            cut = slice(i * 4 * lanes + q * lanes, i * 4 * lanes + (q + 1) * lanes)

            @pl.when((q // 2 == pos[3]) & (q % 2 == pos[1]))
            def _():
                ht_keep[k, 0:base, :] = ht[0:base, cut].astype(BF)
                ht_keep[k, base:feat, :] = high[:, cut].astype(BF)

            @pl.when((q // 2 == pos[3]) & (q % 2 != pos[1]))
            def _():
                ht_give[k, 0:base, :] = ht[0:base, cut].astype(BF)
                ht_give[k, base:feat, :] = high[:, cut].astype(BF)


def last_kernel(pos, b_mine, b_recv, lat, back1, gain, gcol, wq, wk, out, gt_keep, gt_give, scr, *, scale, items):
    chans, width = wk.shape
    feat = scr.shape[0]
    base = feat - 16
    b = (b_mine[...].astype(F32) + b_recv[...].astype(F32)) * scale
    bs = b[0:chans, :]
    rows_grad = tn((bs * gcol[...]).astype(BF), wk[...]).astype(BF)
    ng = nt(rows_grad, wq[...])
    n, r = stats(lat[0 : back1.shape[0], :].astype(F32))
    rounded = (n * gain[...]).astype(BF)
    gain_grad = jnp.sum(ng * n, axis=0, keepdims=True)
    out[...] = (back1[...] + norm_back(ng * gain[...], n, r)).astype(BF).reshape(out.shape)
    scr[...] = jnp.zeros(scr.shape, F32)
    scr[0:chans, :] = bs
    gt = nn(scr[...].astype(BF), rounded)
    row = lax.broadcasted_iota(jnp.int32, (16, width), 0) + base
    high = gt[base:feat]
    g_high = gain_grad.astype(BF).astype(F32)
    high = jnp.where(row == chans, g_high, high)
    high = jnp.where(row == chans + 1, gain_grad - g_high, high)
    lanes = width // (4 * items)
    for i in range(items):
        for q in range(4):
            k = lax.rem(i - pos[4] + items, items)
            yr = (q // 2) ^ pos[3]
            cut = slice(i * 4 * lanes + q * lanes, i * 4 * lanes + (q + 1) * lanes)

            @pl.when(q % 2 == pos[1])
            def _():
                gt_keep[yr, k, 0:base, :] = gt[0:base, cut].astype(BF)
                gt_keep[yr, k, base:feat, :] = high[:, cut].astype(BF)

            @pl.when(q % 2 != pos[1])
            def _():
                gt_give[yr, k, 0:base, :] = gt[0:base, cut].astype(BF)
                gt_give[yr, k, base:feat, :] = high[:, cut].astype(BF)


def columns(pos, width, items):
    lanes = width // (4 * items)
    at = []
    for lr in range(4):
        for k in range(items):
            start = lax.rem(pos[4] + k, items) * 4 * lanes + (pos[0] ^ lr) * lanes
            at.append(pl.multiple_of(start, lanes))
    return at, lanes


def join(full, parts, at, lanes):
    if lanes % 128 == 0:
        for off, part in zip(at, parts):
            full[:, pl.ds(off, lanes)] = part[...].astype(F32)
        return
    r = lax.broadcasted_iota(jnp.int32, (lanes, full.shape[1]), 0)
    c = lax.broadcasted_iota(jnp.int32, (lanes, full.shape[1]), 1)
    full[...] = jnp.zeros(full.shape, F32)
    for off, part in zip(at, parts):
        full[...] = full[...] + nn(part[...], (c == r + off).astype(F32).astype(BF))


def row_sums(prod):
    ones = jnp.ones((8, prod.shape[1]), BF)
    return nt(ones, prod.astype(BF))[0:1]


def value_kernel(pos, *refs, items):
    parts, refs = refs[: 4 * items], refs[4 * items :]
    gcol, wv, co, value_out, cross_out, vsum_out, *gains, full = refs
    feat = full.shape[0]
    parts = [p[feat : 2 * feat, :] for p in parts]
    chans, width = wv.shape
    rows = cross_out.shape[0]
    at, lanes = columns(pos, width, items)
    join(full, parts, at, lanes)
    hb = full[0:chans, :].astype(BF)
    for k in range(3):
        lo = chans + 2 * k
        gains[k][...] = full[lo : lo + 1, :] + full[lo + 1 : lo + 2, :]
    one = own_columns(width, rows, pos[5])
    wsel = (nn(wv[...], one) * gcol[...]).astype(BF)
    cross_out[...] = tn(wsel, hb)
    v = nt(hb, co[...])
    vsum_out[...] = row_sums(v * wv[...].astype(F32))
    value_out[...] = v * gcol[...]


def own_columns(width, rows, index):
    r = lax.broadcasted_iota(jnp.int32, (width, rows), 0)
    c = lax.broadcasted_iota(jnp.int32, (width, rows), 1)
    return (r == c + index * rows).astype(F32).astype(BF)


def key_kernel(pos, *refs, items):
    parts, refs = refs[: 4 * items], refs[4 * items :]
    gcol, wk, wq, vsum, *refs = refs
    key_out, query_out, psum_out, gain_out, full = refs
    feat = full.shape[0]
    parts = [p[0:feat, :] for p in parts]
    chans, width = wk.shape
    rows = query_out.shape[0]
    at, lanes = columns(pos, width, items)
    join(full, parts, at, lanes)
    gb = full[0:chans, :].astype(BF)
    gain_out[...] = full[chans : chans + 1, :] + full[chans + 1 : chans + 2, :]
    one = own_columns(lanes, rows, pos[2])
    sel = (nn(parts[0][0:chans, :], one) * gcol[...]).astype(BF)
    query_out[...] = tn(sel, wk[...])
    k = nn(gb, wq[...])
    psum_out[...] = row_sums(k * wk[...].astype(F32)) + vsum[...]
    key_out[...] = k * gcol[...]


def swap(x, kind, lat):
    if kind == "core":
        perm = [(s, s ^ 1) for s in range(lat)]
    else:
        perm = [(s, s ^ 2) for s in range(lat)]
    return lax.ppermute(x, "lat", perm)


def fetch(x, axis, n, r):
    return lax.ppermute(x, axis, [((d + r) % n, d) for d in range(n)])


def send(x, axis, n, r):
    return lax.ppermute(x, axis, [(d, (d + r) % n) for d in range(n)])


def near_first(n):
    return sorted(range(1, n), key=lambda r: min(r, n - r))


def plane(x, items, lat, y, k, back=False):
    perm = []
    for i in range(items):
        for l in range(lat):
            far = ((i + k) % items) * lat + (l ^ (2 * y))
            near = i * lat + l
            perm.append((far, near) if back else (near, far))
    return lax.ppermute(x, ("item", "lat"), perm)


class AllSum:
    def __init__(self, keep, give, items, pix, lat):
        self.sizes = items, pix, lat
        self.both = keep, swap(give, "core", lat)
        self.part = (lambda y, k: (y, k)) if keep.ndim == 4 else (lambda y, k: (k,))
        ys = 2 if keep.ndim == 4 else 1
        self.spots = [(y, k) for y in range(ys) for k in range(items)]

    def first(self):
        return [(BF, [(v, self.part(*at)) for v in self.both]) for at in self.spots]

    def after_first(self, res):
        items, _, lat = self.sizes
        self.terms = [res[0]] + [
            plane(v, items, lat, *at) for at, v in zip(self.spots[1:], res[1:])
        ]

    def now(self):
        return [(BF, [(v, ALL) for v in self.terms])]

    def all_pix(self, own):
        pix = self.sizes[1]
        self.terms = [own] + [fetch(own, "pix", pix, r) for r in near_first(pix)]

    def pix_pair(self, own, bit):
        pix = self.sizes[1]
        self.terms = [own, lax.ppermute(own, "pix", [(d, d ^ bit) for d in range(pix)])]

    def spread(self, total):
        items, _, lat = self.sizes
        near = [
            total if not (y or k) else plane(total, items, lat, y, k, back=True)
            for y in range(2)
            for k in range(items)
        ]
        far = [swap(v, "core", lat) for v in near]
        self.parts = near[:items] + far[:items] + near[items:] + far[items:]

    def spread_items(self, total):
        items = self.sizes[0]
        self.pieces = [total] + [fetch(total, "item", items, k) for k in range(1, items)]


def join_kernel(pos, *refs):
    *terms, rows, total, out0, out1, out2, out3 = refs
    value = terms[0][...].astype(F32)
    for t in terms[1:]:
        value = value + t[...].astype(F32)
    total[...] = value.astype(BF)
    for r, out in enumerate((out0, out1, out2, out3)):
        out[...] = rows[lax.rem(pos[2] + r, 4)]


def home_kernel(pos, *refs):
    *pieces, out = refs
    for r, p in enumerate(pieces):
        out[lax.rem(pos[2] - r + 4, 4)] = p[...]


def both_kernel(pos, *refs):
    *terms, other, out = refs
    feat = other.shape[0]
    value = terms[0][...].astype(F32)
    for t in terms[1:]:
        value = value + t[...].astype(F32)
    out[0:feat, :] = value.astype(BF)
    out[feat : 2 * feat, :] = other[...]


class Units:
    def __init__(self, mine, give, cols, items, pix, lat):
        self.sizes, self.cols = (items, pix, lat), cols
        self.both = mine, swap(give, "core", lat)

    def over_core(self):
        items = self.sizes[0]
        n = self.both[0].shape[0] // items
        return [(BF, [(v, (slice(k * n, (k + 1) * n),)) for v in self.both]) for k in range(items)]

    def hold(self, res):
        self.held = res

    def copies(self, first=0):
        return [(BF, [(v, ALL)]) for v in self.held[first:]]

    def over_items(self, res):
        items = self.sizes[0]
        self.terms = [self.held[0]] + [send(v, "item", items, k + 1) for k, v in enumerate(res)]

    def halves(self):
        n = self.terms[0].shape[0] // 2
        return [(BF, [(v, (slice(h * n, (h + 1) * n),)) for v in self.terms]) for h in range(2)]

    def over_pix(self, res, bit):
        pix = self.sizes[1]
        got = lax.ppermute(res[1], "pix", [(d, d ^ bit) for d in range(pix)])
        self.terms = [res[0], got]

    def grads(self):
        at, wanted = 0, []
        for c in self.cols:
            wanted.append((F32, [(v, (slice(None), slice(at, at + c))) for v in self.terms]))
            at += c
        return wanted


def make_units(chain, groups, items, pix, lat, deps=()):
    rows, width = groups[0][0][0].shape
    outs, ins, cols = [], [], []
    for pairs in groups:
        cols.append([right.shape[1] for _, right in pairs])
        outs += [((width // 4, sum(cols[-1])), BF)] * 2
        ins += [v for pair in pairs for v in pair]
    res = chain.run(
        lambda *r: matrix_kernel(*r, groups=[len(g) for g in groups], items=items, pix=pix),
        outs,
        ins,
        [pltpu.VMEM((width, rows), F32), pltpu.VMEM((width // 4, rows), F32)],
        deps=deps,
    )
    return [Units(res[2 * g], res[2 * g + 1], c, items, pix, lat) for g, c in enumerate(cols)]


def body(
    latents,
    pixels,
    size_ids,
    cross_gain,
    pixel_gain,
    query_weight,
    key_weight,
    value_weight,
    cross_output,
    first_gain,
    first_up,
    first_down,
    self_gain,
    self_inputs,
    self_output,
    second_gain,
    second_up,
    second_down,
    cotangent,
):
    images, lat_rows, width = latents.shape
    pix_rows, chans = pixels.shape[1:]
    lat, pix, items = lax.axis_size("lat"), lax.axis_size("pix"), lax.axis_size("item")
    assert lat == 4 and pix == 4 and images == pix
    feat = -(-(chans + 4) // 16) * 16
    l, z, it = lax.axis_index("lat"), lax.axis_index("pix"), lax.axis_index("item")
    core, yy = l % 2, l // 2
    block = l * pix + z
    pos = jnp.stack(
        [l, core, z, yy, it, it * (lat * pix) + block, block * pix_rows]
    ).astype(jnp.int32)
    chain = Chain(pos)
    rows = images * lat_rows
    lats = lat * rows
    lanes = width // (4 * items)
    scale = 1.0 / math.sqrt(width)
    row = lambda v: v.reshape(1, -1)
    (gcol,) = chain.run(column_kernel, [((chans, 1), F32)], [row(pixel_gain)])

    piece = ((2 * lat_rows, width), BF)
    shares = chain.run(share_kernel, [piece] * pix, [latents, cotangent])
    shares = [shares[0]] + [send(shares[k], "pix", pix, k) for k in range(1, pix)]
    ptile = min(512, pix_rows // 2)
    steps = pix_rows // ptile // 2
    feats = jnp.transpose(pixels, (2, 0, 1))

    def norm_half(part, before):
        start = part * steps
        (res,) = chain.run(
            lambda *r: pixel_norm_kernel(
                *r, tile=ptile, start=start, total=pix_rows * lat * pix
            ),
            [((images, feat, pix_rows), BF)],
            [size_ids, feats] + before,
            [pltpu.VMEM((chans, images, ptile), F32), pltpu.VMEM((16, ptile), F32)],
            grid=steps,
            in_specs=[SM, pl.BlockSpec((chans, images, ptile), lambda t, pos: (0, 0, t + start))]
            + [ANY] * part,
            out_specs=[pl.BlockSpec((images, feat, ptile), lambda t, pos: (0, 0, t + start))],
            aliases={3: 0} if part else {},
        )
        return res

    normed = norm_half(0, [])
    (qkt,) = chain.run(
        lambda *r: query_kernel(*r, scale=scale),
        [((feat, rows), BF)],
        [latents, row(cross_gain), query_weight, key_weight, gcol],
        [pltpu.VMEM((feat, rows), F32)],
    )
    level = [qkt] + [fetch(qkt, "pix", pix, r) for r in range(1, pix)]
    (stack,) = chain.run(
        lambda *r: stack_kernel(*r, images=images), [((images * feat, rows), BF)], level
    )
    normed = norm_half(1, [normed])
    stack_y = swap(stack, "y", lat)
    query = [stack, swap(stack, "core", lat), stack_y, swap(stack_y, "core", lat)]
    order = [1, 3, 2, 0]

    image_of = lambda r: lambda t, pos: (lax.rem(pos[2] + r, images), 0, 0)
    image_spec = lambda r: pl.BlockSpec((1, feat, pix_rows), image_of(r))
    half = ((feat, lats // 2), BF)
    full = ((feat, lats), BF)
    powered, query_all, part, from_z = {}, {}, {}, []

    def cross(r):
        powered[r], mine, give, query_all[r] = chain.run(
            lambda *a: cross_kernel(*a, at=r * feat),
            [((lats, pix_rows), BF), half, half, full],
            [*query, normed],
            [pltpu.VMEM((lats, feat), BF), pltpu.VMEM((feat, lats), F32)],
            in_specs=[None] * 4 + [image_spec(r)],
            work=3 * 10**9,
            limit=WIDE_LIMIT,
        )
        part[r] = mine, swap(give, "core", lat)

    def halves(*which):
        return [(BF, [(v, ALL) for v in part[r]]) for r in which]

    def pass_on(which, res):
        from_z.extend(send(v, "pix", pix, r) for r, v in zip(which, res))

    cross(order[0])
    cross(order[1])
    pass_on(order[:1], chain.sums(halves(order[0])))
    cross(order[2])
    (lc_mine,) = chain.run(gather_kernel, [((2 * rows, width), BF)], shares)
    lc_recv = swap(lc_mine, "y", lat)
    pass_on(order[1:3], chain.sums(halves(*order[1:3])))
    cross(order[3])
    (a_mine,) = chain.sums([(BF, [(v, ALL) for v in [*part[0], *from_z]])])
    a_recv = swap(a_mine, "y", lat)
    r2 = 2 * rows
    sq = (r2, width)
    att, tot, res1, nt2, hid1, act1, res2, nt3, q, kv = chain.run(
        first_kernel,
        [((chans, r2), F32), ((1, r2), F32), (sq, F32), (sq, BF), (sq, F32), (sq, BF), (sq, F32), (sq, BF), (sq, BF), ((r2, 2 * width), BF)],
        [a_mine, a_recv, lc_mine, lc_recv, gcol, value_weight, cross_output, row(first_gain), first_up, first_down, row(self_gain), self_inputs],
        [pltpu.VMEM(sq, BF)],
        limit=WIDE_LIMIT,
    )
    kv2 = swap(kv, "core", lat)
    image_rows = ((images, lat_rows, width), BF)
    rows_piece = ((lat_rows, width), BF)
    deal = lambda v: [v[0]] + [send(v[r], "pix", pix, r) for r in range(1, pix)]
    *out, selfr, sent3, back3, nt4, act2, hg2, gain2, dq, dkv, dkv_send, cot = chain.run(
        second_kernel,
        [rows_piece] * 4 + [(sq, BF), (sq, BF), (sq, F32), (sq, BF), (sq, BF), (sq, BF), ((1, width), F32), (sq, BF), ((r2, 2 * width), BF), ((r2, 2 * width), BF), (sq, BF)],
        [q, kv, kv2, res2, lc_mine, lc_recv, self_output, row(second_gain), second_up, second_down],
        [
            pltpu.VMEM((HEADS, r2, 2 * r2), BF),
            pltpu.VMEM(sq, F32),
            pltpu.VMEM((r2, 128), F32),
            pltpu.VMEM(sq, F32),
        ],
        limit=WIDE_LIMIT,
    )
    dkv2 = swap(dkv_send, "core", lat)
    (units_two,) = make_units(
        chain, [[(nt4, hg2), (act2, cot), (selfr, sent3)]], items, pix, lat
    )
    pg, sent2, hg1, back1, gvt, ht_give, ht_keep = chain.run(
        lambda *r: third_kernel(*r, items=items),
        [((r2, 3 * width), BF), (sq, BF), (sq, BF), ((rows, width), F32), ((feat, r2), BF)]
        + [((items, feat, lanes), BF)] * 2,
        [dq, dkv, dkv2, back3, res2, res1, hid1, att, tot, gcol, value_weight, cross_output, row(first_gain), first_up, first_down, row(self_gain), self_inputs, gain2],
        [pltpu.VMEM((feat, r2), F32), pltpu.VMEM(sq, F32)],
        limit=WIDE_LIMIT,
    )
    gv_at = {r: (fetch(gvt, "pix", pix, r) if r else gvt) for r in order}
    gv_both = {r: (v, swap(v, "core", lat)) for r, v in gv_at.items()}
    ht = AllSum(ht_keep, ht_give, items, pix, lat)
    (latents_out,) = chain.run(home_kernel, [image_rows], deal(out), work=SMALL)
    units_two.hold(chain.sums(units_two.over_core()))
    units_two.over_items(units_two.held[1:])
    (units_rest,) = make_units(
        chain, [[(nt3, pg), (nt2, hg1), (act1, sent2)]], items, pix, lat
    )
    first = ht.first()
    res = chain.sums(first + units_rest.over_core() + [(BF, [(gv_at[1], ALL)])])
    ht.after_first(res[: len(first)])
    units_rest.hold(res[len(first) : -1])
    gv_both[1] = gv_at[1], swap(res[-1], "core", lat)
    res = chain.sums(units_rest.copies(1) + units_two.halves())
    units_rest.over_items(res[: items - 1])
    units_two.over_pix(res[items - 1 :], 1)

    grad, part, from_z = None, {}, []

    def back(r, deps=()):
        nonlocal grad
        ins = [*gv_both[r], normed, powered[r], query_all[r]]
        grad, mine, give = chain.run(
            lambda *a: pixel_back_kernel(*a, chans=chans),
            [((images, feat, pix_rows), BF), half, half],
            ins + ([] if grad is None else [grad]),
            [
                pltpu.VMEM((feat, lats), BF),
                pltpu.VMEM((lats, feat), BF),
                pltpu.VMEM((feat, lats), BF),
                pltpu.VMEM((feat, lats), F32),
            ],
            in_specs=[None, None, image_spec(r), None, None] + ([] if grad is None else [ANY]),
            out_specs=[image_spec(r), None, None],
            aliases={} if grad is None else {6: 0},
            limit=WIDE_LIMIT,
            deps=deps,
        )
        part[r] = mine, swap(give, "core", lat)

    back(order[0], [gv_at[r] for r in order])
    ht.pix_pair(*chain.sums(ht.now()), 1)
    back(order[1], [v[1] for v in gv_both.values()])
    res = chain.sums(halves(order[0]) + ht.now() + units_two.halves())
    pass_on(order[:1], res[:1])
    ht.pix_pair(res[1], 2)
    units_two.over_pix(res[2:], 2)
    back(order[2])
    pass_on(order[1:3], chain.sums(halves(*order[1:3])))
    back(order[3])
    (pixel_grad,) = chain.run(
        interleave_kernel,
        [((chans, images, pix_rows), BF)],
        [grad],
        [pltpu.VMEM((chans, images, ptile), F32)],
        grid=pix_rows // ptile,
        in_specs=[pl.BlockSpec((images, feat, ptile), lambda t, pos: (0, 0, t))],
        out_specs=[pl.BlockSpec((chans, images, ptile), lambda t, pos: (0, 0, t))],
    )

    (ht_total,) = chain.sums(ht.now())

    def y_halves(pos, *refs):
        *terms, mine, give = refs
        for out, y in ((mine, pos[3]), (give, 1 - pos[3])):
            total = None
            for v in terms:
                v = v[:, pl.ds(pl.multiple_of(y * rows, rows), rows)].astype(F32)
                total = v if total is None else total + v
            out[...] = total.astype(out.dtype)

    quarter = (feat, rows)
    b_mine, b_give = chain.run(y_halves, [(quarter, F32), (quarter, BF)], [*part[0], *from_z])
    b_recv = swap(b_give, "y", lat)
    latent_grad, gt_keep, gt_give = chain.run(
        lambda *r: last_kernel(*r, scale=scale, items=items),
        [image_rows] + [((2, items, feat, lanes), BF)] * 2,
        [b_mine, b_recv, lc_mine, back1, row(cross_gain), gcol, query_weight, key_weight],
        [pltpu.VMEM((feat, rows), F32)],
    )
    gt = AllSum(gt_keep, gt_give, items, pix, lat)
    res = chain.sums(units_rest.halves() + units_two.grads())
    units_rest.over_pix(res[:2], 1)
    second_up_grad, second_down_grad, self_out_grad = res[2:]
    gt.after_first(chain.sums(gt.first()))
    own, *pieces = chain.run(
        join_kernel, [((feat, lanes), BF)] + [rows_piece] * pix, [*gt.terms, latent_grad]
    )
    gt.all_pix(own)
    gt.spread(
        *chain.run(both_kernel, [((2 * feat, lanes), BF)], [*gt.terms, ht_total])
    )
    own_rows = width // (items * lat * pix)
    results = [((chans, width), F32), ((own_rows, width), F32), ((1, chans), F32)]
    value_grad, cross_out_grad, vsum, gain_first, gain_self, gain_second = chain.run(
        lambda *r: value_kernel(*r, items=items),
        results + [((1, width), F32)] * 3,
        [*gt.parts, gcol, value_weight, cross_output],
        [pltpu.VMEM((feat, width), F32)],
    )
    units_rest.over_pix(chain.sums(units_rest.halves()), 2)
    key_grad, query_grad, psum, cross_gain_grad = chain.run(
        lambda *r: key_kernel(*r, items=items),
        results + [((1, width), F32)],
        [*gt.parts, gcol, key_weight, query_weight, vsum],
        [pltpu.VMEM((feat, width), F32)],
    )
    (latent_grad,) = chain.run(home_kernel, [image_rows], deal(pieces))
    self_in_grad, first_up_grad, first_down_grad = chain.sums(units_rest.grads())
    flat = lambda v: v.reshape(v.shape[1])
    return (
        latents_out,
        latent_grad,
        jnp.transpose(pixel_grad, (1, 2, 0)),
        query_grad,
        cross_out_grad,
        first_up_grad,
        first_down_grad,
        self_in_grad,
        self_out_grad,
        second_up_grad,
        second_down_grad,
        key_grad,
        value_grad,
        flat(cross_gain_grad),
        flat(psum),
        flat(gain_first),
        flat(gain_self),
        flat(gain_second),
    )


def solution(mesh):
    split = P("item", ("lat", "pix"), None)
    in_specs = (split, split, P("item")) + (P(),) * 15 + (split,)
    grads = P(("item", "lat", "pix"), None)
    out_specs = (split, split, split) + (grads,) * 8 + (P(),) * 7
    return jax.shard_map(body, mesh=mesh, in_specs=in_specs, out_specs=out_specs, check_vma=False)
```
